128 devices in a mesh: dp: 32 (over y, x, core), tensor: 4 (over z).
Axes of the slice: x: 4, y: 4, z: 4, core: 2. Of those that a mesh axis runs over, the one named last changes fastest.
Arguments:
- hidden: bfloat16 [8192, 4096], P('dp', 'tensor'), may hold values from -3 to 3
- cotangent: bfloat16 [8192, 4096], P('dp', 'tensor'), may hold values from -3 to 3
- counts: int32 [32, 4], P('dp'), may hold values from 0 to 4, as said below
- slot_of: int32 [32, 4, 4], P('dp'), may hold values from 0 to 31, as said below
- neighbours: bfloat16 [1024, 128, 896], P('dp', 'tensor'), may hold values from -3 to 3
- query_weight: bfloat16 [4096, 2048], P(None, 'tensor'), may hold values from -0.09375 to 0.09375
- key_weight: bfloat16 [896, 2048], P(None, 'tensor'), may hold values from -0.1875 to 0.1875
- value_weight: bfloat16 [896, 2048], P(None, 'tensor'), may hold values from -0.1875 to 0.1875
- out_weight: bfloat16 [2048, 4096], P('tensor'), may hold values from -0.125 to 0.125
- cond_weight: bfloat16 [4096, 1792], P('tensor'), may hold values from -0.09375 to 0.09375
- enc_query: bfloat16 [896, 896], replicated, may hold values from -0.1875 to 0.1875
- enc_out: bfloat16 [896, 896], replicated, may hold values from -0.1875 to 0.1875
Outputs:
- mixed: bfloat16 [8192, 4096], P('dp', 'tensor')
- grad_hidden: bfloat16 [8192, 4096], P('dp', 'tensor')
The draws below stay inside these ranges and needn't reach their ends.
Inputs may be any that keep to these rules, and one draw needn't show every extreme that they name: `slot_of`: within one sequence the entries are distinct. `counts`: every sequence has a block with 4 neighbours.
All inputs are finite; a program needn't handle non-finite values.
Results may differ from the reference program's by a relative error of at most 0.0095.
Values may be sent and summed in bfloat16 or wider, within the bound.
No kernel may reach another device: no remote copies, remote signals or barrier semaphores. Data moves between devices by JAX's collectives and lax.ppermute only.
A program may use at most 128 MiB of HBM per device.

```python
import math
import jax
import jax.numpy as jnp
from jax import lax

D = 4096
HEADS = 16
HEAD_DIM = 128
E = 896
ENC_HEAD_DIM = 128
BLOCK_LEN = 64
NB_LEN = 128
NEIGHBOURS = 4
BLOCKS = 4
SEQS = 32
CAP = 1
SLOTS = 32
TOKENS = 8192
N_TENSOR = 4


def draw_cotangent(key, part):
    key = jax.random.fold_in(key, 17)
    first_key, second_key, third_key = jax.random.split(key, 3)
    seq_len = BLOCKS * BLOCK_LEN
    values = jnp.clip(0.5 * jax.random.normal(first_key, (TOKENS, D), jnp.float32), -3.0, 3.0)
    lowest = 2.5
    magnitude = jax.random.uniform(second_key, (TOKENS, D), jnp.float32, lowest, 3.0)
    signs = jnp.where(jax.random.uniform(third_key, (TOKENS, D), jnp.float32) < 0.5, -1.0, 1.0)
    row_iota = jnp.arange(TOKENS, dtype=jnp.int32)[:, None]
    last_rows = row_iota % seq_len == seq_len - 1
    values = jnp.where(last_rows, signs * magnitude, values)
    return values.astype(jnp.bfloat16)


def draw_counts(key, part):
    key = jax.random.fold_in(key, 5)
    first_key, second_key, third_key, fourth_key = jax.random.split(key, 4)
    raw = jax.random.randint(first_key, (SEQS, BLOCKS), 0, 5 * NEIGHBOURS)
    values = jnp.minimum(raw, NEIGHBOURS)
    full_at = jax.random.randint(second_key, (SEQS, 1), 0, BLOCKS)
    block_iota = jnp.arange(BLOCKS, dtype=jnp.int32)[None, :]
    seq_iota = jnp.arange(SEQS, dtype=jnp.int32)[:, None]
    values = jnp.where(block_iota == full_at, NEIGHBOURS, values)
    empty_seq = jax.random.randint(third_key, (), 0, SEQS)
    offset = jax.random.randint(fourth_key, (), 1, BLOCKS)
    empty_block = (full_at[empty_seq, 0] + offset) % BLOCKS
    values = jnp.where((seq_iota == empty_seq) & (block_iota == empty_block), 0, values)
    return values.astype(jnp.int32)


def draw_slot_of(key, part):
    key = jax.random.fold_in(key, 11)
    row_keys = jax.random.split(key, SEQS)
    item_total = BLOCKS * NEIGHBOURS

    def pick_row(row_key):
        first_key, second_key = jax.random.split(row_key)
        middle = jax.random.permutation(first_key, SLOTS - 2)[:item_total - 2] + 1
        chosen = jnp.concatenate([jnp.array([0, SLOTS - 1], jnp.int32), middle.astype(jnp.int32)])
        order = jax.random.permutation(second_key, item_total)
        return chosen[order]
    picked = jax.vmap(pick_row)(row_keys)
    return picked.reshape(SEQS, BLOCKS, NEIGHBOURS).astype(jnp.int32)


def shard_levels(key, extent, cuts, low, top_value):
    gain, own = 1.0, jax.random.fold_in(key, 6)
    for position, shards_of in cuts:
        draws = jnp.exp(jax.random.uniform(jax.random.fold_in(own, position), (shards_of,), jnp.float32, low / len(cuts), top_value / len(cuts)))
        gain = gain * jnp.repeat(draws, extent[position] // shards_of).reshape([-1 if axis == position else 1 for axis in range(len(extent))])
    return gain


def scatter_about(stream_key, extent, scale, bound, shards=(), kind=jnp.bfloat16):
    result = scale * jax.random.normal(stream_key, extent, jnp.float32)
    if shards:
        result = result * shard_levels(stream_key, extent, shards, -0.22, 0.18)
    return jnp.clip(result, -bound, bound).astype(kind)


def setup_inputs(seed: int = 0) -> dict:
    key_list = jax.random.split(jax.random.key(seed), 13)
    hidden = scatter_about(key_list[0], (TOKENS, D), 0.5, 3.0, ((0, 32), (1, 4)))
    cotangent = draw_cotangent(jax.random.fold_in(key_list[12], 71), 0)
    counts = draw_counts(jax.random.fold_in(key_list[12], 71), 0)
    slot_of = draw_slot_of(jax.random.fold_in(key_list[12], 71), 0)
    neighbours = scatter_about(key_list[4], (SEQS * SLOTS, NB_LEN, E), 1.0, 3.0, ((0, 32), (1, 4)))
    query_weight = scatter_about(key_list[5], (D, HEADS * HEAD_DIM), D ** -0.5, 0.09375, ((1, 4),))
    key_weight = scatter_about(key_list[6], (E, HEADS * HEAD_DIM), E ** -0.5, 0.1875, ((1, 4),))
    value_weight = scatter_about(key_list[7], (E, HEADS * HEAD_DIM), E ** -0.5, 0.1875, ((1, 4),))
    out_weight = scatter_about(key_list[8], (HEADS * HEAD_DIM, D), (HEADS * HEAD_DIM) ** -0.5, 0.125, ((0, 4),))
    cond_weight = scatter_about(key_list[9], (D, 2 * E), D ** -0.5, 0.09375, ((0, 4),))
    enc_query = scatter_about(key_list[10], (E, E), E ** -0.5, 0.1875)
    enc_out = scatter_about(key_list[11], (E, E), E ** -0.5, 0.1875)
    return dict(hidden=hidden, cotangent=cotangent, counts=counts, slot_of=slot_of, neighbours=neighbours, query_weight=query_weight, key_weight=key_weight, value_weight=value_weight, out_weight=out_weight, cond_weight=cond_weight, enc_query=enc_query, enc_out=enc_out)


def multiply(spec, left, right):
    return jnp.einsum(spec, left.astype(jnp.float32), right.astype(jnp.float32))

def reference(hidden, cotangent, counts, slot_of, neighbours, query_weight, key_weight, value_weight, out_weight, cond_weight, enc_query, enc_out):
    tokens = BLOCKS * BLOCK_LEN
    shift = BLOCK_LEN - 1
    item_total = BLOCKS * NEIGHBOURS
    quarter = NB_LEN // N_TENSOR
    enc_heads = E // ENC_HEAD_DIM
    group_heads = HEADS // N_TENSOR
    head_width = HEADS * HEAD_DIM
    scaling = 1.0 / math.sqrt(HEAD_DIM)
    enc_scaling = 1.0 / math.sqrt(ENC_HEAD_DIM)
    low = jnp.bfloat16
    full = jnp.float32
    contract = (((1,), (1,)), ((), ()))

    def per_sequence(packed):
        seq_hidden, seq_cot, seq_counts, seq_slots, seq_index = packed
        query = jnp.dot(seq_hidden, query_weight, preferred_element_type=full).astype(low)
        cond = jnp.dot(seq_hidden, cond_weight, preferred_element_type=full).astype(low)
        cond = cond.reshape(BLOCKS, BLOCK_LEN, 2 * E)
        flat_slots = seq_slots.reshape(item_total)
        row_index = (flat_slots // CAP * SLOTS + seq_index * CAP + flat_slots % CAP).astype(jnp.int32)
        inputs = neighbours[row_index]
        item_cond = jnp.repeat(cond, NEIGHBOURS, axis=0)
        enc_q = jnp.dot(inputs.reshape(-1, E), enc_query, preferred_element_type=full).astype(low)
        enc_q = enc_q.reshape(item_total, NB_LEN, enc_heads, ENC_HEAD_DIM)
        cond_keys = item_cond[:, :, :E].reshape(item_total, BLOCK_LEN, enc_heads, ENC_HEAD_DIM)
        cond_vals = item_cond[:, :, E:].reshape(item_total, BLOCK_LEN, enc_heads, ENC_HEAD_DIM)
        enc_scores = multiply('nrhd,nchd->nhrc', enc_q, cond_keys) * enc_scaling
        enc_exp = jnp.exp(enc_scores)
        enc_p = enc_exp / lax.optimization_barrier(jnp.sum(enc_exp, axis=-1, keepdims=True))
        enc_pb = enc_p.astype(low)
        enc_att = multiply('nhrc,nchd->nrhd', enc_pb, cond_vals).astype(low).reshape(-1, E)
        encoded = (inputs.reshape(-1, E).astype(full) + jnp.dot(enc_att, enc_out, preferred_element_type=full)).astype(low)
        keys = jnp.dot(encoded, key_weight, preferred_element_type=full).astype(low)
        keys = keys.reshape(BLOCKS, NEIGHBOURS * NB_LEN, HEADS, HEAD_DIM)
        vals = jnp.dot(encoded, value_weight, preferred_element_type=full).astype(low)
        vals = vals.reshape(BLOCKS, NEIGHBOURS * NB_LEN, HEADS, HEAD_DIM)
        shifted = jnp.concatenate([query[shift:], jnp.zeros((shift, head_width), low)], axis=0)
        shifted = shifted.reshape(BLOCKS, BLOCK_LEN, HEADS, HEAD_DIM)
        live = jnp.arange(NEIGHBOURS)[None, :] < seq_counts[:, None]
        key_mask = jnp.repeat(live, NB_LEN, axis=1)[:, None, None, :]
        scores = multiply('cqhd,ckhd->chqk', shifted, keys) * scaling
        expd = jnp.where(key_mask, jnp.exp(scores), 0.0)
        totals = lax.optimization_barrier(jnp.sum(expd, axis=-1, keepdims=True))
        has_any = (seq_counts > 0)[:, None, None, None]
        probs = expd / jnp.where(has_any, totals, 1.0)
        probs_low = probs.astype(low)
        context = multiply('chqk,ckhd->cqhd', probs_low, vals).astype(low).reshape(tokens, head_width)
        context = jnp.concatenate([jnp.zeros((shift, head_width), low), context[:tokens - shift]], axis=0)
        attended = jnp.dot(context, out_weight, preferred_element_type=full)
        mixed = (seq_hidden.astype(full) + attended).astype(low)
        d_ctx = lax.dot_general(seq_cot, out_weight, contract, preferred_element_type=full).astype(low)
        d_shift = jnp.concatenate([d_ctx[shift:], jnp.zeros((shift, head_width), low)], axis=0)
        d_shift = d_shift.reshape(BLOCKS, BLOCK_LEN, HEADS, HEAD_DIM)
        d_probs = multiply('cqhd,ckhd->chqk', d_shift, vals)
        d_scores = (probs * (d_probs - lax.optimization_barrier(jnp.sum(probs * d_probs, axis=-1, keepdims=True))) * scaling).astype(low)
        d_query = multiply('chqk,ckhd->cqhd', d_scores, keys).astype(low).reshape(tokens, head_width)
        d_query = jnp.concatenate([jnp.zeros((shift, head_width), low), d_query[:tokens - shift]], axis=0)
        d_keys = multiply('chqk,cqhd->ckhd', d_scores, shifted).astype(low)
        d_vals = multiply('chqk,cqhd->ckhd', probs_low, d_shift).astype(low)
        d_keys = d_keys.reshape(item_total, NB_LEN, N_TENSOR, group_heads * HEAD_DIM)
        d_vals = d_vals.reshape(item_total, NB_LEN, N_TENSOR, group_heads * HEAD_DIM)
        key_groups = key_weight.reshape(E, N_TENSOR, group_heads * HEAD_DIM)
        val_groups = value_weight.reshape(E, N_TENSOR, group_heads * HEAD_DIM)
        group_terms = multiply('irgf,egf->gire', d_keys, key_groups) + multiply('irgf,egf->gire', d_vals, val_groups)
        group_terms = lax.optimization_barrier(group_terms.astype(low)).astype(full)
        d_encoded = lax.optimization_barrier(jnp.sum(group_terms, axis=0)).astype(low)
        d_att = lax.dot_general(d_encoded.reshape(-1, E), enc_out, contract, preferred_element_type=full).astype(low)
        d_att = d_att.reshape(item_total, NB_LEN, enc_heads, ENC_HEAD_DIM)
        d_enc_p = multiply('nrhd,nchd->nhrc', d_att, cond_vals)
        d_enc_scores = (enc_p * (d_enc_p - lax.optimization_barrier(jnp.sum(enc_p * d_enc_p, axis=-1, keepdims=True))) * enc_scaling).astype(low)
        scores_parts = d_enc_scores.reshape(item_total, enc_heads, N_TENSOR, quarter, BLOCK_LEN)
        query_parts = enc_q.reshape(item_total, N_TENSOR, quarter, enc_heads, ENC_HEAD_DIM)
        weight_parts = enc_pb.reshape(item_total, enc_heads, N_TENSOR, quarter, BLOCK_LEN)
        att_parts = d_att.reshape(item_total, N_TENSOR, quarter, enc_heads, ENC_HEAD_DIM)
        key_grads = multiply('nhtrc,ntrhd->ntchd', scores_parts, query_parts).reshape(item_total, N_TENSOR, BLOCK_LEN, E)
        val_grads = multiply('nhtrc,ntrhd->ntchd', weight_parts, att_parts).reshape(item_total, N_TENSOR, BLOCK_LEN, E)
        pieces = jnp.concatenate([key_grads, val_grads], axis=-1).astype(low)
        pieces = pieces.reshape(BLOCKS, NEIGHBOURS, N_TENSOR, BLOCK_LEN, 2 * E).astype(full)
        live_full = live.astype(full)[:, :, None, None, None]
        d_cond = lax.optimization_barrier(jnp.sum(pieces * live_full, axis=(1, 2))).reshape(tokens, 2 * E).astype(low)
        from_query = lax.dot_general(d_query, query_weight, contract, preferred_element_type=full)
        from_cond = lax.dot_general(d_cond, cond_weight, contract, preferred_element_type=full)
        grad_hidden = (seq_cot.astype(full) + from_query + from_cond).astype(low)
        return (mixed, grad_hidden)
    hidden_seqs = hidden.reshape(SEQS, tokens, D)
    cot_seqs = cotangent.reshape(SEQS, tokens, D)
    seq_ids = jnp.arange(SEQS, dtype=jnp.int32)
    mixed, grad_hidden = lax.map(per_sequence, (hidden_seqs, cot_seqs, counts, slot_of, seq_ids))
    return (mixed.reshape(TOKENS, D), grad_hidden.reshape(TOKENS, D))
```

```python
import functools
import math

import jax
import jax.numpy as jnp
from jax import lax
from jax.experimental import pallas as pl
from jax.experimental.pallas import tpu as pltpu
from jax.sharding import PartitionSpec as P

HEAD_DIM = 128
ENC_HEAD_DIM = 128
F32 = jnp.float32
BF16 = jnp.bfloat16
ROWS_T = (((1,), (1,)), ((), ()))
COLS_T = (((0,), (0,)), ((), ()))
PARAMS = pltpu.CompilerParams(
    vmem_limit_bytes=48 * 1024 * 1024, dimension_semantics=("arbitrary",)
)


def dot(a, b, dims=(((1,), (0,)), ((), ()))):
    return lax.dot_general(a, b, dims, preferred_element_type=F32)


def shift_perm(size, k):
    return [(i, (i + k) % size) for i in range(size)]


def in_order(parts, position):
    size = len(parts)
    stacked = jnp.stack(parts[::-1] * 2)
    return lax.dynamic_slice_in_dim(stacked, (size - 1 - position) % size, size, 0)


def exchange(pieces, position, axis="tensor"):
    size = pieces.shape[0]
    out = [lax.dynamic_index_in_dim(pieces, position, 0, keepdims=False)]
    for k in range(1, size):
        piece = lax.dynamic_index_in_dim(pieces, (position + k) % size, 0, keepdims=False)
        out.append(lax.ppermute(piece, axis, shift_perm(size, k)))
    return out


def spread(shard, size, axis="tensor"):
    return [shard] + [lax.ppermute(shard, axis, shift_perm(size, k)) for k in range(1, size)]


def live_columns(count, shape):
    column = lax.broadcasted_iota(jnp.int32, shape, len(shape) - 1)
    return (column // 32) % 4 < count


def encode_kernel(x_ref, cond_ref, enc_query_ref, enc_out_ref, queries_ref, probs_ref, encoded_ref):
    scaling = 1.0 / math.sqrt(ENC_HEAD_DIM)
    width = x_ref.shape[1]
    x = x_ref[...]
    queries_ref[...] = dot(x, enc_query_ref[...]).astype(BF16)
    attended = []
    for head in range(width // ENC_HEAD_DIM):
        cols = slice(head * ENC_HEAD_DIM, (head + 1) * ENC_HEAD_DIM)
        vals = slice(width + head * ENC_HEAD_DIM, width + (head + 1) * ENC_HEAD_DIM)
        scores = dot(cond_ref[:, cols], queries_ref[:, cols], ROWS_T) * scaling
        exponents = jnp.exp(scores)
        weights = exponents / jnp.sum(exponents, axis=0, keepdims=True)
        probs_ref[head] = weights
        attended.append(dot(weights.astype(BF16), cond_ref[:, vals], COLS_T).astype(BF16))
    mixing = dot(jnp.concatenate(attended, axis=1), enc_out_ref[...])
    encoded_ref[...] = (x.astype(F32) + mixing).astype(BF16)


def attend_kernel(
    count_ref, encoded_ref, key_w_ref, val_w_ref, query_ref, keys_ref, vals_ref, probs_ref, ctx_ref
):
    scaling = 1.0 / math.sqrt(HEAD_DIM)
    width = encoded_ref.shape[1]
    encoded = encoded_ref[...]
    key_w = key_w_ref[...].reshape(-1, key_w_ref.shape[3])[:width]
    val_w = val_w_ref[...].reshape(-1, val_w_ref.shape[3])[:width]
    keys_ref[0] = dot(encoded, key_w).astype(BF16)
    vals_ref[0] = dot(encoded, val_w).astype(BF16)
    count = count_ref[0]
    for head in range(query_ref.shape[2] // HEAD_DIM):
        cols = slice(head * HEAD_DIM, (head + 1) * HEAD_DIM)
        scores = dot(query_ref[0, :, cols], keys_ref[0, :, cols], ROWS_T) * scaling
        live = live_columns(count, scores.shape)
        expd = jnp.where(live, jnp.exp(scores), 0.0)
        totals = jnp.sum(expd, axis=1, keepdims=True)
        probs = expd / jnp.where(count > 0, totals, 1.0)
        probs_ref[0, head] = probs
        ctx_ref[:, cols] = dot(probs.astype(BF16), vals_ref[0, :, cols]).astype(BF16)


def backward_kernel(
    count_ref,
    keys_ref,
    vals_ref,
    probs_ref,
    query_ref,
    d_ctx_ref,
    key_w_ref,
    val_w_ref,
    enc_out_ref,
    enc_probs_ref,
    enc_queries_ref,
    cond_ref,
    d_query_ref,
    d_cond_ref,
    total_ref,
):
    step = pl.program_id(0)
    scaling = 1.0 / math.sqrt(HEAD_DIM)
    width = total_ref.shape[1]
    key_w = key_w_ref[...].reshape(-1, key_w_ref.shape[3])[:width]
    val_w = val_w_ref[...].reshape(-1, val_w_ref.shape[3])[:width]
    d_keys, d_vals = [], []
    for head in range(query_ref.shape[2] // HEAD_DIM):
        cols = slice(head * HEAD_DIM, (head + 1) * HEAD_DIM)
        probs = probs_ref[0, head]
        d_ctx = d_ctx_ref[0, :, cols]
        d_probs = dot(d_ctx, vals_ref[0, :, cols], ROWS_T)
        weighted = probs * d_probs
        d_scores = (weighted - probs * jnp.sum(weighted, axis=1, keepdims=True)) * scaling
        d_scores = d_scores.astype(BF16)
        d_query_ref[:, cols] = dot(d_scores, keys_ref[0, :, cols]).astype(BF16)
        d_keys.append(dot(d_scores, query_ref[0, :, cols], COLS_T).astype(BF16))
        d_vals.append(dot(probs.astype(BF16), d_ctx, COLS_T).astype(BF16))
    term = dot(jnp.concatenate(d_keys, axis=1), key_w, ROWS_T)
    term = term + dot(jnp.concatenate(d_vals, axis=1), val_w, ROWS_T)
    term = term.astype(BF16).astype(F32)

    @pl.when(step == 0)
    def _():
        total_ref[...] = term

    @pl.when(step > 0)
    def _():
        total_ref[...] += term

    @pl.when(step == pl.num_programs(0) - 1)
    def _():
        count = count_ref[0]
        d_att = dot(total_ref[...].astype(BF16), enc_out_ref[...], ROWS_T).astype(BF16)
        for head in range(width // ENC_HEAD_DIM):
            cols = slice(head * ENC_HEAD_DIM, (head + 1) * ENC_HEAD_DIM)
            vcols = slice(width + head * ENC_HEAD_DIM, width + (head + 1) * ENC_HEAD_DIM)
            probs = enc_probs_ref[head]
            d_probs = dot(cond_ref[:, vcols], d_att[:, cols], ROWS_T)
            weighted = probs * d_probs
            d_scores = (weighted - probs * jnp.sum(weighted, axis=0, keepdims=True)) * (
                1.0 / math.sqrt(ENC_HEAD_DIM)
            )
            live = live_columns(count, probs.shape)
            d_scores = jnp.where(live, d_scores, 0.0).astype(BF16)
            low = jnp.where(live, probs, 0.0).astype(BF16)
            d_cond_ref[:, cols] = dot(d_scores, enc_queries_ref[:, cols]).astype(BF16)
            d_cond_ref[:, vcols] = dot(low, d_att[:, cols]).astype(BF16)


def shift_down(rows, by):
    moved = pltpu.roll(rows, by, 0)
    index = lax.broadcasted_iota(jnp.int32, rows.shape, 0)
    return jnp.where(index >= by, moved, 0.0)


def mix_kernel(by, ctx_ref, weight_ref, base_ref, out_ref, total_ref):
    step = pl.program_id(0)
    half = weight_ref.shape[2] // 2
    wide = weight_ref.shape[3]
    ctx = ctx_ref[...]

    @pl.when(step == 0)
    def _():
        total_ref[...] = jnp.zeros_like(total_ref)

    for side in range(2):
        weight = weight_ref[:, :, side * half : (side + 1) * half, :].reshape(-1, wide)
        total_ref[:, side * wide : (side + 1) * wide] += dot(ctx, weight)

    @pl.when(step == pl.num_programs(0) - 1)
    def _():
        moved = shift_down(total_ref[...], by)
        out_ref[...] = (base_ref[...].astype(F32) + moved).astype(out_ref.dtype)


def query_grad_kernel(by, d_query_ref, weight_ref, base_ref, out_ref, total_ref):
    step = pl.program_id(0)
    weight = weight_ref[...].reshape(-1, weight_ref.shape[3])
    term = dot(d_query_ref[...], weight, ROWS_T)

    @pl.when(step == 0)
    def _():
        total_ref[...] = term

    @pl.when(step > 0)
    def _():
        total_ref[...] += term

    @pl.when(step == pl.num_programs(0) - 1)
    def _():
        out_ref[...] = base_ref[...].astype(F32) + shift_down(total_ref[...], by)


def whole(shape):
    return pl.BlockSpec(shape, lambda g: (0,) * len(shape))


def shards(
    hidden,
    cotangent,
    counts,
    slot_of,
    neighbours,
    query_weight,
    key_weight,
    value_weight,
    out_weight,
    cond_weight,
    enc_query,
    enc_out,
):
    tokens, part_width = hidden.shape
    head_width = query_weight.shape[1]
    blocks = counts.shape[1]
    slots_per = slot_of.shape[2]
    item_total = blocks * slots_per
    slot_total, quarter, enc_width = neighbours.shape
    block_len = tokens // blocks
    shift = block_len - 1
    n_tensor = lax.axis_size("tensor")
    n_dp = lax.axis_size("dp")
    here = lax.axis_index("tensor")
    row = lax.axis_index("dp")
    all_width = head_width * n_tensor
    sds = jax.ShapeDtypeStruct

    wq_part = lax.dynamic_slice_in_dim(
        query_weight.reshape(n_tensor, part_width, head_width), row * 32, 32, 1
    )
    wo_part = lax.dynamic_slice_in_dim(out_weight, row * 16, 16, 0)
    wo_part = wo_part.reshape(16, n_tensor, 2, head_width).transpose(1, 2, 0, 3)
    wo_part = wo_part.reshape(n_tensor, 32, head_width)
    kv_part = jnp.concatenate(
        [
            lax.dynamic_slice_in_dim(key_weight, row * 32, 32, 0),
            lax.dynamic_slice_in_dim(value_weight, row * 32, 32, 0),
        ],
        axis=0,
    )
    kv_part = jnp.broadcast_to(kv_part[None], (n_tensor, 64, head_width))
    weight_parts = jnp.concatenate([kv_part, wq_part, wo_part], axis=1)
    weight_parts = in_order(exchange(weight_parts, here), here)
    gathered = lax.all_gather(weight_parts, "dp", axis=0)

    def weight_spec(index):
        return pl.BlockSpec((n_dp, 1, 32, head_width), lambda g: (0, g, index, 0))

    cond_part = dot(hidden, cond_weight).astype(BF16).reshape(blocks, block_len, 2 * enc_width)
    cond_got = exchange(cond_part, here)
    cond = sum(part.astype(F32) for part in cond_got).astype(BF16)

    seq_counts = counts[0]
    live = jnp.arange(slots_per)[None, :] < seq_counts[:, None]
    slot_flat = slot_of.reshape(item_total)
    matches = (jnp.arange(slot_total)[:, None] == slot_flat[None, :]) & live.reshape(item_total)[
        None, :
    ]
    returned = lax.all_to_all(neighbours, "dp", split_axis=0, concat_axis=0, tiled=True)
    items = jnp.einsum(
        "si,sre->ire", matches.astype(BF16), returned, preferred_element_type=F32
    ).astype(BF16)
    items = items.reshape(blocks, slots_per * quarter, enc_width)
    x = jnp.concatenate(exchange(items, here), axis=0)
    rows = x.shape[0]
    count = lax.dynamic_slice_in_dim(seq_counts, here, 1, 0)

    def projected(array, weight, dims, axis):
        total = None
        for k, part in enumerate(spread(array, n_tensor)):
            block = lax.dynamic_slice_in_dim(
                weight, ((here - k) % n_tensor) * part_width, part_width, axis
            )
            term = dot(part, block, dims)
            total = term if total is None else total + term
        total = total.astype(BF16)
        total = jnp.concatenate([total[shift:], jnp.zeros((shift, head_width), BF16)], axis=0)
        total = total.reshape(blocks, block_len, head_width)
        return in_order(exchange(total, here), here)

    query = projected(hidden, query_weight, (((1,), (0,)), ((), ())), 0)
    d_ctx = projected(cotangent, out_weight, ROWS_T, 1)

    enc_queries, enc_probs, encoded = pl.pallas_call(
        encode_kernel,
        out_shape=(
            sds((rows, enc_width), BF16),
            sds((enc_width // ENC_HEAD_DIM, block_len, rows), F32),
            sds((rows, enc_width), BF16),
        ),
        compiler_params=pltpu.CompilerParams(vmem_limit_bytes=48 * 1024 * 1024),
        name="encode",
    )(x, cond, enc_query, enc_out)

    heads_here = head_width // HEAD_DIM
    smem = pl.BlockSpec(memory_space=pltpu.SMEM)
    group = lambda *shape: pl.BlockSpec((1,) + shape, lambda g: (g,) + (0,) * len(shape))
    columns = pl.BlockSpec((block_len, head_width), lambda g: (0, g))
    keys, vals, probs, ctx = pl.pallas_call(
        attend_kernel,
        grid=(n_tensor,),
        in_specs=[
            smem,
            whole((rows, enc_width)),
            weight_spec(0),
            weight_spec(1),
            group(block_len, head_width),
        ],
        out_specs=(
            group(rows, head_width),
            group(rows, head_width),
            group(heads_here, block_len, rows),
            columns,
        ),
        out_shape=(
            sds((n_tensor, rows, head_width), BF16),
            sds((n_tensor, rows, head_width), BF16),
            sds((n_tensor, heads_here, block_len, rows), F32),
            sds((block_len, all_width), BF16),
        ),
        compiler_params=PARAMS,
        name="attend",
    )(count, encoded, gathered, gathered, query)

    d_query, d_cond = pl.pallas_call(
        backward_kernel,
        grid=(n_tensor,),
        in_specs=[
            smem,
            group(rows, head_width),
            group(rows, head_width),
            group(heads_here, block_len, rows),
            group(block_len, head_width),
            group(block_len, head_width),
            weight_spec(0),
            weight_spec(1),
            whole((enc_width, enc_width)),
            whole((enc_width // ENC_HEAD_DIM, block_len, rows)),
            whole((rows, enc_width)),
            whole((block_len, 2 * enc_width)),
        ],
        out_specs=(columns, whole((block_len, 2 * enc_width))),
        out_shape=(
            sds((block_len, all_width), BF16),
            sds((block_len, 2 * enc_width), BF16),
        ),
        scratch_shapes=[pltpu.VMEM((rows, enc_width), F32)],
        compiler_params=PARAMS,
        name="backward",
    )(
        count,
        keys,
        vals,
        probs,
        query,
        d_ctx,
        gathered,
        gathered,
        enc_out,
        enc_probs,
        enc_queries,
        cond,
    )

    all_rows = pl.BlockSpec((tokens, head_width), lambda g: (0, g))
    ctx_all = in_order(spread(ctx, n_tensor), here).reshape(tokens, all_width)
    mixed = pl.pallas_call(
        functools.partial(mix_kernel, shift),
        grid=(n_tensor,),
        in_specs=[all_rows, weight_spec(3), whole((tokens, part_width))],
        out_specs=whole((tokens, part_width)),
        out_shape=sds((tokens, part_width), BF16),
        scratch_shapes=[pltpu.VMEM((tokens, part_width), F32)],
        compiler_params=PARAMS,
        name="mix",
    )(ctx_all, gathered, hidden)

    d_query_all = in_order(spread(d_query, n_tensor), here).reshape(tokens, all_width)
    from_query = pl.pallas_call(
        functools.partial(query_grad_kernel, shift),
        grid=(n_tensor,),
        in_specs=[all_rows, weight_spec(2), whole((tokens, part_width))],
        out_specs=whole((tokens, part_width)),
        out_shape=sds((tokens, part_width), F32),
        scratch_shapes=[pltpu.VMEM((tokens, part_width), F32)],
        compiler_params=PARAMS,
        name="query_grad",
    )(d_query_all, gathered, cotangent)
    d_cond_all = in_order(spread(d_cond, n_tensor), here).reshape(tokens, 2 * enc_width)
    grad_hidden = (from_query + dot(d_cond_all, cond_weight, ROWS_T)).astype(BF16)
    return (mixed, grad_hidden)


def solution(mesh):
    placed = (
        P("dp", "tensor"),
        P("dp", "tensor"),
        P("dp", None),
        P("dp", None, None),
        P("dp", "tensor", None),
        P(None, "tensor"),
        P(None, "tensor"),
        P(None, "tensor"),
        P("tensor", None),
        P("tensor", None),
        P(),
        P(),
    )
    return jax.shard_map(
        shards,
        mesh=mesh,
        in_specs=placed,
        out_specs=(P("dp", "tensor"), P("dp", "tensor")),
        check_vma=False,
    )
```

```python
import functools
import math

import jax
import jax.numpy as jnp
from jax import lax
from jax.experimental import pallas as pl
from jax.experimental.pallas import tpu as pltpu
from jax.sharding import PartitionSpec as P

HEAD_DIM = 128
ENC_HEAD_DIM = 128
F32 = jnp.float32
BF16 = jnp.bfloat16
PLAIN = (((1,), (0,)), ((), ()))
ROWS_T = (((1,), (1,)), ((), ()))
COLS_T = (((0,), (0,)), ((), ()))
SCALING = 1.0 / math.sqrt(HEAD_DIM)
ENC_SCALING = 1.0 / math.sqrt(ENC_HEAD_DIM)
SLICE = 32


def dot(a, b, dims=PLAIN):
    return lax.dot_general(a, b, dims, preferred_element_type=F32)


def call(kernel, name, grid, in_specs, out_specs, out_shape, scratch, flops, nbytes):
    return pl.pallas_call(
        kernel,
        out_shape=out_shape,
        grid_spec=pltpu.PrefetchScalarGridSpec(
            num_scalar_prefetch=1,
            grid=(grid,),
            in_specs=in_specs,
            out_specs=out_specs,
            scratch_shapes=scratch,
        ),
        compiler_params=pltpu.CompilerParams(
            vmem_limit_bytes=56 * 1024 * 1024, dimension_semantics=("arbitrary",)
        ),
        cost_estimate=pl.CostEstimate(flops=flops, bytes_accessed=nbytes, transcendentals=0),
        name=name,
    )


def whole(*shape):
    return pl.BlockSpec(shape, lambda g, s: (0,) * len(shape))


def group(*shape):
    return pl.BlockSpec((1,) + shape, lambda g, s: (g,) + (0,) * len(shape))


def own_columns(rows, width):
    return pl.BlockSpec((rows, width), lambda g, s: (0, (s[0] + g) % 4))


def exchange(pieces, position, axis="tensor"):
    size = pieces.shape[0]
    out = [lax.dynamic_index_in_dim(pieces, position, 0, keepdims=False)]
    for k in range(1, size):
        piece = lax.dynamic_index_in_dim(pieces, (position - k) % size, 0, keepdims=False)
        out.append(lax.ppermute(piece, axis, [(i, (i - k) % size) for i in range(size)]))
    return out


def spread(shard, size, axis="tensor"):
    return [shard] + [
        lax.ppermute(shard, axis, [(i, (i - k) % size) for i in range(size)])
        for k in range(1, size)
    ]


def after(value, earlier):
    return lax.optimization_barrier((value, earlier))[0]


def live_columns(count, shape):
    column = lax.broadcasted_iota(jnp.int32, shape, len(shape) - 1)
    return (column // 32) % 4 < count


def by_heads(array, head_dim):
    head = lax.broadcasted_iota(jnp.int32, array.shape, 1) // head_dim
    zero = jnp.zeros_like(array)
    count = array.shape[1] // head_dim
    return jnp.concatenate([jnp.where(head == h, array, zero) for h in range(count)], axis=0)


def head_blocks(array, rows, head_dim):
    count = array.shape[1] // head_dim
    return [
        array[h * rows : (h + 1) * rows, h * head_dim : (h + 1) * head_dim] for h in range(count)
    ]


def pick(step, refs, target_ref, change):
    for k, ref in enumerate(refs):

        @pl.when(step == k)
        def _(ref=ref):
            target_ref[...] = change(ref[...])


def project_kernel(dims, shift, s_ref, p0, p1, p2, p3, weight_ref, out_ref, total_ref):
    step = pl.program_id(0)
    for k, ref in enumerate((p0, p1, p2, p3)):

        @pl.when(step == k)
        def _(ref=ref, k=k):
            term = dot(ref[...], weight_ref[...], dims)
            total_ref[...] = term if k == 0 else total_ref[...] + term

    @pl.when(step == pl.num_programs(0) - 1)
    def _():
        rows = total_ref.shape[0]
        moved = pltpu.roll(total_ref[...], rows - shift, 0)
        index = lax.broadcasted_iota(jnp.int32, moved.shape, 0)
        out_ref[...] = jnp.where(index < rows - shift, moved, 0.0).astype(BF16)


def encode_kernel(
    s_ref,
    x0,
    x1,
    x2,
    x3,
    c0,
    c1,
    c2,
    c3,
    enc_query_ref,
    enc_out_ref,
    cond_ref,
    queries_ref,
    probs_ref,
    encoded_ref,
):
    width = x0.shape[1]
    x = jnp.concatenate([x0[...], x1[...], x2[...], x3[...]], axis=0)
    cond = (c0[...].astype(F32) + c1[...].astype(F32)) + (
        c2[...].astype(F32) + c3[...].astype(F32)
    )
    cond = cond.astype(BF16)
    cond_ref[...] = cond
    length = cond.shape[0]
    queries = dot(x, enc_query_ref[...]).astype(BF16)
    queries_ref[...] = queries
    scores = dot(by_heads(cond[:, :width], ENC_HEAD_DIM), queries, ROWS_T) * ENC_SCALING
    exponents = jnp.exp(scores).reshape(-1, length, scores.shape[1])
    probs = exponents / jnp.sum(exponents, axis=1, keepdims=True)
    probs = probs.reshape(scores.shape)
    probs_ref[...] = probs
    attended = dot(probs.astype(BF16), by_heads(cond[:, width:], ENC_HEAD_DIM), COLS_T)
    mixing = dot(attended.astype(BF16), enc_out_ref[...])
    encoded_ref[...] = (x.astype(F32) + mixing).astype(BF16)


def attend_kernel(
    s_ref,
    encoded_ref,
    key_w_ref,
    val_w_ref,
    q0,
    q1,
    q2,
    q3,
    keys_ref,
    vals_ref,
    probs_ref,
    ctx_ref,
    query_ref,
):
    width = encoded_ref.shape[1]
    pick(pl.program_id(0), (q0, q1, q2, q3), query_ref, lambda q: by_heads(q, HEAD_DIM))
    encoded = encoded_ref[...]
    keys = dot(encoded, key_w_ref[...].reshape(-1, key_w_ref.shape[3])[:width]).astype(BF16)
    vals = dot(encoded, val_w_ref[...].reshape(-1, val_w_ref.shape[3])[:width]).astype(BF16)
    keys_ref[0] = keys
    vals_ref[0] = vals
    count = s_ref[1]
    scores = dot(query_ref[...], keys, ROWS_T) * SCALING
    expd = jnp.where(live_columns(count, scores.shape), jnp.exp(scores), 0.0)
    totals = jnp.sum(expd, axis=1, keepdims=True)
    probs = expd / jnp.where(count > 0, totals, 1.0)
    probs_ref[0] = probs
    ctx = dot(probs.astype(BF16), vals)
    ctx = head_blocks(ctx, ctx_ref.shape[0], HEAD_DIM)
    ctx_ref[...] = jnp.concatenate(ctx, axis=1).astype(BF16)


def scores_back_kernel(
    s_ref, keys_ref, vals_ref, probs_ref, d0, d1, d2, d3, d_scores_ref, d_query_ref, d_ctx_ref
):
    pick(pl.program_id(0), (d0, d1, d2, d3), d_ctx_ref, lambda d: by_heads(d, HEAD_DIM))
    probs = probs_ref[0]
    d_probs = dot(d_ctx_ref[...], vals_ref[0], ROWS_T)
    weighted = probs * d_probs
    d_scores = (weighted - probs * jnp.sum(weighted, axis=1, keepdims=True)) * SCALING
    d_scores = d_scores.astype(BF16)
    d_scores_ref[0] = d_scores
    d_query = dot(d_scores, keys_ref[0])
    d_query = head_blocks(d_query, d_query_ref.shape[0], HEAD_DIM)
    d_query_ref[...] = jnp.concatenate(d_query, axis=1).astype(BF16)


def encoded_back_kernel(
    s_ref,
    d_scores_ref,
    probs_ref,
    q0,
    q1,
    q2,
    q3,
    d0,
    d1,
    d2,
    d3,
    key_w_ref,
    val_w_ref,
    enc_out_ref,
    enc_probs_ref,
    enc_queries_ref,
    cond_ref,
    d_cond_ref,
    query_ref,
    d_ctx_ref,
    total_ref,
):
    step = pl.program_id(0)
    width = total_ref.shape[1]
    pick(step, (q0, q1, q2, q3), query_ref, lambda q: by_heads(q, HEAD_DIM))
    pick(step, (d0, d1, d2, d3), d_ctx_ref, lambda d: by_heads(d, HEAD_DIM))
    d_keys = dot(d_scores_ref[0], query_ref[...], COLS_T).astype(BF16)
    d_vals = dot(probs_ref[0].astype(BF16), d_ctx_ref[...], COLS_T).astype(BF16)
    term = dot(d_keys, key_w_ref[...].reshape(-1, key_w_ref.shape[3])[:width], ROWS_T)
    term = term + dot(d_vals, val_w_ref[...].reshape(-1, val_w_ref.shape[3])[:width], ROWS_T)
    term = term.astype(BF16).astype(F32)

    @pl.when(step == 0)
    def _():
        total_ref[...] = term

    @pl.when(step > 0)
    def _():
        total_ref[...] += term

    @pl.when(step == pl.num_programs(0) - 1)
    def _():
        length = cond_ref.shape[0]
        d_att = dot(total_ref[...].astype(BF16), enc_out_ref[...], ROWS_T).astype(BF16)
        probs = enc_probs_ref[...]
        d_probs = dot(by_heads(cond_ref[:, width:], ENC_HEAD_DIM), d_att, ROWS_T)
        weighted = probs * d_probs
        sums = jnp.sum(weighted.reshape(-1, length, weighted.shape[1]), axis=1, keepdims=True)
        spread_sums = (probs.reshape(-1, length, probs.shape[1]) * sums).reshape(probs.shape)
        d_scores = (weighted - spread_sums) * ENC_SCALING
        live = live_columns(s_ref[1], probs.shape)
        d_scores = jnp.where(live, d_scores, 0.0).astype(BF16)
        low = jnp.where(live, probs, 0.0).astype(BF16)
        d_keys = head_blocks(dot(d_scores, enc_queries_ref[...]), length, ENC_HEAD_DIM)
        d_vals = head_blocks(dot(low, d_att), length, ENC_HEAD_DIM)
        d_cond_ref[...] = jnp.concatenate(d_keys + d_vals, axis=1).astype(BF16)


def placed_rows(rows, by, shift):
    moved = pltpu.roll(rows, by, 0)
    if shift == 0:
        return moved
    index = lax.broadcasted_iota(jnp.int32, rows.shape, 0)
    return jnp.where(index >= shift, moved, 0.0)


def mix_kernel(shift, s_ref, c0, c1, c2, c3, weight_ref, base_ref, out_ref, total_ref):
    step = pl.program_id(0)
    half = weight_ref.shape[2] // 2
    wide = weight_ref.shape[3]
    length = c0.shape[0]
    ctx = jnp.concatenate([c0[...], c1[...], c2[...], c3[...]], axis=0)

    @pl.when(step == 0)
    def _():
        total_ref[...] = jnp.zeros_like(total_ref)

    for side in range(2):
        weight = weight_ref[:, :, side * half : (side + 1) * half, :].reshape(-1, wide)
        total_ref[:, side * wide : (side + 1) * wide] += dot(ctx, weight)

    @pl.when(step == pl.num_programs(0) - 1)
    def _():
        by = (s_ref[0] * length + shift) % total_ref.shape[0]
        moved = placed_rows(total_ref[...], by, shift)
        out_ref[...] = (base_ref[...].astype(F32) + moved).astype(out_ref.dtype)


def query_grad_kernel(shift, s_ref, c0, c1, c2, c3, weight_ref, base_ref, out_ref, total_ref):
    step = pl.program_id(0)
    length = c0.shape[0]
    weight = weight_ref[...].reshape(-1, weight_ref.shape[3])
    d_query = jnp.concatenate([c0[...], c1[...], c2[...], c3[...]], axis=0)
    term = dot(d_query, weight, ROWS_T)

    @pl.when(step == 0)
    def _():
        total_ref[...] = term

    @pl.when(step > 0)
    def _():
        total_ref[...] += term

    @pl.when(step == pl.num_programs(0) - 1)
    def _():
        by = (s_ref[0] * length + shift) % total_ref.shape[0]
        out_ref[...] = base_ref[...].astype(F32) + placed_rows(total_ref[...], by, shift)


def cond_grad_kernel(s_ref, c0, c1, c2, c3, weight_ref, base_ref, out_ref):
    length = c0.shape[0]
    d_cond = jnp.concatenate([c0[...], c1[...], c2[...], c3[...]], axis=0)
    term = dot(d_cond, weight_ref[...], ROWS_T)
    by = s_ref[0] * length
    out_ref[...] = (base_ref[...] + placed_rows(term, by, 0)).astype(out_ref.dtype)


def shards(
    hidden,
    cotangent,
    counts,
    slot_of,
    neighbours,
    query_weight,
    key_weight,
    value_weight,
    out_weight,
    cond_weight,
    enc_query,
    enc_out,
):
    tokens, part_width = hidden.shape
    head_width = query_weight.shape[1]
    blocks = counts.shape[1]
    slots_per = slot_of.shape[2]
    item_total = blocks * slots_per
    slot_total, quarter, enc_width = neighbours.shape
    block_len = tokens // blocks
    shift = block_len - 1
    n_tensor = lax.axis_size("tensor")
    n_dp = lax.axis_size("dp")
    here = lax.axis_index("tensor")
    row = lax.axis_index("dp")
    all_width = head_width * n_tensor
    rows = slots_per * quarter * n_tensor
    enc_rows = enc_width // ENC_HEAD_DIM * block_len
    head_rows = head_width // HEAD_DIM * block_len
    sds = jax.ShapeDtypeStruct

    seq_counts = counts[0]
    count = lax.dynamic_slice_in_dim(seq_counts, here, 1, 0)
    scalars = jnp.concatenate([here.astype(jnp.int32)[None], count])

    wq_part = lax.dynamic_slice_in_dim(
        query_weight.reshape(n_tensor, part_width, head_width), row * SLICE, SLICE, 1
    )
    wo_part = lax.dynamic_slice_in_dim(out_weight, row * (SLICE // 2), SLICE // 2, 0)
    wo_part = wo_part.reshape(SLICE // 2, n_tensor, 2, head_width).transpose(1, 2, 0, 3)
    wo_part = wo_part.reshape(n_tensor, SLICE, head_width)
    kv_part = jnp.concatenate(
        [
            lax.dynamic_slice_in_dim(key_weight, row * SLICE, SLICE, 0),
            lax.dynamic_slice_in_dim(value_weight, row * SLICE, SLICE, 0),
        ],
        axis=0,
    )
    kv_part = jnp.broadcast_to(kv_part[None], (n_tensor, 2 * SLICE, head_width))
    weight_parts = exchange(jnp.concatenate([kv_part, wq_part, wo_part], axis=1), here)
    kv_parts = jnp.stack([part[: 2 * SLICE] for part in weight_parts])
    qo_parts = jnp.stack([part[2 * SLICE :] for part in weight_parts])
    kv_all = lax.all_gather(kv_parts, "dp", axis=0)

    def weight_spec(index):
        return pl.BlockSpec((n_dp, 1, SLICE, head_width), lambda g, s: (0, g, index, 0))

    cond_part = dot(hidden, cond_weight).astype(BF16).reshape(blocks, block_len, 2 * enc_width)
    cond_parts = exchange(cond_part, here)

    live = jnp.arange(slots_per)[None, :] < seq_counts[:, None]
    slot_flat = slot_of.reshape(item_total)
    matches = (jnp.arange(slot_total)[:, None] == slot_flat[None, :]) & live.reshape(item_total)[
        None, :
    ]
    returned = lax.all_to_all(neighbours, "dp", split_axis=0, concat_axis=0, tiled=True)
    items = jnp.einsum(
        "si,sre->ire", matches.astype(BF16), returned, preferred_element_type=F32
    ).astype(BF16)
    x_parts = exchange(items.reshape(blocks, slots_per * quarter, enc_width), here)

    def projected(array, weight, dims, weight_block, weight_map, name):
        full = whole(tokens, part_width)
        result = call(
            functools.partial(project_kernel, dims, shift),
            name,
            n_tensor,
            [full] * 4 + [pl.BlockSpec(weight_block, weight_map)],
            whole(tokens, head_width),
            sds((tokens, head_width), BF16),
            [pltpu.VMEM((tokens, head_width), F32)],
            2 * tokens * part_width * n_tensor * head_width,
            7_000_000,
        )(scalars, *spread(array, n_tensor), weight)
        return result

    query = projected(
        hidden,
        query_weight,
        PLAIN,
        (part_width, head_width),
        lambda g, s: ((s[0] + g) % 4, 0),
        "query",
    )
    query_parts = exchange(query.reshape(blocks, block_len, head_width), here)
    qo_all = lax.all_gather(after(qo_parts, query), "dp", axis=0)
    d_ctx = projected(
        after(cotangent, query),
        out_weight,
        ROWS_T,
        (head_width, part_width),
        lambda g, s: (0, (s[0] + g) % 4),
        "d_ctx",
    )
    d_ctx_parts = exchange(d_ctx.reshape(blocks, block_len, head_width), here)

    x_spec = whole(slots_per * quarter, enc_width)
    c_spec = whole(block_len, 2 * enc_width)
    w_spec = whole(enc_width, enc_width)
    r_spec = whole(rows, enc_width)
    p_spec = whole(enc_rows, rows)
    cond, enc_queries, enc_probs, encoded = call(
        encode_kernel,
        "encode",
        1,
        [x_spec] * 4 + [c_spec] * 4 + [w_spec] * 2,
        (c_spec, r_spec, p_spec, r_spec),
        (
            sds((block_len, 2 * enc_width), BF16),
            sds((rows, enc_width), BF16),
            sds((enc_rows, rows), F32),
            sds((rows, enc_width), BF16),
        ),
        [],
        3_000_000_000,
        10_000_000,
    )(scalars, *x_parts, *cond_parts, enc_query, enc_out)

    q_spec = whole(block_len, head_width)
    big = pltpu.VMEM((head_rows, head_width), BF16)
    keys, vals, probs, ctx = call(
        attend_kernel,
        "attend",
        n_tensor,
        [r_spec, weight_spec(0), weight_spec(1)] + [q_spec] * 4,
        (
            group(rows, head_width),
            group(rows, head_width),
            group(head_rows, rows),
            own_columns(block_len, head_width),
        ),
        (
            sds((n_tensor, rows, head_width), BF16),
            sds((n_tensor, rows, head_width), BF16),
            sds((n_tensor, head_rows, rows), F32),
            sds((block_len, all_width), BF16),
        ),
        [big],
        6_000_000_000,
        16_000_000,
    )(scalars, encoded, kv_all, kv_all, *query_parts)
    ctx_parts = spread(ctx, n_tensor)

    d_scores, d_query = call(
        scores_back_kernel,
        "scores_back",
        n_tensor,
        [group(rows, head_width), group(rows, head_width), group(head_rows, rows)] + [q_spec] * 4,
        (group(head_rows, rows), own_columns(block_len, head_width)),
        (sds((n_tensor, head_rows, rows), BF16), sds((block_len, all_width), BF16)),
        [big],
        2_000_000_000,
        8_000_000,
    )(scalars, keys, vals, probs, *d_ctx_parts)
    d_query_parts = spread(d_query, n_tensor)

    d_cond = call(
        encoded_back_kernel,
        "encoded_back",
        n_tensor,
        [group(head_rows, rows), group(head_rows, rows)]
        + [q_spec] * 8
        + [weight_spec(0), weight_spec(1), w_spec, p_spec, r_spec, c_spec],
        c_spec,
        sds((block_len, 2 * enc_width), BF16),
        [big, big, pltpu.VMEM((rows, enc_width), F32)],
        8_000_000_000,
        16_000_000,
    )(
        scalars,
        d_scores,
        probs,
        *query_parts,
        *d_ctx_parts,
        kv_all,
        kv_all,
        enc_out,
        enc_probs,
        enc_queries,
        cond,
    )
    d_cond_parts = spread(d_cond, n_tensor)

    out_spec = whole(tokens, part_width)
    acc = pltpu.VMEM((tokens, part_width), F32)
    col_spec = own_columns(block_len, head_width)
    mixed = call(
        functools.partial(mix_kernel, shift),
        "mix",
        n_tensor,
        [col_spec] * 4 + [weight_spec(1), out_spec],
        out_spec,
        sds((tokens, part_width), BF16),
        [acc],
        1_100_000_000,
        6_000_000,
    )(scalars, *ctx_parts, qo_all, hidden)
    from_query = call(
        functools.partial(query_grad_kernel, shift),
        "query_grad",
        n_tensor,
        [col_spec] * 4 + [weight_spec(0), out_spec],
        out_spec,
        sds((tokens, part_width), F32),
        [acc],
        1_100_000_000,
        7_000_000,
    )(scalars, *d_query_parts, qo_all, cotangent)
    grad_hidden = call(
        cond_grad_kernel,
        "cond_grad",
        1,
        [c_spec] * 4 + [whole(part_width, 2 * enc_width), out_spec],
        out_spec,
        sds((tokens, part_width), BF16),
        [],
        1_000_000_000,
        6_000_000,
    )(scalars, *d_cond_parts, cond_weight, from_query)
    return (mixed, grad_hidden)


def solution(mesh):
    placed = (
        P("dp", "tensor"),
        P("dp", "tensor"),
        P("dp", None),
        P("dp", None, None),
        P("dp", "tensor", None),
        P(None, "tensor"),
        P(None, "tensor"),
        P(None, "tensor"),
        P("tensor", None),
        P("tensor", None),
        P(),
        P(),
    )
    return jax.shard_map(
        shards,
        mesh=mesh,
        in_specs=placed,
        out_specs=(P("dp", "tensor"), P("dp", "tensor")),
        check_vma=False,
    )
```

```python
import functools
import math

import jax
import jax.numpy as jnp
from jax import lax
from jax.experimental import pallas as pl
from jax.experimental.pallas import tpu as pltpu
from jax.sharding import PartitionSpec as P

HEAD_DIM = 128
ENC_HEAD_DIM = 128
F32 = jnp.float32
BF16 = jnp.bfloat16
PLAIN = (((1,), (0,)), ((), ()))
ROWS_T = (((1,), (1,)), ((), ()))
COLS_T = (((0,), (0,)), ((), ()))
SCALING = 1.0 / math.sqrt(HEAD_DIM)
ENC_SCALING = 1.0 / math.sqrt(ENC_HEAD_DIM)
SLICE = 32


def dot(a, b, dims=PLAIN):
    return lax.dot_general(a, b, dims, preferred_element_type=F32)


def call(kernel, name, grid, in_specs, out_specs, out_shape, scratch, vmem_mib):
    return pl.pallas_call(
        kernel,
        out_shape=out_shape,
        grid_spec=pltpu.PrefetchScalarGridSpec(
            num_scalar_prefetch=1,
            grid=(grid,),
            in_specs=in_specs,
            out_specs=out_specs,
            scratch_shapes=scratch,
        ),
        compiler_params=pltpu.CompilerParams(
            vmem_limit_bytes=vmem_mib * 1024 * 1024, dimension_semantics=("arbitrary",)
        ),
        name=name,
    )


def whole(*shape):
    return pl.BlockSpec(shape, lambda g, s: (0,) * len(shape))


def group(*shape):
    return pl.BlockSpec((1,) + shape, lambda g, s: (g,) + (0,) * len(shape))


def exchange(pieces, position, axis="tensor"):
    size = pieces.shape[0]
    out = [lax.dynamic_index_in_dim(pieces, position, 0, keepdims=False)]
    for k in range(1, size):
        piece = lax.dynamic_index_in_dim(pieces, (position - k) % size, 0, keepdims=False)
        out.append(lax.ppermute(piece, axis, [(i, (i - k) % size) for i in range(size)]))
    return out


def spread(shard, size, axis="tensor"):
    return [shard] + [
        lax.ppermute(shard, axis, [(i, (i - k) % size) for i in range(size)])
        for k in range(1, size)
    ]


def after(value, earlier):
    return lax.optimization_barrier((value, earlier))[0]


def live_columns(count, shape):
    column = lax.broadcasted_iota(jnp.int32, shape, len(shape) - 1)
    return (column // 32) % 4 < count


def by_heads(array, head_dim):
    head = lax.broadcasted_iota(jnp.int32, array.shape, 1) // head_dim
    zero = jnp.zeros_like(array)
    count = array.shape[1] // head_dim
    return jnp.concatenate([jnp.where(head == h, array, zero) for h in range(count)], axis=0)


def head_blocks(array, rows, head_dim):
    count = array.shape[1] // head_dim
    return [
        array[h * rows : (h + 1) * rows, h * head_dim : (h + 1) * head_dim] for h in range(count)
    ]


def project_kernel(dims, shift, s_ref, p0, p1, p2, p3, weight_ref, *rest):
    out_ref, total_ref = rest[-2:]
    step = pl.program_id(0)
    for k, ref in enumerate((p0, p1, p2, p3)):

        @pl.when(step == k)
        def _(ref=ref, k=k):
            term = dot(ref[...], weight_ref[...], dims)
            total_ref[...] = term if k == 0 else total_ref[...] + term

    @pl.when(step == pl.num_programs(0) - 1)
    def _():
        rows = total_ref.shape[0]
        moved = pltpu.roll(total_ref[...], rows - shift, 0)
        index = lax.broadcasted_iota(jnp.int32, moved.shape, 0)
        result = jnp.where(index < rows - shift, moved, 0.0).astype(BF16)
        if len(rest) == 2:
            out_ref[...] = result
        else:
            blocks, _, length, _ = out_ref.shape
            for block in range(blocks):
                span = slice(block * length, (block + 1) * length)
                out_ref[block, 0] = rest[0][span, :]
                out_ref[block, 1] = result[span, :]


def encode_kernel(
    s_ref,
    x_ref,
    c0,
    c1,
    c2,
    c3,
    enc_query_ref,
    enc_out_ref,
    cond_ref,
    queries_ref,
    probs_ref,
    encoded_ref,
):
    width = x_ref.shape[1]
    x = x_ref[...]
    cond = (c0[...].astype(F32) + c1[...].astype(F32)) + (
        c2[...].astype(F32) + c3[...].astype(F32)
    )
    cond = cond.astype(BF16)
    cond_ref[...] = cond
    length = cond.shape[0]
    queries = dot(x, enc_query_ref[...]).astype(BF16)
    queries_ref[...] = queries
    attended = []
    for head in range(width // ENC_HEAD_DIM):
        cols = slice(head * ENC_HEAD_DIM, (head + 1) * ENC_HEAD_DIM)
        vals = slice(width + head * ENC_HEAD_DIM, width + (head + 1) * ENC_HEAD_DIM)
        exponents = jnp.exp(dot(cond[:, cols], queries[:, cols], ROWS_T) * ENC_SCALING)
        probs = exponents / jnp.sum(exponents, axis=0, keepdims=True)
        probs_ref[head * length : (head + 1) * length, :] = probs
        attended.append(dot(probs.astype(BF16), cond[:, vals], COLS_T).astype(BF16))
    attended = jnp.concatenate(attended, axis=1)
    mixing = dot(attended, enc_out_ref[...])
    encoded_ref[...] = (x.astype(F32) + mixing).astype(BF16)


def attention_kernel(
    s_ref,
    encoded_ref,
    key_w_ref,
    val_w_ref,
    query_ref,
    probs_ref,
    d_scores_ref,
    out_ref,
):
    width = encoded_ref.shape[1]
    length = out_ref.shape[1]
    encoded = encoded_ref[...]
    keys = dot(encoded, key_w_ref[...].reshape(-1, key_w_ref.shape[3])[:width]).astype(BF16)
    vals = dot(encoded, val_w_ref[...].reshape(-1, val_w_ref.shape[3])[:width]).astype(BF16)
    count = s_ref[1]
    scores = dot(by_heads(query_ref[0, 0], HEAD_DIM), keys, ROWS_T) * SCALING
    expd = jnp.where(live_columns(count, scores.shape), jnp.exp(scores), 0.0)
    totals = jnp.sum(expd, axis=1, keepdims=True)
    probs = expd / jnp.where(count > 0, totals, 1.0)
    probs_low = probs.astype(BF16)
    probs_ref[0] = probs_low
    ctx = head_blocks(dot(probs_low, vals), length, HEAD_DIM)
    out_ref[0] = jnp.concatenate(ctx, axis=1).astype(BF16)
    weighted = probs * dot(by_heads(query_ref[0, 1], HEAD_DIM), vals, ROWS_T)
    d_scores = (weighted - probs * jnp.sum(weighted, axis=1, keepdims=True)) * SCALING
    d_scores = d_scores.astype(BF16)
    d_scores_ref[0] = d_scores
    d_query = head_blocks(dot(d_scores, keys), length, HEAD_DIM)
    out_ref[1] = jnp.concatenate(d_query, axis=1).astype(BF16)


def encoded_back_kernel(
    s_ref,
    d_scores_ref,
    probs_ref,
    query_ref,
    key_w_ref,
    val_w_ref,
    enc_out_ref,
    enc_probs_ref,
    enc_queries_ref,
    cond_ref,
    d_cond_ref,
    total_ref,
):
    step = pl.program_id(0)
    width = total_ref.shape[1]
    d_keys = dot(d_scores_ref[0], by_heads(query_ref[0, 0], HEAD_DIM), COLS_T).astype(BF16)
    d_vals = dot(probs_ref[0], by_heads(query_ref[0, 1], HEAD_DIM), COLS_T).astype(BF16)
    term = dot(d_keys, key_w_ref[...].reshape(-1, key_w_ref.shape[3])[:width], ROWS_T)
    term = term + dot(d_vals, val_w_ref[...].reshape(-1, val_w_ref.shape[3])[:width], ROWS_T)
    term = term.astype(BF16).astype(F32)

    @pl.when(step == 0)
    def _():
        total_ref[...] = term

    @pl.when(step > 0)
    def _():
        total_ref[...] += term

    @pl.when(step == pl.num_programs(0) - 1)
    def _():
        length = cond_ref.shape[0]
        d_att = dot(total_ref[...].astype(BF16), enc_out_ref[...], ROWS_T).astype(BF16)
        probs = enc_probs_ref[...]
        d_probs = dot(by_heads(cond_ref[:, width:], ENC_HEAD_DIM), d_att, ROWS_T)
        weighted = probs * d_probs
        sums = jnp.sum(weighted.reshape(-1, length, weighted.shape[1]), axis=1, keepdims=True)
        spread_sums = (probs.reshape(-1, length, probs.shape[1]) * sums).reshape(probs.shape)
        d_scores = (weighted - spread_sums) * ENC_SCALING
        live = live_columns(s_ref[1], probs.shape)
        d_scores = jnp.where(live, d_scores, 0.0).astype(BF16)
        low = jnp.where(live, probs, 0.0).astype(BF16)
        d_keys = head_blocks(dot(d_scores, enc_queries_ref[...]), length, ENC_HEAD_DIM)
        d_vals = head_blocks(dot(low, d_att), length, ENC_HEAD_DIM)
        d_cond_ref[...] = jnp.concatenate(d_keys + d_vals, axis=1).astype(BF16)


def placed_rows(rows, by, shift):
    moved = pltpu.roll(rows, by, 0)
    if shift == 0:
        return moved
    index = lax.broadcasted_iota(jnp.int32, rows.shape, 0)
    return jnp.where(index >= shift, moved, 0.0)


def mix_kernel(shift, s_ref, c0, c1, c2, c3, weight_ref, base_ref, out_ref, total_ref):
    step = pl.program_id(0)
    half = weight_ref.shape[2] // 2
    wide = weight_ref.shape[3]
    length = c0.shape[1]
    ctx = jnp.concatenate([c0[0], c1[0], c2[0], c3[0]], axis=0)

    @pl.when(step == 0)
    def _():
        total_ref[...] = jnp.zeros_like(total_ref)

    for side in range(2):
        weight = weight_ref[:, :, side * half : (side + 1) * half, :].reshape(-1, wide)
        total_ref[:, side * wide : (side + 1) * wide] += dot(ctx, weight)

    @pl.when(step == pl.num_programs(0) - 1)
    def _():
        by = (s_ref[0] * length + shift) % total_ref.shape[0]
        moved = placed_rows(total_ref[...], by, shift)
        out_ref[...] = (base_ref[...].astype(F32) + moved).astype(out_ref.dtype)


def query_grad_kernel(shift, s_ref, c0, c1, c2, c3, weight_ref, base_ref, out_ref, total_ref):
    step = pl.program_id(0)
    length = c0.shape[1]
    weight = weight_ref[...].reshape(-1, weight_ref.shape[3])
    d_query = jnp.concatenate([c0[0], c1[0], c2[0], c3[0]], axis=0)
    term = dot(d_query, weight, ROWS_T)

    @pl.when(step == 0)
    def _():
        total_ref[...] = term

    @pl.when(step > 0)
    def _():
        total_ref[...] += term

    @pl.when(step == pl.num_programs(0) - 1)
    def _():
        by = (s_ref[0] * length + shift) % total_ref.shape[0]
        out_ref[...] = base_ref[...].astype(F32) + placed_rows(total_ref[...], by, shift)


def cond_grad_kernel(s_ref, c0, c1, c2, c3, weight_ref, base_ref, out_ref):
    length = c0.shape[0]
    d_cond = jnp.concatenate([c0[...], c1[...], c2[...], c3[...]], axis=0)
    term = dot(d_cond, weight_ref[...], ROWS_T)
    by = s_ref[0] * length
    out_ref[...] = (base_ref[...] + placed_rows(term, by, 0)).astype(out_ref.dtype)


def shards(
    hidden,
    cotangent,
    counts,
    slot_of,
    neighbours,
    query_weight,
    key_weight,
    value_weight,
    out_weight,
    cond_weight,
    enc_query,
    enc_out,
):
    tokens, part_width = hidden.shape
    head_width = query_weight.shape[1]
    blocks = counts.shape[1]
    slots_per = slot_of.shape[2]
    item_total = blocks * slots_per
    slot_total, quarter, enc_width = neighbours.shape
    block_len = tokens // blocks
    shift = block_len - 1
    n_tensor = lax.axis_size("tensor")
    n_dp = lax.axis_size("dp")
    here = lax.axis_index("tensor")
    row = lax.axis_index("dp")
    all_width = head_width * n_tensor
    rows = slots_per * quarter * n_tensor
    enc_rows = enc_width // ENC_HEAD_DIM * block_len
    head_rows = head_width // HEAD_DIM * block_len
    sds = jax.ShapeDtypeStruct

    seq_counts = counts[0]
    count = lax.dynamic_slice_in_dim(seq_counts, here, 1, 0)
    scalars = jnp.concatenate([here.astype(jnp.int32)[None], count])

    wq_part = lax.dynamic_slice_in_dim(
        query_weight.reshape(n_tensor, part_width, head_width), row * SLICE, SLICE, 1
    )
    wo_part = lax.dynamic_slice_in_dim(out_weight, row * (SLICE // 2), SLICE // 2, 0)
    wo_part = wo_part.reshape(SLICE // 2, n_tensor, 2, head_width).transpose(1, 2, 0, 3)
    wo_part = wo_part.reshape(n_tensor, SLICE, head_width)
    kv_part = jnp.concatenate(
        [
            lax.dynamic_slice_in_dim(key_weight, row * SLICE, SLICE, 0),
            lax.dynamic_slice_in_dim(value_weight, row * SLICE, SLICE, 0),
        ],
        axis=0,
    )
    kv_part = jnp.broadcast_to(kv_part[None], (n_tensor, 2 * SLICE, head_width))
    weight_parts = exchange(jnp.concatenate([kv_part, wq_part, wo_part], axis=1), here)
    kv_parts = jnp.stack([part[: 2 * SLICE] for part in weight_parts])
    qo_parts = jnp.stack([part[2 * SLICE :] for part in weight_parts])
    kv_all = lax.all_gather(kv_parts, "dp", axis=0)

    def weight_spec(index):
        return pl.BlockSpec((n_dp, 1, SLICE, head_width), lambda g, s: (0, g, index, 0))

    cond_part = dot(hidden, cond_weight).astype(BF16).reshape(blocks, block_len, 2 * enc_width)
    cond_parts = tuple(exchange(cond_part, here))
    hidden_parts = tuple(spread(hidden, n_tensor))

    live = jnp.arange(slots_per)[None, :] < after(seq_counts, (cond_parts[1:], hidden_parts[1:]))[:, None]
    slot_flat = slot_of.reshape(item_total)
    matches = (jnp.arange(slot_total)[:, None] == slot_flat[None, :]) & live.reshape(item_total)[
        None, :
    ]
    returned = lax.all_to_all(neighbours, "dp", split_axis=0, concat_axis=0, tiled=True)
    items = jnp.einsum(
        "si,sre->ire", matches.astype(BF16), returned, preferred_element_type=F32
    ).astype(BF16)
    items = items.reshape(blocks, slots_per * quarter, enc_width)
    x = lax.all_to_all(items, "tensor", split_axis=0, concat_axis=0, tiled=True)
    x = x.reshape(rows, enc_width)

    def projected(parts, weight, dims, weight_block, weight_map, name, before=None):
        out = (tokens, head_width)
        if before is not None:
            out = (blocks, 2, block_len, head_width)
        return call(
            functools.partial(project_kernel, dims, shift),
            name,
            n_tensor,
            [whole(tokens, part_width)] * 4
            + [pl.BlockSpec(weight_block, weight_map)]
            + ([] if before is None else [whole(tokens, head_width)]),
            whole(*out),
            sds(out, BF16),
            [pltpu.VMEM((tokens, head_width), F32)],
            16,
        )(scalars, *parts, weight, *([] if before is None else [before]))

    query = projected(
        after(hidden_parts, x),
        query_weight,
        PLAIN,
        (part_width, head_width),
        lambda g, s: ((s[0] + g) % 4, 0),
        "query",
    )
    qo_all = lax.all_gather(after(qo_parts, items), "dp", axis=0)
    query_d_ctx = projected(
        spread(after(cotangent, (hidden_parts[1:], cond_parts[1:])), n_tensor),
        out_weight,
        ROWS_T,
        (head_width, part_width),
        lambda g, s: (0, (s[0] + g) % 4),
        "d_ctx",
        before=query,
    )
    query_d_ctx = lax.all_to_all(query_d_ctx, "tensor", split_axis=0, concat_axis=0, tiled=True)

    c_spec = whole(block_len, 2 * enc_width)
    w_spec = whole(enc_width, enc_width)
    r_spec = whole(rows, enc_width)
    p_spec = whole(enc_rows, rows)
    cond, enc_queries, enc_probs, encoded = call(
        encode_kernel,
        "encode",
        1,
        [r_spec] + [c_spec] * 4 + [w_spec] * 2,
        (c_spec, r_spec, p_spec, r_spec),
        (
            sds((block_len, 2 * enc_width), BF16),
            sds((rows, enc_width), BF16),
            sds((enc_rows, rows), F32),
            sds((rows, enc_width), BF16),
        ),
        [],
        24,
    )(scalars, x, *cond_parts, enc_query, enc_out)

    q_spec = pl.BlockSpec((1, 2, block_len, head_width), lambda g, s: ((s[0] + g) % 4, 0, 0, 0))
    probs, d_scores, both = call(
        attention_kernel,
        "attention",
        n_tensor,
        [r_spec, weight_spec(0), weight_spec(1), q_spec],
        (
            group(head_rows, rows),
            group(head_rows, rows),
            pl.BlockSpec((2, block_len, head_width), lambda g, s: (0, 0, (s[0] + g) % 4)),
        ),
        (
            sds((n_tensor, head_rows, rows), BF16),
            sds((n_tensor, head_rows, rows), BF16),
            sds((2, block_len, all_width), BF16),
        ),
        [],
        28,
    )(scalars, encoded, kv_all, kv_all, query_d_ctx)
    both_parts = spread(both, n_tensor)

    d_cond = call(
        encoded_back_kernel,
        "encoded_back",
        n_tensor,
        [group(head_rows, rows), group(head_rows, rows)]
        + [q_spec, weight_spec(0), weight_spec(1), w_spec, p_spec, r_spec, c_spec],
        c_spec,
        sds((block_len, 2 * enc_width), BF16),
        [pltpu.VMEM((rows, enc_width), F32)],
        32,
    )(
        scalars,
        d_scores,
        probs,
        query_d_ctx,
        kv_all,
        kv_all,
        enc_out,
        enc_probs,
        enc_queries,
        cond,
    )
    d_cond_parts = spread(d_cond, n_tensor)

    out_spec = whole(tokens, part_width)
    acc = pltpu.VMEM((tokens, part_width), F32)

    def col_spec(which):
        return pl.BlockSpec(
            (1, block_len, head_width), lambda g, s: (which, 0, (s[0] + g) % 4)
        )

    mixed = call(
        functools.partial(mix_kernel, shift),
        "mix",
        n_tensor,
        [col_spec(0)] * 4 + [weight_spec(1), out_spec],
        out_spec,
        sds((tokens, part_width), BF16),
        [acc],
        16,
    )(scalars, *both_parts, qo_all, hidden)
    from_query = call(
        functools.partial(query_grad_kernel, shift),
        "query_grad",
        n_tensor,
        [col_spec(1)] * 4 + [weight_spec(0), out_spec],
        out_spec,
        sds((tokens, part_width), F32),
        [acc],
        16,
    )(scalars, *both_parts, qo_all, cotangent)
    grad_hidden = call(
        cond_grad_kernel,
        "cond_grad",
        1,
        [c_spec] * 4 + [whole(part_width, 2 * enc_width), out_spec],
        out_spec,
        sds((tokens, part_width), BF16),
        [],
        16,
    )(scalars, *d_cond_parts, cond_weight, from_query)
    return (mixed, grad_hidden)


def solution(mesh):
    placed = (
        P("dp", "tensor"),
        P("dp", "tensor"),
        P("dp", None),
        P("dp", None, None),
        P("dp", "tensor", None),
        P(None, "tensor"),
        P(None, "tensor"),
        P(None, "tensor"),
        P("tensor", None),
        P("tensor", None),
        P(),
        P(),
    )
    return jax.shard_map(
        shards,
        mesh=mesh,
        in_specs=placed,
        out_specs=(P("dp", "tensor"), P("dp", "tensor")),
        check_vma=False,
    )
```

```python
import functools
import math

import jax
import jax.numpy as jnp
from jax import lax
from jax.experimental import pallas as pl
from jax.experimental.pallas import tpu as pltpu
from jax.sharding import PartitionSpec as P

HEAD_DIM = 128
ENC_HEAD_DIM = 128
F32 = jnp.float32
BF16 = jnp.bfloat16
PLAIN = (((1,), (0,)), ((), ()))
ROWS_T = (((1,), (1,)), ((), ()))
COLS_T = (((0,), (0,)), ((), ()))
SCALING = 1.0 / math.sqrt(HEAD_DIM)
ENC_SCALING = 1.0 / math.sqrt(ENC_HEAD_DIM)
SLICE = 32


def dot(a, b, dims=PLAIN):
    return lax.dot_general(a, b, dims, preferred_element_type=F32)


def call(kernel, name, grid, in_specs, out_specs, out_shape, scratch, vmem_mib):
    return pl.pallas_call(
        kernel,
        out_shape=out_shape,
        grid_spec=pltpu.PrefetchScalarGridSpec(
            num_scalar_prefetch=1,
            grid=(grid,),
            in_specs=in_specs,
            out_specs=out_specs,
            scratch_shapes=scratch,
        ),
        compiler_params=pltpu.CompilerParams(
            vmem_limit_bytes=vmem_mib * 1024 * 1024, dimension_semantics=("arbitrary",)
        ),
        name=name,
    )


def whole(*shape):
    return pl.BlockSpec(shape, lambda g, s: (0,) * len(shape))


def group(*shape):
    return pl.BlockSpec((1,) + shape, lambda g, s: (g,) + (0,) * len(shape))


def exchange(pieces, position, axis="tensor"):
    size = pieces.shape[0]
    out = [lax.dynamic_index_in_dim(pieces, position, 0, keepdims=False)]
    for k in range(1, size):
        piece = lax.dynamic_index_in_dim(pieces, (position - k) % size, 0, keepdims=False)
        out.append(lax.ppermute(piece, axis, [(i, (i - k) % size) for i in range(size)]))
    return out


def spread(shard, size, axis="tensor"):
    return [shard] + [
        lax.ppermute(shard, axis, [(i, (i - k) % size) for i in range(size)])
        for k in range(1, size)
    ]


def after(value, earlier):
    return lax.optimization_barrier((value, earlier))[0]


def live_columns(count, shape):
    column = lax.broadcasted_iota(jnp.int32, shape, len(shape) - 1)
    return (column // 32) % 4 < count


def by_heads(array, head_dim):
    head = lax.broadcasted_iota(jnp.int32, array.shape, 1) // head_dim
    zero = jnp.zeros_like(array)
    count = array.shape[1] // head_dim
    return jnp.concatenate([jnp.where(head == h, array, zero) for h in range(count)], axis=0)


def head_blocks(array, rows, head_dim):
    count = array.shape[1] // head_dim
    return [
        array[h * rows : (h + 1) * rows, h * head_dim : (h + 1) * head_dim] for h in range(count)
    ]


def pack_kernel(s_ref, hidden_ref, weight_ref, own_ref, p1, p2, p3, total_ref):
    length, width = own_ref.shape
    rows, part = hidden_ref.shape
    total_ref[...] = dot(hidden_ref[...], weight_ref[...])

    def block_of(k):
        start = pl.multiple_of(((s_ref[0] + 4 - k) % 4) * length, length)
        return total_ref[pl.ds(start, length), :].astype(BF16)

    own_ref[...] = block_of(0)
    for k, ref in ((1, p1), (2, p2), (3, p3)):
        block = block_of(k)
        ref[:rows, :] = hidden_ref[...]
        ref[rows : rows + length, :] = block[:, :part]
        ref[rows + length :, : width - part] = block[:, part:]
        ref[rows + length :, width - part :] = jnp.zeros((length, 2 * part - width), BF16)


def project_kernel(dims, shift, s_ref, p0, p1, p2, p3, weight_ref, *rest):
    out_ref, total_ref = rest[-2:]
    step = pl.program_id(0)
    for k, ref in enumerate((p0, p1, p2, p3)):

        @pl.when(step == k)
        def _(ref=ref, k=k):
            term = dot(ref[: total_ref.shape[0], :], weight_ref[...], dims)
            total_ref[...] = term if k == 0 else total_ref[...] + term

    @pl.when(step == pl.num_programs(0) - 1)
    def _():
        rows = total_ref.shape[0]
        moved = pltpu.roll(total_ref[...], rows - shift, 0)
        index = lax.broadcasted_iota(jnp.int32, moved.shape, 0)
        result = jnp.where(index < rows - shift, moved, 0.0).astype(BF16)
        if len(rest) == 2:
            out_ref[...] = result
        else:
            blocks, _, length, _ = out_ref.shape
            for block in range(blocks):
                span = slice(block * length, (block + 1) * length)
                out_ref[block, 0] = rest[0][span, :]
                out_ref[block, 1] = result[span, :]


def encode_kernel(
    s_ref,
    x_ref,
    c0,
    c1,
    c2,
    c3,
    enc_query_ref,
    enc_out_ref,
    cond_ref,
    queries_ref,
    probs_ref,
    encoded_ref,
):
    width = x_ref.shape[1]
    x = x_ref[...]
    half = c1.shape[0] // 2
    cond = c0[...].astype(F32)
    for ref in (c1, c2, c3):
        low, high = ref[:half, :], ref[half:, : 2 * width - ref.shape[1]]
        cond = cond + jnp.concatenate([low, high], axis=1).astype(F32)
    cond = cond.astype(BF16)
    cond_ref[...] = cond
    length = cond.shape[0]
    queries = dot(x, enc_query_ref[...]).astype(BF16)
    queries_ref[...] = queries
    attended = []
    for head in range(width // ENC_HEAD_DIM):
        cols = slice(head * ENC_HEAD_DIM, (head + 1) * ENC_HEAD_DIM)
        vals = slice(width + head * ENC_HEAD_DIM, width + (head + 1) * ENC_HEAD_DIM)
        exponents = jnp.exp(dot(cond[:, cols], queries[:, cols], ROWS_T) * ENC_SCALING)
        probs = exponents / jnp.sum(exponents, axis=0, keepdims=True)
        probs_ref[head * length : (head + 1) * length, :] = probs
        attended.append(dot(probs.astype(BF16), cond[:, vals], COLS_T).astype(BF16))
    attended = jnp.concatenate(attended, axis=1)
    mixing = dot(attended, enc_out_ref[...])
    encoded_ref[...] = (x.astype(F32) + mixing).astype(BF16)


def attention_kernel(
    s_ref,
    encoded_ref,
    key_w_ref,
    val_w_ref,
    query_ref,
    probs_ref,
    d_scores_ref,
    out_ref,
):
    width = encoded_ref.shape[1]
    length = out_ref.shape[1]
    encoded = encoded_ref[...]
    keys = dot(encoded, key_w_ref[...].reshape(-1, key_w_ref.shape[3])[:width]).astype(BF16)
    vals = dot(encoded, val_w_ref[...].reshape(-1, val_w_ref.shape[3])[:width]).astype(BF16)
    count = s_ref[1]
    scores = dot(by_heads(query_ref[0, 0], HEAD_DIM), keys, ROWS_T) * SCALING
    expd = jnp.where(live_columns(count, scores.shape), jnp.exp(scores), 0.0)
    totals = jnp.sum(expd, axis=1, keepdims=True)
    probs = expd / jnp.where(count > 0, totals, 1.0)
    probs_low = probs.astype(BF16)
    probs_ref[0] = probs_low
    ctx = head_blocks(dot(probs_low, vals), length, HEAD_DIM)
    out_ref[0] = jnp.concatenate(ctx, axis=1).astype(BF16)
    weighted = probs * dot(by_heads(query_ref[0, 1], HEAD_DIM), vals, ROWS_T)
    d_scores = (weighted - probs * jnp.sum(weighted, axis=1, keepdims=True)) * SCALING
    d_scores = d_scores.astype(BF16)
    d_scores_ref[0] = d_scores
    d_query = head_blocks(dot(d_scores, keys), length, HEAD_DIM)
    out_ref[1] = jnp.concatenate(d_query, axis=1).astype(BF16)


def encoded_back_kernel(
    s_ref,
    d_scores_ref,
    probs_ref,
    query_ref,
    key_w_ref,
    val_w_ref,
    enc_out_ref,
    enc_probs_ref,
    enc_queries_ref,
    cond_ref,
    d_cond_ref,
    total_ref,
):
    step = pl.program_id(0)
    width = total_ref.shape[1]
    d_keys = dot(d_scores_ref[0], by_heads(query_ref[0, 0], HEAD_DIM), COLS_T).astype(BF16)
    d_vals = dot(probs_ref[0], by_heads(query_ref[0, 1], HEAD_DIM), COLS_T).astype(BF16)
    term = dot(d_keys, key_w_ref[...].reshape(-1, key_w_ref.shape[3])[:width], ROWS_T)
    term = term + dot(d_vals, val_w_ref[...].reshape(-1, val_w_ref.shape[3])[:width], ROWS_T)
    term = term.astype(BF16).astype(F32)

    @pl.when(step == 0)
    def _():
        total_ref[...] = term

    @pl.when(step > 0)
    def _():
        total_ref[...] += term

    @pl.when(step == pl.num_programs(0) - 1)
    def _():
        length = cond_ref.shape[0]
        d_att = dot(total_ref[...].astype(BF16), enc_out_ref[...], ROWS_T).astype(BF16)
        probs = enc_probs_ref[...]
        d_probs = dot(by_heads(cond_ref[:, width:], ENC_HEAD_DIM), d_att, ROWS_T)
        weighted = probs * d_probs
        sums = jnp.sum(weighted.reshape(-1, length, weighted.shape[1]), axis=1, keepdims=True)
        spread_sums = (probs.reshape(-1, length, probs.shape[1]) * sums).reshape(probs.shape)
        d_scores = (weighted - spread_sums) * ENC_SCALING
        live = live_columns(s_ref[1], probs.shape)
        d_scores = jnp.where(live, d_scores, 0.0).astype(BF16)
        low = jnp.where(live, probs, 0.0).astype(BF16)
        d_keys = head_blocks(dot(d_scores, enc_queries_ref[...]), length, ENC_HEAD_DIM)
        d_vals = head_blocks(dot(low, d_att), length, ENC_HEAD_DIM)
        d_cond_ref[...] = jnp.concatenate(d_keys + d_vals, axis=1).astype(BF16)


def placed_rows(rows, by, shift):
    moved = pltpu.roll(rows, by, 0)
    if shift == 0:
        return moved
    index = lax.broadcasted_iota(jnp.int32, rows.shape, 0)
    return jnp.where(index >= shift, moved, 0.0)


def outputs_kernel(
    shift,
    s_ref,
    c0,
    c1,
    c2,
    c3,
    out_w_ref,
    query_w_ref,
    hidden_ref,
    cotangent_ref,
    mixed_ref,
    grad_ref,
    mixed_sum_ref,
    grad_sum_ref,
):
    step = pl.program_id(0)
    half = out_w_ref.shape[2] // 2
    wide = out_w_ref.shape[3]
    length = c0.shape[1]
    parts = (c0, c1, c2, c3)
    ctx = jnp.concatenate([ref[0] for ref in parts], axis=0)
    d_query = jnp.concatenate([ref[1] for ref in parts], axis=0)

    @pl.when(step == 0)
    def _():
        mixed_sum_ref[...] = jnp.zeros_like(mixed_sum_ref)
        grad_sum_ref[...] = jnp.zeros_like(grad_sum_ref)

    for side in range(2):
        weight = out_w_ref[:, :, side * half : (side + 1) * half, :].reshape(-1, wide)
        mixed_sum_ref[:, side * wide : (side + 1) * wide] += dot(ctx, weight)
    grad_sum_ref[...] += dot(d_query, query_w_ref[...].reshape(-1, wide), ROWS_T)

    @pl.when(step == pl.num_programs(0) - 1)
    def _():
        by = (s_ref[0] * length + shift) % mixed_ref.shape[0]
        moved = placed_rows(mixed_sum_ref[...], by, shift)
        mixed_ref[...] = (hidden_ref[...].astype(F32) + moved).astype(mixed_ref.dtype)
        moved = placed_rows(grad_sum_ref[...], by, shift)
        grad_ref[...] = cotangent_ref[...].astype(F32) + moved


def cond_grad_kernel(s_ref, c0, c1, c2, c3, weight_ref, base_ref, out_ref):
    length = c0.shape[0]
    d_cond = jnp.concatenate([c0[...], c1[...], c2[...], c3[...]], axis=0)
    term = dot(d_cond, weight_ref[...], ROWS_T)
    by = s_ref[0] * length
    out_ref[...] = (base_ref[...] + placed_rows(term, by, 0)).astype(out_ref.dtype)


def shards(
    hidden,
    cotangent,
    counts,
    slot_of,
    neighbours,
    query_weight,
    key_weight,
    value_weight,
    out_weight,
    cond_weight,
    enc_query,
    enc_out,
):
    tokens, part_width = hidden.shape
    head_width = query_weight.shape[1]
    blocks = counts.shape[1]
    slots_per = slot_of.shape[2]
    item_total = blocks * slots_per
    slot_total, quarter, enc_width = neighbours.shape
    block_len = tokens // blocks
    shift = block_len - 1
    n_tensor = lax.axis_size("tensor")
    n_dp = lax.axis_size("dp")
    here = lax.axis_index("tensor")
    row = lax.axis_index("dp")
    all_width = head_width * n_tensor
    rows = slots_per * quarter * n_tensor
    enc_rows = enc_width // ENC_HEAD_DIM * block_len
    head_rows = head_width // HEAD_DIM * block_len
    sds = jax.ShapeDtypeStruct

    seq_counts = counts[0]
    count = lax.dynamic_slice_in_dim(seq_counts, here, 1, 0)
    scalars = jnp.concatenate([here.astype(jnp.int32)[None], count])

    wq_part = lax.dynamic_slice_in_dim(
        query_weight.reshape(n_tensor, part_width, head_width), row * SLICE, SLICE, 1
    )
    wo_part = lax.dynamic_slice_in_dim(out_weight, row * (SLICE // 2), SLICE // 2, 0)
    wo_part = wo_part.reshape(SLICE // 2, n_tensor, 2, head_width).transpose(1, 2, 0, 3)
    wo_part = wo_part.reshape(n_tensor, SLICE, head_width)
    kv_part = jnp.concatenate(
        [
            lax.dynamic_slice_in_dim(key_weight, row * SLICE, SLICE, 0),
            lax.dynamic_slice_in_dim(value_weight, row * SLICE, SLICE, 0),
        ],
        axis=0,
    )
    kv_all = lax.all_gather(kv_part, ("dp", "tensor"), axis=0)
    kv_all = kv_all.reshape(n_dp, n_tensor, 2 * SLICE, head_width)
    qo_parts = jnp.stack(exchange(jnp.concatenate([wq_part, wo_part], axis=1), here))

    def weight_spec(index):
        return pl.BlockSpec((n_dp, 1, SLICE, head_width), lambda g, s: (0, g, index, 0))

    packed = sds((tokens + 2 * block_len, part_width), BF16)
    own_cond, *to_send = call(
        pack_kernel,
        "pack",
        1,
        [whole(tokens, part_width), whole(part_width, 2 * enc_width)],
        (whole(block_len, 2 * enc_width),) + (whole(*packed.shape),) * 3,
        (sds((block_len, 2 * enc_width), BF16),) + (packed,) * 3,
        [pltpu.VMEM((tokens, 2 * enc_width), F32)],
        20,
    )(scalars, hidden, cond_weight)
    got = tuple(
        lax.ppermute(array, "tensor", [(i, (i - k) % n_tensor) for i in range(n_tensor)])
        for k, array in enumerate(to_send, 1)
    )

    live = jnp.arange(slots_per)[None, :] < after(seq_counts, got)[:, None]
    slot_flat = slot_of.reshape(item_total)
    matches = (jnp.arange(slot_total)[:, None] == slot_flat[None, :]) & live.reshape(item_total)[
        None, :
    ]
    returned = lax.all_to_all(neighbours, "dp", split_axis=0, concat_axis=0, tiled=True)
    items = jnp.einsum(
        "si,sre->ire", matches.astype(BF16), returned, preferred_element_type=F32
    ).astype(BF16)
    items = items.reshape(blocks, slots_per * quarter, enc_width)
    x = lax.all_to_all(items, "tensor", split_axis=0, concat_axis=0, tiled=True)
    x = x.reshape(rows, enc_width)

    def projected(parts, weight, dims, weight_block, weight_map, name, before=None):
        out = (tokens, head_width)
        if before is not None:
            out = (blocks, 2, block_len, head_width)
        return call(
            functools.partial(project_kernel, dims, shift),
            name,
            n_tensor,
            [whole(*part.shape) for part in parts]
            + [pl.BlockSpec(weight_block, weight_map)]
            + ([] if before is None else [whole(tokens, head_width)]),
            whole(*out),
            sds(out, BF16),
            [pltpu.VMEM((tokens, head_width), F32)],
            16,
        )(scalars, *parts, weight, *([] if before is None else [before]))

    query = projected(
        after((hidden,) + got, x),
        query_weight,
        PLAIN,
        (part_width, head_width),
        lambda g, s: ((s[0] + g) % 4, 0),
        "query",
    )
    qo_all = lax.all_gather(after(qo_parts, items), "dp", axis=0)
    query_d_ctx = projected(
        spread(after(cotangent, (got, items)), n_tensor),
        out_weight,
        ROWS_T,
        (head_width, part_width),
        lambda g, s: (0, (s[0] + g) % 4),
        "d_ctx",
        before=query,
    )
    query_d_ctx = lax.all_to_all(query_d_ctx, "tensor", split_axis=0, concat_axis=0, tiled=True)

    c_spec = whole(block_len, 2 * enc_width)
    w_spec = whole(enc_width, enc_width)
    r_spec = whole(rows, enc_width)
    p_spec = whole(enc_rows, rows)
    cond, enc_queries, enc_probs, encoded = call(
        encode_kernel,
        "encode",
        1,
        [r_spec, c_spec] + [pl.BlockSpec((2 * block_len, part_width), lambda g, s: (2, 0))] * 3
        + [w_spec] * 2,
        (c_spec, r_spec, p_spec, r_spec),
        (
            sds((block_len, 2 * enc_width), BF16),
            sds((rows, enc_width), BF16),
            sds((enc_rows, rows), F32),
            sds((rows, enc_width), BF16),
        ),
        [],
        60,
    )(scalars, x, own_cond, *got, enc_query, enc_out)

    q_spec = group(2, block_len, head_width)
    probs, d_scores, both = call(
        attention_kernel,
        "attention",
        n_tensor,
        [r_spec, weight_spec(0), weight_spec(1), q_spec],
        (
            group(head_rows, rows),
            group(head_rows, rows),
            pl.BlockSpec((2, block_len, head_width), lambda g, s: (0, 0, g)),
        ),
        (
            sds((n_tensor, head_rows, rows), BF16),
            sds((n_tensor, head_rows, rows), BF16),
            sds((2, block_len, all_width), BF16),
        ),
        [],
        60,
    )(scalars, encoded, kv_all, kv_all, query_d_ctx)
    both_parts = spread(both, n_tensor)

    d_cond = call(
        encoded_back_kernel,
        "encoded_back",
        n_tensor,
        [group(head_rows, rows), group(head_rows, rows)]
        + [q_spec, weight_spec(0), weight_spec(1), w_spec, p_spec, r_spec, c_spec],
        c_spec,
        sds((block_len, 2 * enc_width), BF16),
        [pltpu.VMEM((rows, enc_width), F32)],
        60,
    )(
        scalars,
        d_scores,
        probs,
        query_d_ctx,
        kv_all,
        kv_all,
        enc_out,
        enc_probs,
        enc_queries,
        cond,
    )
    d_cond_parts = spread(d_cond, n_tensor)

    out_spec = whole(tokens, part_width)
    acc = pltpu.VMEM((tokens, part_width), F32)
    both_spec = pl.BlockSpec((2, block_len, head_width), lambda g, s: (0, 0, (s[0] + g) % 4))
    mixed, from_query = call(
        functools.partial(outputs_kernel, shift),
        "outputs",
        n_tensor,
        [both_spec] * 4 + [weight_spec(1), weight_spec(0), out_spec, out_spec],
        (out_spec, out_spec),
        (sds((tokens, part_width), BF16), sds((tokens, part_width), F32)),
        [acc, acc],
        60,
    )(scalars, *both_parts, qo_all, qo_all, hidden, cotangent)
    grad_hidden = call(
        cond_grad_kernel,
        "cond_grad",
        1,
        [c_spec] * 4 + [whole(part_width, 2 * enc_width), out_spec],
        out_spec,
        sds((tokens, part_width), BF16),
        [],
        16,
    )(scalars, *d_cond_parts, cond_weight, from_query)
    return (mixed, grad_hidden)


def solution(mesh):
    placed = (
        P("dp", "tensor"),
        P("dp", "tensor"),
        P("dp", None),
        P("dp", None, None),
        P("dp", "tensor", None),
        P(None, "tensor"),
        P(None, "tensor"),
        P(None, "tensor"),
        P("tensor", None),
        P("tensor", None),
        P(),
        P(),
    )
    return jax.shard_map(
        shards,
        mesh=mesh,
        in_specs=placed,
        out_specs=(P("dp", "tensor"), P("dp", "tensor")),
        check_vma=False,
    )
```

```python
import functools
import math

import jax
import jax.numpy as jnp
from jax import lax
from jax.experimental import pallas as pl
from jax.experimental.pallas import tpu as pltpu
from jax.sharding import PartitionSpec as P

HEAD_DIM = 128
ENC_HEAD_DIM = 128
F32 = jnp.float32
BF16 = jnp.bfloat16
PLAIN = (((1,), (0,)), ((), ()))
ROWS_T = (((1,), (1,)), ((), ()))
COLS_T = (((0,), (0,)), ((), ()))
SCALING = 1.0 / math.sqrt(HEAD_DIM)
ENC_SCALING = 1.0 / math.sqrt(ENC_HEAD_DIM)
SLICE = 32


def dot(a, b, dims=PLAIN):
    return lax.dot_general(a, b, dims, preferred_element_type=F32)


def call(kernel, name, grid, in_specs, out_specs, out_shape, scratch, vmem_mib):
    return pl.pallas_call(
        kernel,
        out_shape=out_shape,
        grid_spec=pltpu.PrefetchScalarGridSpec(
            num_scalar_prefetch=1,
            grid=(grid,),
            in_specs=in_specs,
            out_specs=out_specs,
            scratch_shapes=scratch,
        ),
        compiler_params=pltpu.CompilerParams(
            vmem_limit_bytes=vmem_mib * 1024 * 1024, dimension_semantics=("arbitrary",)
        ),
        name=name,
    )


def whole(*shape):
    return pl.BlockSpec(shape, lambda g, s: (0,) * len(shape))


def group(*shape):
    return pl.BlockSpec((1,) + shape, lambda g, s: (g,) + (0,) * len(shape))


def exchange(pieces, position, axis="tensor"):
    size = pieces.shape[0]
    out = [lax.dynamic_index_in_dim(pieces, position, 0, keepdims=False)]
    for k in range(1, size):
        piece = lax.dynamic_index_in_dim(pieces, (position - k) % size, 0, keepdims=False)
        out.append(lax.ppermute(piece, axis, [(i, (i - k) % size) for i in range(size)]))
    return out


def spread(shard, size, axis="tensor"):
    return [shard] + [
        lax.ppermute(shard, axis, [(i, (i - k) % size) for i in range(size)])
        for k in range(1, size)
    ]


def after(value, earlier):
    return lax.optimization_barrier((value, earlier))[0]


def live_columns(count, shape):
    column = lax.broadcasted_iota(jnp.int32, shape, len(shape) - 1)
    return (column // 32) % 4 < count


def by_heads(array, head_dim):
    head = lax.broadcasted_iota(jnp.int32, array.shape, 1) // head_dim
    zero = jnp.zeros_like(array)
    count = array.shape[1] // head_dim
    return jnp.concatenate([jnp.where(head == h, array, zero) for h in range(count)], axis=0)


def head_blocks(array, rows, head_dim):
    count = array.shape[1] // head_dim
    return [
        array[h * rows : (h + 1) * rows, h * head_dim : (h + 1) * head_dim] for h in range(count)
    ]


def pack_kernel(s_ref, hidden_ref, weight_ref, own_ref, p1, p2, p3, total_ref):
    length, width = own_ref.shape
    rows, part = hidden_ref.shape
    total_ref[...] = dot(hidden_ref[...], weight_ref[...])

    def block_of(k):
        start = pl.multiple_of(((s_ref[0] + 4 - k) % 4) * length, length)
        return total_ref[pl.ds(start, length), :].astype(BF16)

    own_ref[...] = block_of(0)
    for k, ref in ((1, p1), (2, p2), (3, p3)):
        block = block_of(k)
        ref[:rows, :] = hidden_ref[...]
        ref[rows : rows + length, :] = block[:, :part]
        ref[rows + length :, : width - part] = block[:, part:]
        ref[rows + length :, width - part :] = jnp.zeros((length, 2 * part - width), BF16)


def project(dims, parts, weight_ref, total_ref):
    step = pl.program_id(0)
    for k, ref in enumerate(parts):

        @pl.when(step == k)
        def _(ref=ref, k=k):
            term = dot(ref[: total_ref.shape[0], :], weight_ref[...], dims)
            total_ref[...] = term if k == 0 else total_ref[...] + term


def shifted_up(total_ref, shift):
    rows = total_ref.shape[0]
    moved = pltpu.roll(total_ref[...], rows - shift, 0)
    index = lax.broadcasted_iota(jnp.int32, moved.shape, 0)
    return jnp.where(index < rows - shift, moved, 0.0)


def query_kernel(
    shift, s_ref, p0, p1, p2, p3, weight_ref, cot_ref, own_ref, o1, o2, o3, total_ref
):
    project(PLAIN, (p0, p1, p2, p3), weight_ref, total_ref)

    @pl.when(pl.program_id(0) == pl.num_programs(0) - 1)
    def _():
        rows, wide = total_ref.shape
        half = own_ref.shape[0]
        total_ref[...] = shifted_up(total_ref, shift)

        def halves_of(k):
            start = pl.multiple_of(((s_ref[0] + 4 - k) % 4) * 2 * half, 2 * half)
            block = total_ref[pl.ds(start, 2 * half), :].astype(BF16)
            return block[:half, :], block[half:, :]

        own_ref[:, :wide], own_ref[:, wide:] = halves_of(0)
        for k, ref in ((1, o1), (2, o2), (3, o3)):
            ref[:rows, :] = cot_ref[...]
            ref[rows:, :wide], ref[rows:, wide:] = halves_of(k)


def d_ctx_kernel(shift, s_ref, p0, p1, p2, p3, weight_ref, out_ref, total_ref):
    project(ROWS_T, (p0, p1, p2, p3), weight_ref, total_ref)

    @pl.when(pl.program_id(0) == pl.num_programs(0) - 1)
    def _():
        out_ref[...] = shifted_up(total_ref, shift).astype(BF16)


def pick_query(refs, heads_ref):
    step = pl.program_id(0)
    for k, ref in enumerate(refs):

        @pl.when(step == k)
        def _(ref=ref):
            wide = ref.shape[1] // 2
            query = jnp.concatenate([ref[:, :wide], ref[:, wide:]], axis=0)
            heads_ref[...] = by_heads(query, HEAD_DIM)


def encode_kernel(
    s_ref,
    x_ref,
    c0,
    c1,
    c2,
    c3,
    enc_query_ref,
    enc_out_ref,
    cond_ref,
    queries_ref,
    probs_ref,
    encoded_ref,
):
    width = x_ref.shape[1]
    x = x_ref[...]
    half = c1.shape[0] // 2
    cond = c0[...].astype(F32)
    for ref in (c1, c2, c3):
        low, high = ref[:half, :], ref[half:, : 2 * width - ref.shape[1]]
        cond = cond + jnp.concatenate([low, high], axis=1).astype(F32)
    cond = cond.astype(BF16)
    cond_ref[...] = cond
    length = cond.shape[0]
    queries = dot(x, enc_query_ref[...]).astype(BF16)
    queries_ref[...] = queries
    attended = []
    for head in range(width // ENC_HEAD_DIM):
        cols = slice(head * ENC_HEAD_DIM, (head + 1) * ENC_HEAD_DIM)
        vals = slice(width + head * ENC_HEAD_DIM, width + (head + 1) * ENC_HEAD_DIM)
        exponents = jnp.exp(dot(cond[:, cols], queries[:, cols], ROWS_T) * ENC_SCALING)
        probs = exponents / jnp.sum(exponents, axis=0, keepdims=True)
        probs_ref[head * length : (head + 1) * length, :] = probs
        attended.append(dot(probs.astype(BF16), cond[:, vals], COLS_T).astype(BF16))
    attended = jnp.concatenate(attended, axis=1)
    mixing = dot(attended, enc_out_ref[...])
    encoded_ref[...] = (x.astype(F32) + mixing).astype(BF16)


def attend_kernel(
    s_ref,
    encoded_ref,
    key_w_ref,
    val_w_ref,
    q0,
    q1,
    q2,
    q3,
    keys_ref,
    vals_ref,
    probs_ref,
    ctx_ref,
    query_ref,
):
    width = encoded_ref.shape[1]
    pick_query((q0, q1, q2, q3), query_ref)
    encoded = encoded_ref[...]
    keys = dot(encoded, key_w_ref[...].reshape(-1, key_w_ref.shape[3])[:width]).astype(BF16)
    vals = dot(encoded, val_w_ref[...].reshape(-1, val_w_ref.shape[3])[:width]).astype(BF16)
    keys_ref[0] = keys
    vals_ref[0] = vals
    count = s_ref[1]
    scores = dot(query_ref[...], keys, ROWS_T) * SCALING
    expd = jnp.where(live_columns(count, scores.shape), jnp.exp(scores), 0.0)
    totals = jnp.sum(expd, axis=1, keepdims=True)
    probs = expd / jnp.where(count > 0, totals, 1.0)
    probs_ref[0] = probs
    ctx = head_blocks(dot(probs.astype(BF16), vals), ctx_ref.shape[0], HEAD_DIM)
    ctx_ref[...] = jnp.concatenate(ctx, axis=1).astype(BF16)


def scores_back_kernel(
    s_ref, keys_ref, vals_ref, probs_ref, ctx_ref, d_ctx_ref, low_ref, d_scores_ref, out_ref
):
    probs = probs_ref[0]
    low_ref[0] = probs.astype(BF16)
    weighted = probs * dot(by_heads(d_ctx_ref[0], HEAD_DIM), vals_ref[0], ROWS_T)
    d_scores = (weighted - probs * jnp.sum(weighted, axis=1, keepdims=True)) * SCALING
    d_scores = d_scores.astype(BF16)
    d_scores_ref[0] = d_scores
    out_ref[0] = ctx_ref[...]
    d_query = head_blocks(dot(d_scores, keys_ref[0]), out_ref.shape[1], HEAD_DIM)
    out_ref[1] = jnp.concatenate(d_query, axis=1).astype(BF16)


def encoded_back_kernel(
    s_ref,
    d_scores_ref,
    probs_ref,
    q0,
    q1,
    q2,
    q3,
    d_ctx_ref,
    key_w_ref,
    val_w_ref,
    enc_out_ref,
    enc_probs_ref,
    enc_queries_ref,
    cond_ref,
    d_cond_ref,
    query_ref,
    total_ref,
):
    step = pl.program_id(0)
    width = total_ref.shape[1]
    pick_query((q0, q1, q2, q3), query_ref)
    d_keys = dot(d_scores_ref[0], query_ref[...], COLS_T).astype(BF16)
    d_vals = dot(probs_ref[0], by_heads(d_ctx_ref[0], HEAD_DIM), COLS_T).astype(BF16)
    term = dot(d_keys, key_w_ref[...].reshape(-1, key_w_ref.shape[3])[:width], ROWS_T)
    term = term + dot(d_vals, val_w_ref[...].reshape(-1, val_w_ref.shape[3])[:width], ROWS_T)
    term = term.astype(BF16).astype(F32)

    @pl.when(step == 0)
    def _():
        total_ref[...] = term

    @pl.when(step > 0)
    def _():
        total_ref[...] += term

    @pl.when(step == pl.num_programs(0) - 1)
    def _():
        length = cond_ref.shape[0]
        d_att = dot(total_ref[...].astype(BF16), enc_out_ref[...], ROWS_T).astype(BF16)
        probs = enc_probs_ref[...]
        d_probs = dot(by_heads(cond_ref[:, width:], ENC_HEAD_DIM), d_att, ROWS_T)
        weighted = probs * d_probs
        sums = jnp.sum(weighted.reshape(-1, length, weighted.shape[1]), axis=1, keepdims=True)
        spread_sums = (probs.reshape(-1, length, probs.shape[1]) * sums).reshape(probs.shape)
        d_scores = (weighted - spread_sums) * ENC_SCALING
        live = live_columns(s_ref[1], probs.shape)
        d_scores = jnp.where(live, d_scores, 0.0).astype(BF16)
        low = jnp.where(live, probs, 0.0).astype(BF16)
        d_keys = head_blocks(dot(d_scores, enc_queries_ref[...]), length, ENC_HEAD_DIM)
        d_vals = head_blocks(dot(low, d_att), length, ENC_HEAD_DIM)
        d_cond_ref[...] = jnp.concatenate(d_keys + d_vals, axis=1).astype(BF16)


def placed_rows(rows, by, shift):
    moved = pltpu.roll(rows, by, 0)
    if shift == 0:
        return moved
    index = lax.broadcasted_iota(jnp.int32, rows.shape, 0)
    return jnp.where(index >= shift, moved, 0.0)


def outputs_kernel(
    shift,
    s_ref,
    c0,
    c1,
    c2,
    c3,
    out_w_ref,
    query_w_ref,
    hidden_ref,
    cotangent_ref,
    mixed_ref,
    grad_ref,
    mixed_sum_ref,
    grad_sum_ref,
):
    step = pl.program_id(0)
    half = out_w_ref.shape[2] // 2
    wide = out_w_ref.shape[3]
    length = c0.shape[1]
    parts = (c0, c1, c2, c3)
    ctx = jnp.concatenate([ref[0] for ref in parts], axis=0)
    d_query = jnp.concatenate([ref[1] for ref in parts], axis=0)

    @pl.when(step == 0)
    def _():
        mixed_sum_ref[...] = jnp.zeros_like(mixed_sum_ref)
        grad_sum_ref[...] = jnp.zeros_like(grad_sum_ref)

    for side in range(2):
        weight = out_w_ref[:, :, side * half : (side + 1) * half, :].reshape(-1, wide)
        mixed_sum_ref[:, side * wide : (side + 1) * wide] += dot(ctx, weight)
    grad_sum_ref[...] += dot(d_query, query_w_ref[...].reshape(-1, wide), ROWS_T)

    @pl.when(step == pl.num_programs(0) - 1)
    def _():
        by = (s_ref[0] * length + shift) % mixed_ref.shape[0]
        moved = placed_rows(mixed_sum_ref[...], by, shift)
        mixed_ref[...] = (hidden_ref[...].astype(F32) + moved).astype(mixed_ref.dtype)
        moved = placed_rows(grad_sum_ref[...], by, shift)
        grad_ref[...] = cotangent_ref[...].astype(F32) + moved


def cond_grad_kernel(s_ref, c0, c1, c2, c3, weight_ref, base_ref, out_ref):
    length = c0.shape[0]
    d_cond = jnp.concatenate([c0[...], c1[...], c2[...], c3[...]], axis=0)
    term = dot(d_cond, weight_ref[...], ROWS_T)
    by = s_ref[0] * length
    out_ref[...] = (base_ref[...] + placed_rows(term, by, 0)).astype(out_ref.dtype)


def shards(
    hidden,
    cotangent,
    counts,
    slot_of,
    neighbours,
    query_weight,
    key_weight,
    value_weight,
    out_weight,
    cond_weight,
    enc_query,
    enc_out,
):
    tokens, part_width = hidden.shape
    head_width = query_weight.shape[1]
    blocks = counts.shape[1]
    slots_per = slot_of.shape[2]
    item_total = blocks * slots_per
    slot_total, quarter, enc_width = neighbours.shape
    block_len = tokens // blocks
    shift = block_len - 1
    n_tensor = lax.axis_size("tensor")
    n_dp = lax.axis_size("dp")
    here = lax.axis_index("tensor")
    row = lax.axis_index("dp")
    all_width = head_width * n_tensor
    rows = slots_per * quarter * n_tensor
    enc_rows = enc_width // ENC_HEAD_DIM * block_len
    head_rows = head_width // HEAD_DIM * block_len
    sds = jax.ShapeDtypeStruct

    seq_counts = counts[0]
    count = lax.dynamic_slice_in_dim(seq_counts, here, 1, 0)
    scalars = jnp.concatenate([here.astype(jnp.int32)[None], count])

    wq_part = lax.dynamic_slice_in_dim(
        query_weight.reshape(n_tensor, part_width, head_width), row * SLICE, SLICE, 1
    )
    wo_part = lax.dynamic_slice_in_dim(out_weight, row * (SLICE // 2), SLICE // 2, 0)
    wo_part = wo_part.reshape(SLICE // 2, n_tensor, 2, head_width).transpose(1, 2, 0, 3)
    wo_part = wo_part.reshape(n_tensor, SLICE, head_width)
    kv_part = jnp.concatenate(
        [
            lax.dynamic_slice_in_dim(key_weight, row * SLICE, SLICE, 0),
            lax.dynamic_slice_in_dim(value_weight, row * SLICE, SLICE, 0),
        ],
        axis=0,
    )
    kv_part = jnp.broadcast_to(kv_part[None], (n_tensor, 2 * SLICE, head_width))
    weight_parts = exchange(jnp.concatenate([kv_part, wq_part, wo_part], axis=1), here)
    kv_parts = jnp.stack([part[: 2 * SLICE] for part in weight_parts])
    qo_parts = jnp.stack([part[2 * SLICE :] for part in weight_parts])

    def weight_spec(index):
        return pl.BlockSpec((n_dp, 1, SLICE, head_width), lambda g, s: (0, g, index, 0))

    packed = sds((tokens + 2 * block_len, part_width), BF16)
    own_cond, *to_send = call(
        pack_kernel,
        "pack",
        1,
        [whole(tokens, part_width), whole(part_width, 2 * enc_width)],
        (whole(block_len, 2 * enc_width),) + (whole(*packed.shape),) * 3,
        (sds((block_len, 2 * enc_width), BF16),) + (packed,) * 3,
        [pltpu.VMEM((tokens, 2 * enc_width), F32)],
        20,
    )(scalars, hidden, cond_weight)
    kv_all = lax.all_gather(after(kv_parts, own_cond), "dp", axis=0)
    got = tuple(
        lax.ppermute(array, "tensor", [(i, (i - k) % n_tensor) for i in range(n_tensor)])
        for k, array in enumerate(to_send, 1)
    )

    live = jnp.arange(slots_per)[None, :] < after(seq_counts, got)[:, None]
    slot_flat = slot_of.reshape(item_total)
    matches = (jnp.arange(slot_total)[:, None] == slot_flat[None, :]) & live.reshape(item_total)[
        None, :
    ]
    returned = lax.all_to_all(after(neighbours, kv_parts), "dp", split_axis=0, concat_axis=0, tiled=True)
    items = jnp.einsum(
        "si,sre->ire", matches.astype(BF16), returned, preferred_element_type=F32
    ).astype(BF16)
    items = items.reshape(blocks, slots_per * quarter, enc_width)
    x = lax.all_to_all(items, "tensor", split_axis=0, concat_axis=0, tiled=True)
    x = x.reshape(rows, enc_width)

    acc = pltpu.VMEM((tokens, head_width), F32)
    part_spec = whole(tokens, part_width)
    halves = block_len // 2
    packed_query = sds((tokens + halves, part_width), BF16)
    own_query, *to_send = call(
        functools.partial(query_kernel, shift),
        "query",
        n_tensor,
        [part_spec]
        + [whole(*packed.shape)] * 3
        + [pl.BlockSpec((part_width, head_width), lambda g, s: ((s[0] + g) % 4, 0)), part_spec],
        (whole(halves, part_width),) + (whole(*packed_query.shape),) * 3,
        (sds((halves, part_width), BF16),) + (packed_query,) * 3,
        [acc],
        20,
    )(scalars, hidden, *got, query_weight, cotangent)
    got_query = tuple(
        lax.ppermute(array, "tensor", [(i, (i - k) % n_tensor) for i in range(n_tensor)])
        for k, array in enumerate(to_send, 1)
    )
    qo_all = lax.all_gather(after(qo_parts, items), "dp", axis=0)
    d_ctx = call(
        functools.partial(d_ctx_kernel, shift),
        "d_ctx",
        n_tensor,
        [part_spec]
        + [whole(*packed_query.shape)] * 3
        + [pl.BlockSpec((head_width, part_width), lambda g, s: (0, (s[0] + g) % 4))],
        whole(tokens, head_width),
        sds((tokens, head_width), BF16),
        [acc],
        16,
    )(scalars, cotangent, *got_query, out_weight)
    d_ctx = d_ctx.reshape(blocks, block_len, head_width)
    d_ctx = lax.all_to_all(after(d_ctx, x), "tensor", split_axis=0, concat_axis=0, tiled=True)

    c_spec = whole(block_len, 2 * enc_width)
    w_spec = whole(enc_width, enc_width)
    r_spec = whole(rows, enc_width)
    p_spec = whole(enc_rows, rows)
    cond, enc_queries, enc_probs, encoded = call(
        encode_kernel,
        "encode",
        1,
        [r_spec, c_spec] + [pl.BlockSpec((2 * block_len, part_width), lambda g, s: (2, 0))] * 3
        + [w_spec] * 2,
        (c_spec, r_spec, p_spec, r_spec),
        (
            sds((block_len, 2 * enc_width), BF16),
            sds((rows, enc_width), BF16),
            sds((enc_rows, rows), F32),
            sds((rows, enc_width), BF16),
        ),
        [],
        60,
    )(scalars, x, own_cond, *got, enc_query, enc_out)

    q_specs = [whole(halves, part_width)] + [
        pl.BlockSpec((halves, part_width), lambda g, s: (tokens // halves, 0))
    ] * 3
    queries = (own_query,) + got_query
    col_spec = pl.BlockSpec((block_len, head_width), lambda g, s: (0, (s[0] + g) % 4))
    d_spec = pl.BlockSpec((1, block_len, head_width), lambda g, s: ((s[0] + g) % 4, 0, 0))
    both_spec = pl.BlockSpec((2, block_len, head_width), lambda g, s: (0, 0, (s[0] + g) % 4))
    big = pltpu.VMEM((head_rows, head_width), BF16)
    keys, vals, probs, ctx = call(
        attend_kernel,
        "attend",
        n_tensor,
        [r_spec, weight_spec(0), weight_spec(1)] + q_specs,
        (group(rows, head_width), group(rows, head_width), group(head_rows, rows), col_spec),
        (
            sds((n_tensor, rows, head_width), BF16),
            sds((n_tensor, rows, head_width), BF16),
            sds((n_tensor, head_rows, rows), F32),
            sds((block_len, all_width), BF16),
        ),
        [big],
        40,
    )(scalars, encoded, kv_all, kv_all, *queries)
    low, d_scores, both = call(
        scores_back_kernel,
        "scores_back",
        n_tensor,
        [group(rows, head_width), group(rows, head_width), group(head_rows, rows), col_spec, d_spec],
        (group(head_rows, rows), group(head_rows, rows), both_spec),
        (
            sds((n_tensor, head_rows, rows), BF16),
            sds((n_tensor, head_rows, rows), BF16),
            sds((2, block_len, all_width), BF16),
        ),
        [],
        20,
    )(scalars, keys, vals, probs, ctx, d_ctx)
    both_parts = spread(both, n_tensor)

    d_cond = call(
        encoded_back_kernel,
        "encoded_back",
        n_tensor,
        [group(head_rows, rows), group(head_rows, rows)]
        + q_specs
        + [d_spec, weight_spec(0), weight_spec(1), w_spec, p_spec, r_spec, c_spec],
        c_spec,
        sds((block_len, 2 * enc_width), BF16),
        [big, pltpu.VMEM((rows, enc_width), F32)],
        60,
    )(
        scalars,
        d_scores,
        low,
        *queries,
        d_ctx,
        kv_all,
        kv_all,
        enc_out,
        enc_probs,
        enc_queries,
        cond,
    )
    d_cond_parts = spread(d_cond, n_tensor)

    out_spec = whole(tokens, part_width)
    acc = pltpu.VMEM((tokens, part_width), F32)
    mixed, from_query = call(
        functools.partial(outputs_kernel, shift),
        "outputs",
        n_tensor,
        [both_spec] * 4 + [weight_spec(1), weight_spec(0), out_spec, out_spec],
        (out_spec, out_spec),
        (sds((tokens, part_width), BF16), sds((tokens, part_width), F32)),
        [acc, acc],
        60,
    )(scalars, *both_parts, qo_all, qo_all, hidden, cotangent)
    grad_hidden = call(
        cond_grad_kernel,
        "cond_grad",
        1,
        [c_spec] * 4 + [whole(part_width, 2 * enc_width), out_spec],
        out_spec,
        sds((tokens, part_width), BF16),
        [],
        16,
    )(scalars, *d_cond_parts, cond_weight, from_query)
    return (mixed, grad_hidden)


def solution(mesh):
    placed = (
        P("dp", "tensor"),
        P("dp", "tensor"),
        P("dp", None),
        P("dp", None, None),
        P("dp", "tensor", None),
        P(None, "tensor"),
        P(None, "tensor"),
        P(None, "tensor"),
        P("tensor", None),
        P("tensor", None),
        P(),
        P(),
    )
    return jax.shard_map(
        shards,
        mesh=mesh,
        in_specs=placed,
        out_specs=(P("dp", "tensor"), P("dp", "tensor")),
        check_vma=False,
    )
```

```python
import functools
import math

import jax
import jax.numpy as jnp
from jax import lax
from jax.experimental import pallas as pl
from jax.experimental.pallas import tpu as pltpu
from jax.sharding import PartitionSpec as P

HEAD_DIM = 128
ENC_HEAD_DIM = 128
F32 = jnp.float32
BF16 = jnp.bfloat16
PLAIN = (((1,), (0,)), ((), ()))
ROWS_T = (((1,), (1,)), ((), ()))
COLS_T = (((0,), (0,)), ((), ()))
SCALING = 1.0 / math.sqrt(HEAD_DIM)
ENC_SCALING = 1.0 / math.sqrt(ENC_HEAD_DIM)
SLICE = 32


def dot(a, b, dims=PLAIN):
    return lax.dot_general(a, b, dims, preferred_element_type=F32)


def call(kernel, name, grid, in_specs, out_specs, out_shape, scratch, vmem_mib):
    return pl.pallas_call(
        kernel,
        out_shape=out_shape,
        grid_spec=pltpu.PrefetchScalarGridSpec(
            num_scalar_prefetch=1,
            grid=(grid,),
            in_specs=in_specs,
            out_specs=out_specs,
            scratch_shapes=scratch,
        ),
        compiler_params=pltpu.CompilerParams(
            vmem_limit_bytes=vmem_mib * 1024 * 1024, dimension_semantics=("arbitrary",)
        ),
        name=name,
    )


def whole(*shape):
    return pl.BlockSpec(shape, lambda g, s: (0,) * len(shape))


def group(*shape):
    return pl.BlockSpec((1,) + shape, lambda g, s: (g,) + (0,) * len(shape))


def exchange(pieces, position, axis="tensor"):
    size = pieces.shape[0]
    out = [lax.dynamic_index_in_dim(pieces, position, 0, keepdims=False)]
    for k in range(1, size):
        piece = lax.dynamic_index_in_dim(pieces, (position - k) % size, 0, keepdims=False)
        out.append(lax.ppermute(piece, axis, [(i, (i - k) % size) for i in range(size)]))
    return out


def spread(shard, size, axis="tensor"):
    return [shard] + [
        lax.ppermute(shard, axis, [(i, (i - k) % size) for i in range(size)])
        for k in range(1, size)
    ]


def after(value, earlier):
    return lax.optimization_barrier((value, earlier))[0]


def live_columns(count, shape):
    column = lax.broadcasted_iota(jnp.int32, shape, len(shape) - 1)
    return (column // 32) % 4 < count


def by_heads(array, head_dim):
    head = lax.broadcasted_iota(jnp.int32, array.shape, 1) // head_dim
    zero = jnp.zeros_like(array)
    count = array.shape[1] // head_dim
    return jnp.concatenate([jnp.where(head == h, array, zero) for h in range(count)], axis=0)


def head_blocks(array, rows, head_dim):
    count = array.shape[1] // head_dim
    return [
        array[h * rows : (h + 1) * rows, h * head_dim : (h + 1) * head_dim] for h in range(count)
    ]


def cond_kernel(s_ref, hidden_ref, weight_ref, c0, c1, c2, c3, total_ref):
    length = c0.shape[0]
    total_ref[...] = dot(hidden_ref[...], weight_ref[...])
    for k, ref in enumerate((c0, c1, c2, c3)):
        start = pl.multiple_of(((s_ref[0] + 4 - k) % 4) * length, length)
        ref[...] = total_ref[pl.ds(start, length), :].astype(BF16)


def project_kernel(dims, shift, s_ref, p0, p1, p2, p3, weight_ref, *rest):
    out_ref, total_ref = rest[-2:]
    step = pl.program_id(0)
    for k, ref in enumerate((p0, p1, p2, p3)):

        @pl.when(step == k)
        def _(ref=ref, k=k):
            term = dot(ref[: total_ref.shape[0], :], weight_ref[...], dims)
            total_ref[...] = term if k == 0 else total_ref[...] + term

    @pl.when(step == pl.num_programs(0) - 1)
    def _():
        rows = total_ref.shape[0]
        moved = pltpu.roll(total_ref[...], rows - shift, 0)
        index = lax.broadcasted_iota(jnp.int32, moved.shape, 0)
        result = jnp.where(index < rows - shift, moved, 0.0).astype(BF16)
        if len(rest) == 2:
            out_ref[...] = result
        else:
            blocks, _, length, _ = out_ref.shape
            for block in range(blocks):
                span = slice(block * length, (block + 1) * length)
                out_ref[block, 0] = rest[0][span, :]
                out_ref[block, 1] = result[span, :]


def encode_kernel(
    s_ref,
    x_ref,
    c0,
    c1,
    c2,
    c3,
    enc_query_ref,
    enc_out_ref,
    cond_ref,
    queries_ref,
    probs_ref,
    encoded_ref,
):
    width = x_ref.shape[1]
    x = x_ref[...]
    cond = (c0[...].astype(F32) + c1[...].astype(F32)) + (
        c2[...].astype(F32) + c3[...].astype(F32)
    )
    cond = cond.astype(BF16)
    cond_ref[...] = cond
    length = cond.shape[0]
    queries = dot(x, enc_query_ref[...]).astype(BF16)
    queries_ref[...] = queries
    attended = []
    for head in range(width // ENC_HEAD_DIM):
        cols = slice(head * ENC_HEAD_DIM, (head + 1) * ENC_HEAD_DIM)
        vals = slice(width + head * ENC_HEAD_DIM, width + (head + 1) * ENC_HEAD_DIM)
        exponents = jnp.exp(dot(cond[:, cols], queries[:, cols], ROWS_T) * ENC_SCALING)
        probs = exponents / jnp.sum(exponents, axis=0, keepdims=True)
        probs_ref[head * length : (head + 1) * length, :] = probs
        attended.append(dot(probs.astype(BF16), cond[:, vals], COLS_T).astype(BF16))
    attended = jnp.concatenate(attended, axis=1)
    mixing = dot(attended, enc_out_ref[...])
    encoded_ref[...] = (x.astype(F32) + mixing).astype(BF16)


def attention_kernel(
    s_ref,
    encoded_ref,
    key_w_ref,
    val_w_ref,
    query_ref,
    probs_ref,
    d_scores_ref,
    out_ref,
):
    width = encoded_ref.shape[1]
    length = out_ref.shape[1]
    encoded = encoded_ref[...]
    keys = dot(encoded, key_w_ref[...].reshape(-1, key_w_ref.shape[3])[:width]).astype(BF16)
    vals = dot(encoded, val_w_ref[...].reshape(-1, val_w_ref.shape[3])[:width]).astype(BF16)
    count = s_ref[1]
    scores = dot(by_heads(query_ref[0, 0], HEAD_DIM), keys, ROWS_T) * SCALING
    expd = jnp.where(live_columns(count, scores.shape), jnp.exp(scores), 0.0)
    totals = jnp.sum(expd, axis=1, keepdims=True)
    probs = expd / jnp.where(count > 0, totals, 1.0)
    probs_low = probs.astype(BF16)
    probs_ref[0] = probs_low
    ctx = head_blocks(dot(probs_low, vals), length, HEAD_DIM)
    out_ref[0] = jnp.concatenate(ctx, axis=1).astype(BF16)
    weighted = probs * dot(by_heads(query_ref[0, 1], HEAD_DIM), vals, ROWS_T)
    d_scores = (weighted - probs * jnp.sum(weighted, axis=1, keepdims=True)) * SCALING
    d_scores = d_scores.astype(BF16)
    d_scores_ref[0] = d_scores
    d_query = head_blocks(dot(d_scores, keys), length, HEAD_DIM)
    out_ref[1] = jnp.concatenate(d_query, axis=1).astype(BF16)


def encoded_back_kernel(
    s_ref,
    d_scores_ref,
    probs_ref,
    query_ref,
    key_w_ref,
    val_w_ref,
    enc_out_ref,
    enc_probs_ref,
    enc_queries_ref,
    cond_ref,
    d_cond_ref,
    total_ref,
):
    step = pl.program_id(0)
    width = total_ref.shape[1]
    d_keys = dot(d_scores_ref[0], by_heads(query_ref[0, 0], HEAD_DIM), COLS_T).astype(BF16)
    d_vals = dot(probs_ref[0], by_heads(query_ref[0, 1], HEAD_DIM), COLS_T).astype(BF16)
    term = dot(d_keys, key_w_ref[...].reshape(-1, key_w_ref.shape[3])[:width], ROWS_T)
    term = term + dot(d_vals, val_w_ref[...].reshape(-1, val_w_ref.shape[3])[:width], ROWS_T)
    term = term.astype(BF16).astype(F32)

    @pl.when(step == 0)
    def _():
        total_ref[...] = term

    @pl.when(step > 0)
    def _():
        total_ref[...] += term

    @pl.when(step == pl.num_programs(0) - 1)
    def _():
        length = cond_ref.shape[0]
        d_att = dot(total_ref[...].astype(BF16), enc_out_ref[...], ROWS_T).astype(BF16)
        probs = enc_probs_ref[...]
        d_probs = dot(by_heads(cond_ref[:, width:], ENC_HEAD_DIM), d_att, ROWS_T)
        weighted = probs * d_probs
        sums = jnp.sum(weighted.reshape(-1, length, weighted.shape[1]), axis=1, keepdims=True)
        spread_sums = (probs.reshape(-1, length, probs.shape[1]) * sums).reshape(probs.shape)
        d_scores = (weighted - spread_sums) * ENC_SCALING
        live = live_columns(s_ref[1], probs.shape)
        d_scores = jnp.where(live, d_scores, 0.0).astype(BF16)
        low = jnp.where(live, probs, 0.0).astype(BF16)
        d_keys = head_blocks(dot(d_scores, enc_queries_ref[...]), length, ENC_HEAD_DIM)
        d_vals = head_blocks(dot(low, d_att), length, ENC_HEAD_DIM)
        d_cond_ref[...] = jnp.concatenate(d_keys + d_vals, axis=1).astype(BF16)


def placed_rows(rows, by, shift):
    moved = pltpu.roll(rows, by, 0)
    if shift == 0:
        return moved
    index = lax.broadcasted_iota(jnp.int32, rows.shape, 0)
    return jnp.where(index >= shift, moved, 0.0)


def outputs_kernel(
    shift,
    s_ref,
    c0,
    c1,
    c2,
    c3,
    out_w_ref,
    query_w_ref,
    hidden_ref,
    cotangent_ref,
    mixed_ref,
    grad_ref,
    mixed_sum_ref,
    grad_sum_ref,
):
    step = pl.program_id(0)
    half = out_w_ref.shape[2] // 2
    wide = out_w_ref.shape[3]
    length = c0.shape[1]
    parts = (c0, c1, c2, c3)
    ctx = jnp.concatenate([ref[0] for ref in parts], axis=0)
    d_query = jnp.concatenate([ref[1] for ref in parts], axis=0)

    @pl.when(step == 0)
    def _():
        mixed_sum_ref[...] = jnp.zeros_like(mixed_sum_ref)
        grad_sum_ref[...] = jnp.zeros_like(grad_sum_ref)

    for side in range(2):
        weight = out_w_ref[:, :, side * half : (side + 1) * half, :].reshape(-1, wide)
        mixed_sum_ref[:, side * wide : (side + 1) * wide] += dot(ctx, weight)
    grad_sum_ref[...] += dot(d_query, query_w_ref[...].reshape(-1, wide), ROWS_T)

    @pl.when(step == pl.num_programs(0) - 1)
    def _():
        by = (s_ref[0] * length + shift) % mixed_ref.shape[0]
        moved = placed_rows(mixed_sum_ref[...], by, shift)
        mixed_ref[...] = (hidden_ref[...].astype(F32) + moved).astype(mixed_ref.dtype)
        moved = placed_rows(grad_sum_ref[...], by, shift)
        grad_ref[...] = cotangent_ref[...].astype(F32) + moved


def cond_grad_kernel(s_ref, c0, c1, c2, c3, weight_ref, base_ref, out_ref):
    length = c0.shape[0]
    d_cond = jnp.concatenate([c0[...], c1[...], c2[...], c3[...]], axis=0)
    term = dot(d_cond, weight_ref[...], ROWS_T)
    by = s_ref[0] * length
    out_ref[...] = (base_ref[...] + placed_rows(term, by, 0)).astype(out_ref.dtype)


def shards(
    hidden,
    cotangent,
    counts,
    slot_of,
    neighbours,
    query_weight,
    key_weight,
    value_weight,
    out_weight,
    cond_weight,
    enc_query,
    enc_out,
):
    tokens, part_width = hidden.shape
    head_width = query_weight.shape[1]
    blocks = counts.shape[1]
    slots_per = slot_of.shape[2]
    item_total = blocks * slots_per
    slot_total, quarter, enc_width = neighbours.shape
    block_len = tokens // blocks
    shift = block_len - 1
    n_tensor = lax.axis_size("tensor")
    n_dp = lax.axis_size("dp")
    here = lax.axis_index("tensor")
    row = lax.axis_index("dp")
    all_width = head_width * n_tensor
    rows = slots_per * quarter * n_tensor
    enc_rows = enc_width // ENC_HEAD_DIM * block_len
    head_rows = head_width // HEAD_DIM * block_len
    sds = jax.ShapeDtypeStruct

    seq_counts = counts[0]
    count = lax.dynamic_slice_in_dim(seq_counts, here, 1, 0)
    scalars = jnp.concatenate([here.astype(jnp.int32)[None], count])

    wq_part = lax.dynamic_slice_in_dim(
        query_weight.reshape(n_tensor, part_width, head_width), row * SLICE, SLICE, 1
    )
    wo_part = lax.dynamic_slice_in_dim(out_weight, row * (SLICE // 2), SLICE // 2, 0)
    wo_part = wo_part.reshape(SLICE // 2, n_tensor, 2, head_width).transpose(1, 2, 0, 3)
    wo_part = wo_part.reshape(n_tensor, SLICE, head_width)
    kv_part = jnp.concatenate(
        [
            lax.dynamic_slice_in_dim(key_weight, row * SLICE, SLICE, 0),
            lax.dynamic_slice_in_dim(value_weight, row * SLICE, SLICE, 0),
        ],
        axis=0,
    )
    kv_part = jnp.broadcast_to(kv_part[None], (n_tensor, 2 * SLICE, head_width))
    weight_parts = exchange(jnp.concatenate([kv_part, wq_part, wo_part], axis=1), here)
    kv_parts = jnp.stack([part[: 2 * SLICE] for part in weight_parts])
    qo_parts = jnp.stack([part[2 * SLICE :] for part in weight_parts])
    hidden_parts = spread(hidden, n_tensor)
    cot_parts = spread(cotangent, n_tensor)
    near = (hidden_parts[1], hidden_parts[3])
    kv_all = lax.all_gather(after(kv_parts, near), "dp", axis=0)

    def weight_spec(index):
        return pl.BlockSpec((n_dp, 1, SLICE, head_width), lambda g, s: (0, g, index, 0))

    c_spec = whole(block_len, 2 * enc_width)
    own_cond, *to_send = call(
        cond_kernel,
        "cond",
        1,
        [whole(tokens, part_width), whole(part_width, 2 * enc_width)],
        (c_spec,) * 4,
        (sds((block_len, 2 * enc_width), BF16),) * 4,
        [pltpu.VMEM((tokens, 2 * enc_width), F32)],
        20,
    )(scalars, hidden, cond_weight)
    cond_parts = [own_cond] + [
        lax.ppermute(array, "tensor", [(i, (i - k) % n_tensor) for i in range(n_tensor)])
        for k, array in enumerate(to_send, 1)
    ]

    live = jnp.arange(slots_per)[None, :] < after(seq_counts, (hidden_parts[1:], cot_parts[1:]))[:, None]
    slot_flat = slot_of.reshape(item_total)
    matches = (jnp.arange(slot_total)[:, None] == slot_flat[None, :]) & live.reshape(item_total)[
        None, :
    ]
    returned = lax.all_to_all(neighbours, "dp", split_axis=0, concat_axis=0, tiled=True)
    items = jnp.einsum(
        "si,sre->ire", matches.astype(BF16), returned, preferred_element_type=F32
    ).astype(BF16)
    items = items.reshape(blocks, slots_per * quarter, enc_width)
    x = lax.all_to_all(items, "tensor", split_axis=0, concat_axis=0, tiled=True)
    x = x.reshape(rows, enc_width)

    def projected(parts, weight, dims, weight_block, weight_map, name, before=None):
        out = (tokens, head_width)
        if before is not None:
            out = (blocks, 2, block_len, head_width)
        return call(
            functools.partial(project_kernel, dims, shift),
            name,
            n_tensor,
            [whole(*part.shape) for part in parts]
            + [pl.BlockSpec(weight_block, weight_map)]
            + ([] if before is None else [whole(tokens, head_width)]),
            whole(*out),
            sds(out, BF16),
            [pltpu.VMEM((tokens, head_width), F32)],
            16,
        )(scalars, *parts, weight, *([] if before is None else [before]))

    query = projected(
        hidden_parts,
        query_weight,
        PLAIN,
        (part_width, head_width),
        lambda g, s: ((s[0] + g) % 4, 0),
        "query",
    )
    qo_all = lax.all_gather(after(qo_parts, items), "dp", axis=0)
    query_d_ctx = projected(
        cot_parts,
        out_weight,
        ROWS_T,
        (head_width, part_width),
        lambda g, s: (0, (s[0] + g) % 4),
        "d_ctx",
        before=query,
    )
    query_d_ctx = lax.all_to_all(
        after(query_d_ctx, (x, cond_parts[1:])), "tensor", split_axis=0, concat_axis=0, tiled=True
    )

    c_spec = whole(block_len, 2 * enc_width)
    w_spec = whole(enc_width, enc_width)
    r_spec = whole(rows, enc_width)
    p_spec = whole(enc_rows, rows)
    cond, enc_queries, enc_probs, encoded = call(
        encode_kernel,
        "encode",
        1,
        [r_spec] + [c_spec] * 4 + [w_spec] * 2,
        (c_spec, r_spec, p_spec, r_spec),
        (
            sds((block_len, 2 * enc_width), BF16),
            sds((rows, enc_width), BF16),
            sds((enc_rows, rows), F32),
            sds((rows, enc_width), BF16),
        ),
        [],
        60,
    )(scalars, x, *cond_parts, enc_query, enc_out)

    q_spec = pl.BlockSpec((1, 2, block_len, head_width), lambda g, s: ((s[0] + g) % 4, 0, 0, 0))
    both_spec = pl.BlockSpec((2, block_len, head_width), lambda g, s: (0, 0, (s[0] + g) % 4))
    probs, d_scores, both = call(
        attention_kernel,
        "attention",
        n_tensor,
        [r_spec, weight_spec(0), weight_spec(1), q_spec],
        (
            group(head_rows, rows),
            group(head_rows, rows),
            both_spec,
        ),
        (
            sds((n_tensor, head_rows, rows), BF16),
            sds((n_tensor, head_rows, rows), BF16),
            sds((2, block_len, all_width), BF16),
        ),
        [],
        60,
    )(scalars, encoded, kv_all, kv_all, query_d_ctx)
    both_parts = spread(both, n_tensor)

    d_cond = call(
        encoded_back_kernel,
        "encoded_back",
        n_tensor,
        [group(head_rows, rows), group(head_rows, rows)]
        + [q_spec, weight_spec(0), weight_spec(1), w_spec, p_spec, r_spec, c_spec],
        c_spec,
        sds((block_len, 2 * enc_width), BF16),
        [pltpu.VMEM((rows, enc_width), F32)],
        60,
    )(
        scalars,
        d_scores,
        probs,
        query_d_ctx,
        kv_all,
        kv_all,
        enc_out,
        enc_probs,
        enc_queries,
        cond,
    )
    d_cond_parts = spread(d_cond, n_tensor)

    out_spec = whole(tokens, part_width)
    acc = pltpu.VMEM((tokens, part_width), F32)
    mixed, from_query = call(
        functools.partial(outputs_kernel, shift),
        "outputs",
        n_tensor,
        [both_spec] * 4 + [weight_spec(1), weight_spec(0), out_spec, out_spec],
        (out_spec, out_spec),
        (sds((tokens, part_width), BF16), sds((tokens, part_width), F32)),
        [acc, acc],
        60,
    )(scalars, *both_parts, qo_all, qo_all, hidden, cotangent)
    grad_hidden = call(
        cond_grad_kernel,
        "cond_grad",
        1,
        [c_spec] * 4 + [whole(part_width, 2 * enc_width), out_spec],
        out_spec,
        sds((tokens, part_width), BF16),
        [],
        16,
    )(scalars, *d_cond_parts, cond_weight, from_query)
    return (mixed, grad_hidden)


def solution(mesh):
    placed = (
        P("dp", "tensor"),
        P("dp", "tensor"),
        P("dp", None),
        P("dp", None, None),
        P("dp", "tensor", None),
        P(None, "tensor"),
        P(None, "tensor"),
        P(None, "tensor"),
        P("tensor", None),
        P("tensor", None),
        P(),
        P(),
    )
    return jax.shard_map(
        shards,
        mesh=mesh,
        in_specs=placed,
        out_specs=(P("dp", "tensor"), P("dp", "tensor")),
        check_vma=False,
    )
```

```python
import functools
import math

import jax
import jax.numpy as jnp
from jax import lax
from jax.experimental import pallas as pl
from jax.experimental.pallas import tpu as pltpu
from jax.sharding import PartitionSpec as P

HEAD_DIM = 128
ENC_HEAD_DIM = 128
F32 = jnp.float32
BF16 = jnp.bfloat16
PLAIN = (((1,), (0,)), ((), ()))
ROWS_T = (((1,), (1,)), ((), ()))
COLS_T = (((0,), (0,)), ((), ()))
SCALING = 1.0 / math.sqrt(HEAD_DIM)
ENC_SCALING = 1.0 / math.sqrt(ENC_HEAD_DIM)
SLICE = 32


def dot(a, b, dims=PLAIN):
    return lax.dot_general(a, b, dims, preferred_element_type=F32)


def call(kernel, name, grid, in_specs, out_specs, out_shape, scratch, vmem_mib):
    return pl.pallas_call(
        kernel,
        out_shape=out_shape,
        grid_spec=pltpu.PrefetchScalarGridSpec(
            num_scalar_prefetch=1,
            grid=(grid,),
            in_specs=in_specs,
            out_specs=out_specs,
            scratch_shapes=scratch,
        ),
        compiler_params=pltpu.CompilerParams(
            vmem_limit_bytes=vmem_mib * 1024 * 1024, dimension_semantics=("arbitrary",)
        ),
        name=name,
    )


def whole(*shape):
    return pl.BlockSpec(shape, lambda g, s: (0,) * len(shape))


def group(*shape):
    return pl.BlockSpec((1,) + shape, lambda g, s: (g,) + (0,) * len(shape))


def exchange(pieces, position, axis="tensor"):
    size = pieces.shape[0]
    out = [lax.dynamic_index_in_dim(pieces, position, 0, keepdims=False)]
    for k in range(1, size):
        piece = lax.dynamic_index_in_dim(pieces, (position - k) % size, 0, keepdims=False)
        out.append(lax.ppermute(piece, axis, [(i, (i - k) % size) for i in range(size)]))
    return out


def spread(shard, size, axis="tensor"):
    return [shard] + [
        lax.ppermute(shard, axis, [(i, (i - k) % size) for i in range(size)])
        for k in range(1, size)
    ]


def after(value, earlier):
    return lax.optimization_barrier((value, earlier))[0]


def live_columns(count, shape):
    column = lax.broadcasted_iota(jnp.int32, shape, len(shape) - 1)
    return (column // 32) % 4 < count


def by_heads(array, head_dim):
    head = lax.broadcasted_iota(jnp.int32, array.shape, 1) // head_dim
    zero = jnp.zeros_like(array)
    count = array.shape[1] // head_dim
    return jnp.concatenate([jnp.where(head == h, array, zero) for h in range(count)], axis=0)


def head_blocks(array, rows, head_dim):
    count = array.shape[1] // head_dim
    return [
        array[h * rows : (h + 1) * rows, h * head_dim : (h + 1) * head_dim] for h in range(count)
    ]


def cond_kernel(s_ref, hidden_ref, weight_ref, c0, c1, c2, c3, total_ref):
    length = c0.shape[0]
    total_ref[...] = dot(hidden_ref[...], weight_ref[...])
    for k, ref in enumerate((c0, c1, c2, c3)):
        start = pl.multiple_of(((s_ref[0] + 4 - k) % 4) * length, length)
        ref[...] = total_ref[pl.ds(start, length), :].astype(BF16)


def project_kernel(dims, shift, s_ref, p0, p1, p2, p3, weight_ref, *rest):
    out_ref, total_ref = rest[-2:]
    step = pl.program_id(0)
    for k, ref in enumerate((p0, p1, p2, p3)):

        @pl.when(step == k)
        def _(ref=ref, k=k):
            term = dot(ref[: total_ref.shape[0], :], weight_ref[...], dims)
            total_ref[...] = term if k == 0 else total_ref[...] + term

    @pl.when(step == pl.num_programs(0) - 1)
    def _():
        rows = total_ref.shape[0]
        moved = pltpu.roll(total_ref[...], rows - shift, 0)
        index = lax.broadcasted_iota(jnp.int32, moved.shape, 0)
        result = jnp.where(index < rows - shift, moved, 0.0).astype(BF16)
        if len(rest) == 2:
            out_ref[...] = result
        else:
            blocks, _, length, _ = out_ref.shape
            for block in range(blocks):
                span = slice(block * length, (block + 1) * length)
                out_ref[block, 0] = rest[0][span, :]
                out_ref[block, 1] = result[span, :]


def encode_kernel(
    s_ref,
    x_ref,
    c0,
    c1,
    c2,
    c3,
    enc_query_ref,
    enc_out_ref,
    cond_ref,
    queries_ref,
    probs_ref,
    encoded_ref,
):
    width = x_ref.shape[1]
    x = x_ref[...]
    cond = (c0[...].astype(F32) + c1[...].astype(F32)) + (
        c2[...].astype(F32) + c3[...].astype(F32)
    )
    cond = cond.astype(BF16)
    cond_ref[...] = cond
    length = cond.shape[0]
    queries = dot(x, enc_query_ref[...]).astype(BF16)
    queries_ref[...] = queries
    attended = []
    for head in range(width // ENC_HEAD_DIM):
        cols = slice(head * ENC_HEAD_DIM, (head + 1) * ENC_HEAD_DIM)
        vals = slice(width + head * ENC_HEAD_DIM, width + (head + 1) * ENC_HEAD_DIM)
        exponents = jnp.exp(dot(cond[:, cols], queries[:, cols], ROWS_T) * ENC_SCALING)
        probs = exponents / jnp.sum(exponents, axis=0, keepdims=True)
        probs_ref[head * length : (head + 1) * length, :] = probs
        attended.append(dot(probs.astype(BF16), cond[:, vals], COLS_T).astype(BF16))
    attended = jnp.concatenate(attended, axis=1)
    mixing = dot(attended, enc_out_ref[...])
    encoded_ref[...] = (x.astype(F32) + mixing).astype(BF16)


def pick(refs, query_ref, d_ctx_ref):
    for k, ref in enumerate(refs):

        @pl.when(pl.program_id(0) == k)
        def _(ref=ref):
            query_ref[...] = by_heads(ref[0], HEAD_DIM)
            d_ctx_ref[...] = by_heads(ref[1], HEAD_DIM)


def attention_kernel(
    s_ref,
    encoded_ref,
    key_w_ref,
    val_w_ref,
    q0,
    q1,
    q2,
    q3,
    probs_ref,
    d_scores_ref,
    out_ref,
    query_ref,
    d_ctx_ref,
):
    width = encoded_ref.shape[1]
    length = out_ref.shape[1]
    pick((q0, q1, q2, q3), query_ref, d_ctx_ref)
    encoded = encoded_ref[...]
    keys = dot(encoded, key_w_ref[...].reshape(-1, key_w_ref.shape[3])[:width]).astype(BF16)
    vals = dot(encoded, val_w_ref[...].reshape(-1, val_w_ref.shape[3])[:width]).astype(BF16)
    count = s_ref[1]
    scores = dot(query_ref[...], keys, ROWS_T) * SCALING
    expd = jnp.where(live_columns(count, scores.shape), jnp.exp(scores), 0.0)
    totals = jnp.sum(expd, axis=1, keepdims=True)
    probs = expd / jnp.where(count > 0, totals, 1.0)
    probs_low = probs.astype(BF16)
    probs_ref[0] = probs_low
    ctx = head_blocks(dot(probs_low, vals), length, HEAD_DIM)
    out_ref[0] = jnp.concatenate(ctx, axis=1).astype(BF16)
    weighted = probs * dot(d_ctx_ref[...], vals, ROWS_T)
    d_scores = (weighted - probs * jnp.sum(weighted, axis=1, keepdims=True)) * SCALING
    d_scores = d_scores.astype(BF16)
    d_scores_ref[0] = d_scores
    d_query = head_blocks(dot(d_scores, keys), length, HEAD_DIM)
    out_ref[1] = jnp.concatenate(d_query, axis=1).astype(BF16)


def encoded_back_kernel(
    s_ref,
    d_scores_ref,
    probs_ref,
    q0,
    q1,
    q2,
    q3,
    key_w_ref,
    val_w_ref,
    enc_out_ref,
    enc_probs_ref,
    enc_queries_ref,
    cond_ref,
    d_cond_ref,
    query_ref,
    d_ctx_ref,
    total_ref,
):
    step = pl.program_id(0)
    width = total_ref.shape[1]
    pick((q0, q1, q2, q3), query_ref, d_ctx_ref)
    d_keys = dot(d_scores_ref[0], query_ref[...], COLS_T).astype(BF16)
    d_vals = dot(probs_ref[0], d_ctx_ref[...], COLS_T).astype(BF16)
    term = dot(d_keys, key_w_ref[...].reshape(-1, key_w_ref.shape[3])[:width], ROWS_T)
    term = term + dot(d_vals, val_w_ref[...].reshape(-1, val_w_ref.shape[3])[:width], ROWS_T)
    term = term.astype(BF16).astype(F32)

    @pl.when(step == 0)
    def _():
        total_ref[...] = term

    @pl.when(step > 0)
    def _():
        total_ref[...] += term

    @pl.when(step == pl.num_programs(0) - 1)
    def _():
        length = cond_ref.shape[0]
        d_att = dot(total_ref[...].astype(BF16), enc_out_ref[...], ROWS_T).astype(BF16)
        probs = enc_probs_ref[...]
        d_probs = dot(by_heads(cond_ref[:, width:], ENC_HEAD_DIM), d_att, ROWS_T)
        weighted = probs * d_probs
        sums = jnp.sum(weighted.reshape(-1, length, weighted.shape[1]), axis=1, keepdims=True)
        spread_sums = (probs.reshape(-1, length, probs.shape[1]) * sums).reshape(probs.shape)
        d_scores = (weighted - spread_sums) * ENC_SCALING
        live = live_columns(s_ref[1], probs.shape)
        d_scores = jnp.where(live, d_scores, 0.0).astype(BF16)
        low = jnp.where(live, probs, 0.0).astype(BF16)
        d_keys = head_blocks(dot(d_scores, enc_queries_ref[...]), length, ENC_HEAD_DIM)
        d_vals = head_blocks(dot(low, d_att), length, ENC_HEAD_DIM)
        d_cond_ref[...] = jnp.concatenate(d_keys + d_vals, axis=1).astype(BF16)


def placed_rows(rows, by, shift):
    moved = pltpu.roll(rows, by, 0)
    if shift == 0:
        return moved
    index = lax.broadcasted_iota(jnp.int32, rows.shape, 0)
    return jnp.where(index >= shift, moved, 0.0)


def outputs_kernel(
    shift,
    s_ref,
    c0,
    c1,
    c2,
    c3,
    out_w_ref,
    query_w_ref,
    hidden_ref,
    cotangent_ref,
    mixed_ref,
    grad_ref,
    mixed_sum_ref,
    grad_sum_ref,
):
    step = pl.program_id(0)
    half = out_w_ref.shape[2] // 2
    wide = out_w_ref.shape[3]
    length = c0.shape[1]
    parts = (c0, c1, c2, c3)
    ctx = jnp.concatenate([ref[0] for ref in parts], axis=0)
    d_query = jnp.concatenate([ref[1] for ref in parts], axis=0)

    @pl.when(step == 0)
    def _():
        mixed_sum_ref[...] = jnp.zeros_like(mixed_sum_ref)
        grad_sum_ref[...] = jnp.zeros_like(grad_sum_ref)

    for side in range(2):
        weight = out_w_ref[:, :, side * half : (side + 1) * half, :].reshape(-1, wide)
        mixed_sum_ref[:, side * wide : (side + 1) * wide] += dot(ctx, weight)
    grad_sum_ref[...] += dot(d_query, query_w_ref[...].reshape(-1, wide), ROWS_T)

    @pl.when(step == pl.num_programs(0) - 1)
    def _():
        by = (s_ref[0] * length + shift) % mixed_ref.shape[0]
        moved = placed_rows(mixed_sum_ref[...], by, shift)
        mixed_ref[...] = (hidden_ref[...].astype(F32) + moved).astype(mixed_ref.dtype)
        moved = placed_rows(grad_sum_ref[...], by, shift)
        grad_ref[...] = cotangent_ref[...].astype(F32) + moved


def cond_grad_kernel(s_ref, c0, c1, c2, c3, weight_ref, base_ref, out_ref):
    length = c0.shape[0]
    d_cond = jnp.concatenate([c0[...], c1[...], c2[...], c3[...]], axis=0)
    term = dot(d_cond, weight_ref[...], ROWS_T)
    by = s_ref[0] * length
    out_ref[...] = (base_ref[...] + placed_rows(term, by, 0)).astype(out_ref.dtype)


def shards(
    hidden,
    cotangent,
    counts,
    slot_of,
    neighbours,
    query_weight,
    key_weight,
    value_weight,
    out_weight,
    cond_weight,
    enc_query,
    enc_out,
):
    tokens, part_width = hidden.shape
    head_width = query_weight.shape[1]
    blocks = counts.shape[1]
    slots_per = slot_of.shape[2]
    item_total = blocks * slots_per
    slot_total, quarter, enc_width = neighbours.shape
    block_len = tokens // blocks
    shift = block_len - 1
    n_tensor = lax.axis_size("tensor")
    n_dp = lax.axis_size("dp")
    here = lax.axis_index("tensor")
    row = lax.axis_index("dp")
    all_width = head_width * n_tensor
    rows = slots_per * quarter * n_tensor
    enc_rows = enc_width // ENC_HEAD_DIM * block_len
    head_rows = head_width // HEAD_DIM * block_len
    sds = jax.ShapeDtypeStruct

    seq_counts = counts[0]
    count = lax.dynamic_slice_in_dim(seq_counts, here, 1, 0)
    scalars = jnp.concatenate([here.astype(jnp.int32)[None], count])

    wq_part = lax.dynamic_slice_in_dim(
        query_weight.reshape(n_tensor, part_width, head_width), row * SLICE, SLICE, 1
    )
    wo_part = lax.dynamic_slice_in_dim(out_weight, row * (SLICE // 2), SLICE // 2, 0)
    wo_part = wo_part.reshape(SLICE // 2, n_tensor, 2, head_width).transpose(1, 2, 0, 3)
    wo_part = wo_part.reshape(n_tensor, SLICE, head_width)
    kv_part = jnp.concatenate(
        [
            lax.dynamic_slice_in_dim(key_weight, row * SLICE, SLICE, 0),
            lax.dynamic_slice_in_dim(value_weight, row * SLICE, SLICE, 0),
        ],
        axis=0,
    )
    kv_part = jnp.broadcast_to(kv_part[None], (n_tensor, 2 * SLICE, head_width))
    weight_parts = exchange(jnp.concatenate([kv_part, wq_part, wo_part], axis=1), here)
    kv_parts = jnp.stack([part[: 2 * SLICE] for part in weight_parts])
    qo_parts = jnp.stack([part[2 * SLICE :] for part in weight_parts])
    hidden_parts = spread(hidden, n_tensor)
    cot_parts = spread(cotangent, n_tensor)
    near = (hidden_parts[1], hidden_parts[3])
    kv_all = lax.all_gather(after(kv_parts, near), "dp", axis=0)

    def weight_spec(index):
        return pl.BlockSpec((n_dp, 1, SLICE, head_width), lambda g, s: (0, g, index, 0))

    c_spec = whole(block_len, 2 * enc_width)
    own_cond, *to_send = call(
        cond_kernel,
        "cond",
        1,
        [whole(tokens, part_width), whole(part_width, 2 * enc_width)],
        (c_spec,) * 4,
        (sds((block_len, 2 * enc_width), BF16),) * 4,
        [pltpu.VMEM((tokens, 2 * enc_width), F32)],
        20,
    )(scalars, hidden, cond_weight)
    cond_parts = [own_cond] + [
        lax.ppermute(array, "tensor", [(i, (i - k) % n_tensor) for i in range(n_tensor)])
        for k, array in enumerate(to_send, 1)
    ]

    def projected(parts, weight, dims, weight_block, weight_map, name, before=None):
        out = (tokens, head_width)
        if before is not None:
            out = (blocks, 2, block_len, head_width)
        return call(
            functools.partial(project_kernel, dims, shift),
            name,
            n_tensor,
            [whole(*part.shape) for part in parts]
            + [pl.BlockSpec(weight_block, weight_map)]
            + ([] if before is None else [whole(tokens, head_width)]),
            whole(*out),
            sds(out, BF16),
            [pltpu.VMEM((tokens, head_width), F32)],
            16,
        )(scalars, *parts, weight, *([] if before is None else [before]))

    query = projected(
        hidden_parts,
        query_weight,
        PLAIN,
        (part_width, head_width),
        lambda g, s: ((s[0] + g) % 4, 0),
        "query",
    )

    live = jnp.arange(slots_per)[None, :] < after(seq_counts, (query, own_cond, cot_parts[1], cot_parts[3]))[:, None]
    slot_flat = slot_of.reshape(item_total)
    matches = (jnp.arange(slot_total)[:, None] == slot_flat[None, :]) & live.reshape(item_total)[
        None, :
    ]
    returned = lax.all_to_all(neighbours, "dp", split_axis=0, concat_axis=0, tiled=True)
    items = jnp.einsum(
        "si,sre->ire", matches.astype(BF16), returned, preferred_element_type=F32
    ).astype(BF16)
    items = items.reshape(blocks, slots_per * quarter, enc_width)
    x = lax.all_to_all(items, "tensor", split_axis=0, concat_axis=0, tiled=True)
    x = x.reshape(rows, enc_width)

    qo_all = lax.all_gather(after(qo_parts, items), "dp", axis=0)
    query_d_ctx = projected(
        after(tuple(cot_parts), (items, cond_parts[1:])),
        out_weight,
        ROWS_T,
        (head_width, part_width),
        lambda g, s: (0, (s[0] + g) % 4),
        "d_ctx",
        before=query,
    )
    query_parts = exchange(query_d_ctx, here)

    c_spec = whole(block_len, 2 * enc_width)
    w_spec = whole(enc_width, enc_width)
    r_spec = whole(rows, enc_width)
    p_spec = whole(enc_rows, rows)
    cond, enc_queries, enc_probs, encoded = call(
        encode_kernel,
        "encode",
        1,
        [r_spec] + [c_spec] * 4 + [w_spec] * 2,
        (c_spec, r_spec, p_spec, r_spec),
        (
            sds((block_len, 2 * enc_width), BF16),
            sds((rows, enc_width), BF16),
            sds((enc_rows, rows), F32),
            sds((rows, enc_width), BF16),
        ),
        [],
        60,
    )(scalars, x, *cond_parts, enc_query, enc_out)

    q_spec = whole(2, block_len, head_width)
    big = pltpu.VMEM((head_rows, head_width), BF16)
    both_spec = pl.BlockSpec((2, block_len, head_width), lambda g, s: (0, 0, (s[0] + g) % 4))
    probs, d_scores, both = call(
        attention_kernel,
        "attention",
        n_tensor,
        [r_spec, weight_spec(0), weight_spec(1)] + [q_spec] * 4,
        (
            group(head_rows, rows),
            group(head_rows, rows),
            both_spec,
        ),
        (
            sds((n_tensor, head_rows, rows), BF16),
            sds((n_tensor, head_rows, rows), BF16),
            sds((2, block_len, all_width), BF16),
        ),
        [big, big],
        60,
    )(scalars, encoded, kv_all, kv_all, *query_parts)
    both_parts = spread(both, n_tensor)

    d_cond = call(
        encoded_back_kernel,
        "encoded_back",
        n_tensor,
        [group(head_rows, rows), group(head_rows, rows)]
        + [q_spec] * 4
        + [weight_spec(0), weight_spec(1), w_spec, p_spec, r_spec, c_spec],
        c_spec,
        sds((block_len, 2 * enc_width), BF16),
        [big, big, pltpu.VMEM((rows, enc_width), F32)],
        60,
    )(
        scalars,
        d_scores,
        probs,
        *query_parts,
        kv_all,
        kv_all,
        enc_out,
        enc_probs,
        enc_queries,
        cond,
    )
    d_cond_parts = spread(d_cond, n_tensor)

    out_spec = whole(tokens, part_width)
    acc = pltpu.VMEM((tokens, part_width), F32)
    mixed, from_query = call(
        functools.partial(outputs_kernel, shift),
        "outputs",
        n_tensor,
        [both_spec] * 4 + [weight_spec(1), weight_spec(0), out_spec, out_spec],
        (out_spec, out_spec),
        (sds((tokens, part_width), BF16), sds((tokens, part_width), F32)),
        [acc, acc],
        60,
    )(scalars, *both_parts, qo_all, qo_all, hidden, cotangent)
    grad_hidden = call(
        cond_grad_kernel,
        "cond_grad",
        1,
        [c_spec] * 4 + [whole(part_width, 2 * enc_width), out_spec],
        out_spec,
        sds((tokens, part_width), BF16),
        [],
        16,
    )(scalars, *d_cond_parts, cond_weight, from_query)
    return (mixed, grad_hidden)


def solution(mesh):
    placed = (
        P("dp", "tensor"),
        P("dp", "tensor"),
        P("dp", None),
        P("dp", None, None),
        P("dp", "tensor", None),
        P(None, "tensor"),
        P(None, "tensor"),
        P(None, "tensor"),
        P("tensor", None),
        P("tensor", None),
        P(),
        P(),
    )
    return jax.shard_map(
        shards,
        mesh=mesh,
        in_specs=placed,
        out_specs=(P("dp", "tensor"), P("dp", "tensor")),
        check_vma=False,
    )
```

```python
import functools
import math

import jax
import jax.numpy as jnp
from jax import lax
from jax.experimental import pallas as pl
from jax.experimental.pallas import tpu as pltpu
from jax.sharding import PartitionSpec as P

HEAD_DIM = 128
ENC_HEAD_DIM = 128
F32 = jnp.float32
BF16 = jnp.bfloat16
PLAIN = (((1,), (0,)), ((), ()))
ROWS_T = (((1,), (1,)), ((), ()))
COLS_T = (((0,), (0,)), ((), ()))
SCALING = 1.0 / math.sqrt(HEAD_DIM)
ENC_SCALING = 1.0 / math.sqrt(ENC_HEAD_DIM)
SLICE = 32


def dot(a, b, dims=PLAIN):
    return lax.dot_general(a, b, dims, preferred_element_type=F32)


def call(kernel, name, grid, in_specs, out_specs, out_shape, scratch, vmem_mib):
    return pl.pallas_call(
        kernel,
        out_shape=out_shape,
        grid_spec=pltpu.PrefetchScalarGridSpec(
            num_scalar_prefetch=1,
            grid=(grid,),
            in_specs=in_specs,
            out_specs=out_specs,
            scratch_shapes=scratch,
        ),
        compiler_params=pltpu.CompilerParams(
            vmem_limit_bytes=vmem_mib * 1024 * 1024, dimension_semantics=("arbitrary",)
        ),
        name=name,
    )


def whole(*shape):
    return pl.BlockSpec(shape, lambda g, s: (0,) * len(shape))


def group(*shape):
    return pl.BlockSpec((1,) + shape, lambda g, s: (g,) + (0,) * len(shape))


def exchange(pieces, position, axis="tensor"):
    size = pieces.shape[0]
    out = [lax.dynamic_index_in_dim(pieces, position, 0, keepdims=False)]
    for k in range(1, size):
        piece = lax.dynamic_index_in_dim(pieces, (position - k) % size, 0, keepdims=False)
        out.append(lax.ppermute(piece, axis, [(i, (i - k) % size) for i in range(size)]))
    return out


def spread(shard, size, axis="tensor"):
    return [shard] + [
        lax.ppermute(shard, axis, [(i, (i - k) % size) for i in range(size)])
        for k in range(1, size)
    ]


def spread_ring(shard, axis="tensor"):
    down = [(i, (i - 1) % 4) for i in range(4)]
    up = [(i, (i + 1) % 4) for i in range(4)]
    half = shard.shape[0] // 2
    next_one = lax.ppermute(shard, axis, down)
    last_one = lax.ppermute(shard, axis, up)
    top = lax.ppermute(next_one[:half], axis, down)
    bottom = lax.ppermute(last_one[half:], axis, up)
    return [shard, next_one, top, bottom, last_one]


def after(value, earlier):
    return lax.optimization_barrier((value, earlier))[0]


def live_columns(count, shape):
    column = lax.broadcasted_iota(jnp.int32, shape, len(shape) - 1)
    return (column // 32) % 4 < count


def by_heads(array, head_dim):
    head = lax.broadcasted_iota(jnp.int32, array.shape, 1) // head_dim
    zero = jnp.zeros_like(array)
    count = array.shape[1] // head_dim
    return jnp.concatenate([jnp.where(head == h, array, zero) for h in range(count)], axis=0)


def head_blocks(array, rows, head_dim):
    count = array.shape[1] // head_dim
    return [
        array[h * rows : (h + 1) * rows, h * head_dim : (h + 1) * head_dim] for h in range(count)
    ]


def cond_kernel(s_ref, hidden_ref, weight_ref, c0, c1, c2, c3, total_ref):
    length = c0.shape[0]
    total_ref[...] = dot(hidden_ref[...], weight_ref[...])
    for k, ref in enumerate((c0, c1, c2, c3)):
        start = pl.multiple_of(((s_ref[0] + 4 - k) % 4) * length, length)
        ref[...] = total_ref[pl.ds(start, length), :].astype(BF16)


def project_kernel(dims, shift, s_ref, p0, p1, top, bottom, p3, weight_ref, *rest):
    out_ref, total_ref = rest[-2:]
    step = pl.program_id(0)
    half = top.shape[0]
    for k, ref in ((0, p0), (1, p1), (3, p3)):

        @pl.when(step == k)
        def _(ref=ref, k=k):
            term = dot(ref[...], weight_ref[...], dims)
            total_ref[...] = term if k == 0 else total_ref[...] + term

    @pl.when(step == 2)
    def _():
        total_ref[:half, :] += dot(top[...], weight_ref[...], dims)
        total_ref[half:, :] += dot(bottom[...], weight_ref[...], dims)

    @pl.when(step == pl.num_programs(0) - 1)
    def _():
        rows = total_ref.shape[0]
        moved = pltpu.roll(total_ref[...], rows - shift, 0)
        index = lax.broadcasted_iota(jnp.int32, moved.shape, 0)
        result = jnp.where(index < rows - shift, moved, 0.0).astype(BF16)
        if len(rest) == 2:
            out_ref[...] = result
        else:
            blocks, _, length, _ = out_ref.shape
            for block in range(blocks):
                span = slice(block * length, (block + 1) * length)
                out_ref[block, 0] = rest[0][span, :]
                out_ref[block, 1] = result[span, :]


def encode_kernel(
    s_ref,
    x_ref,
    c0,
    c1,
    c2,
    c3,
    enc_query_ref,
    enc_out_ref,
    cond_ref,
    queries_ref,
    probs_ref,
    encoded_ref,
):
    width = x_ref.shape[1]
    x = x_ref[...]
    cond = (c0[...].astype(F32) + c1[...].astype(F32)) + (
        c2[...].astype(F32) + c3[...].astype(F32)
    )
    cond = cond.astype(BF16)
    cond_ref[...] = cond
    length = cond.shape[0]
    queries = dot(x, enc_query_ref[...]).astype(BF16)
    queries_ref[...] = queries
    attended = []
    for head in range(width // ENC_HEAD_DIM):
        cols = slice(head * ENC_HEAD_DIM, (head + 1) * ENC_HEAD_DIM)
        vals = slice(width + head * ENC_HEAD_DIM, width + (head + 1) * ENC_HEAD_DIM)
        exponents = jnp.exp(dot(cond[:, cols], queries[:, cols], ROWS_T) * ENC_SCALING)
        probs = exponents / jnp.sum(exponents, axis=0, keepdims=True)
        probs_ref[head * length : (head + 1) * length, :] = probs
        attended.append(dot(probs.astype(BF16), cond[:, vals], COLS_T).astype(BF16))
    attended = jnp.concatenate(attended, axis=1)
    mixing = dot(attended, enc_out_ref[...])
    encoded_ref[...] = (x.astype(F32) + mixing).astype(BF16)


def pick(refs, query_ref, d_ctx_ref):
    for k, ref in enumerate(refs):

        @pl.when(pl.program_id(0) == k)
        def _(ref=ref):
            query_ref[...] = by_heads(ref[0], HEAD_DIM)
            d_ctx_ref[...] = by_heads(ref[1], HEAD_DIM)


def attention_kernel(
    s_ref,
    encoded_ref,
    key_w_ref,
    val_w_ref,
    q0,
    q1,
    q2,
    q3,
    probs_ref,
    d_scores_ref,
    out_ref,
    query_ref,
    d_ctx_ref,
):
    width = encoded_ref.shape[1]
    length = out_ref.shape[1]
    pick((q0, q1, q2, q3), query_ref, d_ctx_ref)
    encoded = encoded_ref[...]
    keys = dot(encoded, key_w_ref[...].reshape(-1, key_w_ref.shape[3])[:width]).astype(BF16)
    vals = dot(encoded, val_w_ref[...].reshape(-1, val_w_ref.shape[3])[:width]).astype(BF16)
    count = s_ref[1]
    scores = dot(query_ref[...], keys, ROWS_T) * SCALING
    expd = jnp.where(live_columns(count, scores.shape), jnp.exp(scores), 0.0)
    totals = jnp.sum(expd, axis=1, keepdims=True)
    probs = expd / jnp.where(count > 0, totals, 1.0)
    probs_low = probs.astype(BF16)
    probs_ref[0] = probs_low
    ctx = head_blocks(dot(probs_low, vals), length, HEAD_DIM)
    out_ref[0] = jnp.concatenate(ctx, axis=1).astype(BF16)
    weighted = probs * dot(d_ctx_ref[...], vals, ROWS_T)
    d_scores = (weighted - probs * jnp.sum(weighted, axis=1, keepdims=True)) * SCALING
    d_scores = d_scores.astype(BF16)
    d_scores_ref[0] = d_scores
    d_query = head_blocks(dot(d_scores, keys), length, HEAD_DIM)
    out_ref[1] = jnp.concatenate(d_query, axis=1).astype(BF16)


def encoded_back_kernel(
    s_ref,
    d_scores_ref,
    probs_ref,
    q0,
    q1,
    q2,
    q3,
    key_w_ref,
    val_w_ref,
    enc_out_ref,
    enc_probs_ref,
    enc_queries_ref,
    cond_ref,
    d_cond_ref,
    query_ref,
    d_ctx_ref,
    total_ref,
):
    step = pl.program_id(0)
    width = total_ref.shape[1]
    pick((q0, q1, q2, q3), query_ref, d_ctx_ref)
    d_keys = dot(d_scores_ref[0], query_ref[...], COLS_T).astype(BF16)
    d_vals = dot(probs_ref[0], d_ctx_ref[...], COLS_T).astype(BF16)
    term = dot(d_keys, key_w_ref[...].reshape(-1, key_w_ref.shape[3])[:width], ROWS_T)
    term = term + dot(d_vals, val_w_ref[...].reshape(-1, val_w_ref.shape[3])[:width], ROWS_T)
    term = term.astype(BF16).astype(F32)

    @pl.when(step == 0)
    def _():
        total_ref[...] = term

    @pl.when(step > 0)
    def _():
        total_ref[...] += term

    @pl.when(step == pl.num_programs(0) - 1)
    def _():
        length = cond_ref.shape[0]
        d_att = dot(total_ref[...].astype(BF16), enc_out_ref[...], ROWS_T).astype(BF16)
        probs = enc_probs_ref[...]
        d_probs = dot(by_heads(cond_ref[:, width:], ENC_HEAD_DIM), d_att, ROWS_T)
        weighted = probs * d_probs
        sums = jnp.sum(weighted.reshape(-1, length, weighted.shape[1]), axis=1, keepdims=True)
        spread_sums = (probs.reshape(-1, length, probs.shape[1]) * sums).reshape(probs.shape)
        d_scores = (weighted - spread_sums) * ENC_SCALING
        live = live_columns(s_ref[1], probs.shape)
        d_scores = jnp.where(live, d_scores, 0.0).astype(BF16)
        low = jnp.where(live, probs, 0.0).astype(BF16)
        d_keys = head_blocks(dot(d_scores, enc_queries_ref[...]), length, ENC_HEAD_DIM)
        d_vals = head_blocks(dot(low, d_att), length, ENC_HEAD_DIM)
        d_cond_ref[...] = jnp.concatenate(d_keys + d_vals, axis=1).astype(BF16)


def placed_rows(rows, by, shift):
    moved = pltpu.roll(rows, by, 0)
    if shift == 0:
        return moved
    index = lax.broadcasted_iota(jnp.int32, rows.shape, 0)
    return jnp.where(index >= shift, moved, 0.0)


def outputs_kernel(
    shift,
    s_ref,
    c0,
    c1,
    c2,
    c3,
    out_w_ref,
    query_w_ref,
    hidden_ref,
    cotangent_ref,
    mixed_ref,
    grad_ref,
    mixed_sum_ref,
    grad_sum_ref,
):
    step = pl.program_id(0)
    half = out_w_ref.shape[2] // 2
    wide = out_w_ref.shape[3]
    length = c0.shape[1]
    parts = (c0, c1, c2, c3)
    ctx = jnp.concatenate([ref[0] for ref in parts], axis=0)
    d_query = jnp.concatenate([ref[1] for ref in parts], axis=0)

    @pl.when(step == 0)
    def _():
        mixed_sum_ref[...] = jnp.zeros_like(mixed_sum_ref)
        grad_sum_ref[...] = jnp.zeros_like(grad_sum_ref)

    for side in range(2):
        weight = out_w_ref[:, :, side * half : (side + 1) * half, :].reshape(-1, wide)
        mixed_sum_ref[:, side * wide : (side + 1) * wide] += dot(ctx, weight)
    grad_sum_ref[...] += dot(d_query, query_w_ref[...].reshape(-1, wide), ROWS_T)

    @pl.when(step == pl.num_programs(0) - 1)
    def _():
        by = (s_ref[0] * length + shift) % mixed_ref.shape[0]
        moved = placed_rows(mixed_sum_ref[...], by, shift)
        mixed_ref[...] = (hidden_ref[...].astype(F32) + moved).astype(mixed_ref.dtype)
        moved = placed_rows(grad_sum_ref[...], by, shift)
        grad_ref[...] = cotangent_ref[...].astype(F32) + moved


def shards(
    hidden,
    cotangent,
    counts,
    slot_of,
    neighbours,
    query_weight,
    key_weight,
    value_weight,
    out_weight,
    cond_weight,
    enc_query,
    enc_out,
):
    tokens, part_width = hidden.shape
    head_width = query_weight.shape[1]
    blocks = counts.shape[1]
    slots_per = slot_of.shape[2]
    item_total = blocks * slots_per
    slot_total, quarter, enc_width = neighbours.shape
    block_len = tokens // blocks
    shift = block_len - 1
    n_tensor = lax.axis_size("tensor")
    n_dp = lax.axis_size("dp")
    here = lax.axis_index("tensor")
    row = lax.axis_index("dp")
    all_width = head_width * n_tensor
    rows = slots_per * quarter * n_tensor
    enc_rows = enc_width // ENC_HEAD_DIM * block_len
    head_rows = head_width // HEAD_DIM * block_len
    sds = jax.ShapeDtypeStruct

    seq_counts = counts[0]
    count = lax.dynamic_slice_in_dim(seq_counts, here, 1, 0)
    scalars = jnp.concatenate([here.astype(jnp.int32)[None], count])

    wq_part = lax.dynamic_slice_in_dim(
        query_weight.reshape(n_tensor, part_width, head_width), row * SLICE, SLICE, 1
    )
    wo_part = lax.dynamic_slice_in_dim(out_weight, row * (SLICE // 2), SLICE // 2, 0)
    wo_part = wo_part.reshape(SLICE // 2, n_tensor, 2, head_width).transpose(1, 2, 0, 3)
    wo_part = wo_part.reshape(n_tensor, SLICE, head_width)
    kv_part = jnp.concatenate(
        [
            lax.dynamic_slice_in_dim(key_weight, row * SLICE, SLICE, 0),
            lax.dynamic_slice_in_dim(value_weight, row * SLICE, SLICE, 0),
        ],
        axis=0,
    )
    kv_part = jnp.broadcast_to(kv_part[None], (n_tensor, 2 * SLICE, head_width))
    weight_parts = exchange(jnp.concatenate([kv_part, wq_part, wo_part], axis=1), here)
    kv_parts = jnp.stack([part[: 2 * SLICE] for part in weight_parts])
    qo_parts = jnp.stack([part[2 * SLICE :] for part in weight_parts])
    hidden_parts = spread_ring(hidden)
    cot_parts = spread_ring(cotangent)
    near = (hidden_parts[1], hidden_parts[4])
    kv_all = lax.all_gather(after(kv_parts, near), "dp", axis=0)

    def weight_spec(index):
        return pl.BlockSpec((n_dp, 1, SLICE, head_width), lambda g, s: (0, g, index, 0))

    c_spec = whole(block_len, 2 * enc_width)
    own_cond, *to_send = call(
        cond_kernel,
        "cond",
        1,
        [whole(tokens, part_width), whole(part_width, 2 * enc_width)],
        (c_spec,) * 4,
        (sds((block_len, 2 * enc_width), BF16),) * 4,
        [pltpu.VMEM((tokens, 2 * enc_width), F32)],
        20,
    )(scalars, hidden, cond_weight)
    cond_parts = [own_cond] + [
        lax.ppermute(array, "tensor", [(i, (i - k) % n_tensor) for i in range(n_tensor)])
        for k, array in enumerate(to_send, 1)
    ]

    def projected(parts, weight, dims, weight_block, weight_map, name, before=None):
        out = (tokens, head_width)
        if before is not None:
            out = (blocks, 2, block_len, head_width)
        return call(
            functools.partial(project_kernel, dims, shift),
            name,
            n_tensor,
            [whole(*part.shape) for part in parts]
            + [pl.BlockSpec(weight_block, weight_map)]
            + ([] if before is None else [whole(tokens, head_width)]),
            whole(*out),
            sds(out, BF16),
            [pltpu.VMEM((tokens, head_width), F32)],
            16,
        )(scalars, *parts, weight, *([] if before is None else [before]))

    query = projected(
        hidden_parts,
        query_weight,
        PLAIN,
        (part_width, head_width),
        lambda g, s: ((s[0] + g) % 4, 0),
        "query",
    )

    live = jnp.arange(slots_per)[None, :] < after(seq_counts, (query, cot_parts[1:], cond_parts[1:]))[:, None]
    slot_flat = slot_of.reshape(item_total)
    matches = (jnp.arange(slot_total)[:, None] == slot_flat[None, :]) & live.reshape(item_total)[
        None, :
    ]
    returned = lax.all_to_all(neighbours, "dp", split_axis=0, concat_axis=0, tiled=True)
    items = jnp.einsum(
        "si,sre->ire", matches.astype(BF16), returned, preferred_element_type=F32
    ).astype(BF16)
    items = items.reshape(blocks, slots_per * quarter, enc_width)
    x = lax.all_to_all(items, "tensor", split_axis=0, concat_axis=0, tiled=True)
    x = x.reshape(rows, enc_width)

    qo_all = lax.all_gather(after(qo_parts, items), "dp", axis=0)
    query_d_ctx = projected(
        after(tuple(cot_parts), (items, cond_parts[1:])),
        out_weight,
        ROWS_T,
        (head_width, part_width),
        lambda g, s: (0, (s[0] + g) % 4),
        "d_ctx",
        before=query,
    )
    query_parts = exchange(query_d_ctx, here)

    c_spec = whole(block_len, 2 * enc_width)
    w_spec = whole(enc_width, enc_width)
    r_spec = whole(rows, enc_width)
    p_spec = whole(enc_rows, rows)
    cond, enc_queries, enc_probs, encoded = call(
        encode_kernel,
        "encode",
        1,
        [r_spec] + [c_spec] * 4 + [w_spec] * 2,
        (c_spec, r_spec, p_spec, r_spec),
        (
            sds((block_len, 2 * enc_width), BF16),
            sds((rows, enc_width), BF16),
            sds((enc_rows, rows), F32),
            sds((rows, enc_width), BF16),
        ),
        [],
        60,
    )(scalars, x, *cond_parts, enc_query, enc_out)

    q_spec = whole(2, block_len, head_width)
    big = pltpu.VMEM((head_rows, head_width), BF16)
    both_spec = pl.BlockSpec((2, block_len, head_width), lambda g, s: (0, 0, (s[0] + g) % 4))
    probs, d_scores, both = call(
        attention_kernel,
        "attention",
        n_tensor,
        [r_spec, weight_spec(0), weight_spec(1)] + [q_spec] * 4,
        (
            group(head_rows, rows),
            group(head_rows, rows),
            both_spec,
        ),
        (
            sds((n_tensor, head_rows, rows), BF16),
            sds((n_tensor, head_rows, rows), BF16),
            sds((2, block_len, all_width), BF16),
        ),
        [big, big],
        60,
    )(scalars, encoded, kv_all, kv_all, *query_parts)
    both_parts = spread(both, n_tensor)

    d_cond = call(
        encoded_back_kernel,
        "encoded_back",
        n_tensor,
        [group(head_rows, rows), group(head_rows, rows)]
        + [q_spec] * 4
        + [weight_spec(0), weight_spec(1), w_spec, p_spec, r_spec, c_spec],
        c_spec,
        sds((block_len, 2 * enc_width), BF16),
        [big, big, pltpu.VMEM((rows, enc_width), F32)],
        60,
    )(
        scalars,
        d_scores,
        probs,
        *query_parts,
        kv_all,
        kv_all,
        enc_out,
        enc_probs,
        enc_queries,
        cond,
    )
    d_cond_parts = spread(after(d_cond, both_parts[1]), n_tensor)

    out_spec = whole(tokens, part_width)
    acc = pltpu.VMEM((tokens, part_width), F32)
    mixed, from_query = call(
        functools.partial(outputs_kernel, shift),
        "outputs",
        n_tensor,
        [both_spec] * 4 + [weight_spec(1), weight_spec(0), out_spec, out_spec],
        (out_spec, out_spec),
        (sds((tokens, part_width), BF16), sds((tokens, part_width), F32)),
        [acc, acc],
        60,
    )(scalars, *both_parts, qo_all, qo_all, hidden, cotangent)
    d_cond_parts = after(d_cond_parts, from_query)
    d_cond_all = lax.dynamic_slice_in_dim(
        jnp.stack(d_cond_parts * 2), (n_tensor - here) % n_tensor, n_tensor, 0
    ).reshape(tokens, 2 * enc_width)
    grad_hidden = (from_query + dot(d_cond_all, cond_weight, ROWS_T)).astype(BF16)
    return (mixed, grad_hidden)


def solution(mesh):
    placed = (
        P("dp", "tensor"),
        P("dp", "tensor"),
        P("dp", None),
        P("dp", None, None),
        P("dp", "tensor", None),
        P(None, "tensor"),
        P(None, "tensor"),
        P(None, "tensor"),
        P("tensor", None),
        P("tensor", None),
        P(),
        P(),
    )
    return jax.shard_map(
        shards,
        mesh=mesh,
        in_specs=placed,
        out_specs=(P("dp", "tensor"), P("dp", "tensor")),
        check_vma=False,
    )
```

```python
import functools
import math

import jax
import jax.numpy as jnp
from jax import lax
from jax.experimental import pallas as pl
from jax.experimental.pallas import tpu as pltpu
from jax.sharding import PartitionSpec as P

HEAD_DIM = 128
ENC_HEAD_DIM = 128
F32 = jnp.float32
BF16 = jnp.bfloat16
PLAIN = (((1,), (0,)), ((), ()))
ROWS_T = (((1,), (1,)), ((), ()))
COLS_T = (((0,), (0,)), ((), ()))
SCALING = 1.0 / math.sqrt(HEAD_DIM)
ENC_SCALING = 1.0 / math.sqrt(ENC_HEAD_DIM)
SLICE = 32


def dot(a, b, dims=PLAIN):
    return lax.dot_general(a, b, dims, preferred_element_type=F32)


def call(kernel, name, grid, in_specs, out_specs, out_shape, scratch, vmem_mib):
    return pl.pallas_call(
        kernel,
        out_shape=out_shape,
        grid_spec=pltpu.PrefetchScalarGridSpec(
            num_scalar_prefetch=1,
            grid=(grid,),
            in_specs=in_specs,
            out_specs=out_specs,
            scratch_shapes=scratch,
        ),
        compiler_params=pltpu.CompilerParams(
            vmem_limit_bytes=vmem_mib * 1024 * 1024, dimension_semantics=("arbitrary",)
        ),
        name=name,
    )


def whole(*shape):
    return pl.BlockSpec(shape, lambda g, s: (0,) * len(shape))


def group(*shape):
    return pl.BlockSpec((1,) + shape, lambda g, s: (g,) + (0,) * len(shape))


def exchange(pieces, position, axis="tensor"):
    size = pieces.shape[0]
    out = [lax.dynamic_index_in_dim(pieces, position, 0, keepdims=False)]
    for k in range(1, size):
        piece = lax.dynamic_index_in_dim(pieces, (position - k) % size, 0, keepdims=False)
        out.append(lax.ppermute(piece, axis, [(i, (i - k) % size) for i in range(size)]))
    return out


def spread(shard, size, axis="tensor"):
    return [shard] + [
        lax.ppermute(shard, axis, [(i, (i - k) % size) for i in range(size)])
        for k in range(1, size)
    ]


def spread_ring(shard, axis="tensor"):
    down = [(i, (i - 1) % 4) for i in range(4)]
    up = [(i, (i + 1) % 4) for i in range(4)]
    half = shard.shape[0] // 2
    next_one = lax.ppermute(shard, axis, down)
    last_one = lax.ppermute(shard, axis, up)
    far_top = lax.ppermute(next_one[:half], axis, down)
    far_bottom = lax.ppermute(last_one[half:], axis, up)
    return [shard, next_one, far_top, far_bottom, last_one]


def spread_halves(shard, axis="tensor"):
    down = [(i, (i - 1) % 4) for i in range(4)]
    up = [(i, (i + 1) % 4) for i in range(4)]
    half = shard.shape[0] // 2
    top, bottom = shard[:half], shard[half:]
    next_top = lax.ppermute(top, axis, down)
    last_bottom = lax.ppermute(bottom, axis, up)
    next_bottom = lax.ppermute(bottom, axis, down)
    last_top = lax.ppermute(top, axis, up)
    far_top = lax.ppermute(next_top, axis, down)
    far_bottom = lax.ppermute(last_bottom, axis, up)
    return [shard, next_top, next_bottom, far_top, far_bottom, last_top, last_bottom]


def after(value, earlier):
    return lax.optimization_barrier((value, earlier))[0]


def live_columns(count, shape):
    column = lax.broadcasted_iota(jnp.int32, shape, len(shape) - 1)
    return (column // 32) % 4 < count


def by_heads(array, head_dim):
    head = lax.broadcasted_iota(jnp.int32, array.shape, 1) // head_dim
    zero = jnp.zeros_like(array)
    count = array.shape[1] // head_dim
    return jnp.concatenate([jnp.where(head == h, array, zero) for h in range(count)], axis=0)


def head_blocks(array, rows, head_dim):
    count = array.shape[1] // head_dim
    return [
        array[h * rows : (h + 1) * rows, h * head_dim : (h + 1) * head_dim] for h in range(count)
    ]


def cond_kernel(s_ref, hidden_ref, weight_ref, c0, c1, c2, c3, total_ref):
    length = c0.shape[0]
    total_ref[...] = dot(hidden_ref[...], weight_ref[...])
    for k, ref in enumerate((c0, c1, c2, c3)):
        start = pl.multiple_of(((s_ref[0] + 4 - k) % 4) * length, length)
        ref[...] = total_ref[pl.ds(start, length), :].astype(BF16)


def project_kernel(dims, shift, counts, s_ref, *refs):
    out_ref, total_ref = refs[-2:]
    weight_ref = refs[sum(counts)]
    rest = refs[sum(counts) + 1 :]
    step = pl.program_id(0)
    for k, size in enumerate(counts):
        first = sum(counts[:k])
        parts = refs[first : first + size]

        @pl.when(step == k)
        def _(parts=parts, k=k):
            part = jnp.concatenate([ref[...] for ref in parts], axis=0)
            term = dot(part, weight_ref[...], dims)
            total_ref[...] = term if k == 0 else total_ref[...] + term

    @pl.when(step == pl.num_programs(0) - 1)
    def _():
        rows = total_ref.shape[0]
        moved = pltpu.roll(total_ref[...], rows - shift, 0)
        index = lax.broadcasted_iota(jnp.int32, moved.shape, 0)
        result = jnp.where(index < rows - shift, moved, 0.0).astype(BF16)
        if len(rest) == 2:
            out_ref[...] = result
        else:
            blocks, _, length, _ = out_ref.shape
            for block in range(blocks):
                span = slice(block * length, (block + 1) * length)
                out_ref[block, 0] = rest[0][span, :]
                out_ref[block, 1] = result[span, :]


def encode_kernel(
    s_ref,
    x_ref,
    c0,
    c1,
    c2,
    c3,
    enc_query_ref,
    enc_out_ref,
    cond_ref,
    queries_ref,
    probs_ref,
    encoded_ref,
):
    width = x_ref.shape[1]
    x = x_ref[...]
    cond = (c0[...].astype(F32) + c1[...].astype(F32)) + (
        c2[...].astype(F32) + c3[...].astype(F32)
    )
    cond = cond.astype(BF16)
    cond_ref[...] = cond
    length = cond.shape[0]
    queries = dot(x, enc_query_ref[...]).astype(BF16)
    queries_ref[...] = queries
    attended = []
    for head in range(width // ENC_HEAD_DIM):
        cols = slice(head * ENC_HEAD_DIM, (head + 1) * ENC_HEAD_DIM)
        vals = slice(width + head * ENC_HEAD_DIM, width + (head + 1) * ENC_HEAD_DIM)
        exponents = jnp.exp(dot(cond[:, cols], queries[:, cols], ROWS_T) * ENC_SCALING)
        probs = exponents / jnp.sum(exponents, axis=0, keepdims=True)
        probs_ref[head * length : (head + 1) * length, :] = probs
        attended.append(dot(probs.astype(BF16), cond[:, vals], COLS_T).astype(BF16))
    attended = jnp.concatenate(attended, axis=1)
    mixing = dot(attended, enc_out_ref[...])
    encoded_ref[...] = (x.astype(F32) + mixing).astype(BF16)


def pick(refs, query_ref, d_ctx_ref):
    for k, ref in enumerate(refs):

        @pl.when(pl.program_id(0) == k)
        def _(ref=ref):
            query_ref[...] = by_heads(ref[0], HEAD_DIM)
            d_ctx_ref[...] = by_heads(ref[1], HEAD_DIM)


def attention_kernel(
    s_ref,
    encoded_ref,
    key_w_ref,
    val_w_ref,
    q0,
    q1,
    q2,
    q3,
    probs_ref,
    d_scores_ref,
    out_ref,
    query_ref,
    d_ctx_ref,
):
    width = encoded_ref.shape[1]
    length = out_ref.shape[1]
    pick((q0, q1, q2, q3), query_ref, d_ctx_ref)
    encoded = encoded_ref[...]
    keys = dot(encoded, key_w_ref[...].reshape(-1, key_w_ref.shape[3])[:width]).astype(BF16)
    vals = dot(encoded, val_w_ref[...].reshape(-1, val_w_ref.shape[3])[:width]).astype(BF16)
    count = s_ref[1]
    scores = dot(query_ref[...], keys, ROWS_T) * SCALING
    expd = jnp.where(live_columns(count, scores.shape), jnp.exp(scores), 0.0)
    totals = jnp.sum(expd, axis=1, keepdims=True)
    probs = expd / jnp.where(count > 0, totals, 1.0)
    probs_low = probs.astype(BF16)
    probs_ref[0] = probs_low
    ctx = head_blocks(dot(probs_low, vals), length, HEAD_DIM)
    out_ref[0] = jnp.concatenate(ctx, axis=1).astype(BF16)
    weighted = probs * dot(d_ctx_ref[...], vals, ROWS_T)
    d_scores = (weighted - probs * jnp.sum(weighted, axis=1, keepdims=True)) * SCALING
    d_scores = d_scores.astype(BF16)
    d_scores_ref[0] = d_scores
    d_query = head_blocks(dot(d_scores, keys), length, HEAD_DIM)
    out_ref[1] = jnp.concatenate(d_query, axis=1).astype(BF16)


def encoded_back_kernel(
    s_ref,
    d_scores_ref,
    probs_ref,
    q0,
    q1,
    q2,
    q3,
    key_w_ref,
    val_w_ref,
    enc_out_ref,
    enc_probs_ref,
    enc_queries_ref,
    cond_ref,
    d_cond_ref,
    query_ref,
    d_ctx_ref,
    total_ref,
):
    step = pl.program_id(0)
    width = total_ref.shape[1]
    pick((q0, q1, q2, q3), query_ref, d_ctx_ref)
    d_keys = dot(d_scores_ref[0], query_ref[...], COLS_T).astype(BF16)
    d_vals = dot(probs_ref[0], d_ctx_ref[...], COLS_T).astype(BF16)
    term = dot(d_keys, key_w_ref[...].reshape(-1, key_w_ref.shape[3])[:width], ROWS_T)
    term = term + dot(d_vals, val_w_ref[...].reshape(-1, val_w_ref.shape[3])[:width], ROWS_T)
    term = term.astype(BF16).astype(F32)

    @pl.when(step == 0)
    def _():
        total_ref[...] = term

    @pl.when(step > 0)
    def _():
        total_ref[...] += term

    @pl.when(step == pl.num_programs(0) - 1)
    def _():
        length = cond_ref.shape[0]
        d_att = dot(total_ref[...].astype(BF16), enc_out_ref[...], ROWS_T).astype(BF16)
        probs = enc_probs_ref[...]
        d_probs = dot(by_heads(cond_ref[:, width:], ENC_HEAD_DIM), d_att, ROWS_T)
        weighted = probs * d_probs
        sums = jnp.sum(weighted.reshape(-1, length, weighted.shape[1]), axis=1, keepdims=True)
        spread_sums = (probs.reshape(-1, length, probs.shape[1]) * sums).reshape(probs.shape)
        d_scores = (weighted - spread_sums) * ENC_SCALING
        live = live_columns(s_ref[1], probs.shape)
        d_scores = jnp.where(live, d_scores, 0.0).astype(BF16)
        low = jnp.where(live, probs, 0.0).astype(BF16)
        d_keys = head_blocks(dot(d_scores, enc_queries_ref[...]), length, ENC_HEAD_DIM)
        d_vals = head_blocks(dot(low, d_att), length, ENC_HEAD_DIM)
        d_cond_ref[...] = jnp.concatenate(d_keys + d_vals, axis=1).astype(BF16)


def placed_rows(rows, by, shift):
    moved = pltpu.roll(rows, by, 0)
    if shift == 0:
        return moved
    index = lax.broadcasted_iota(jnp.int32, rows.shape, 0)
    return jnp.where(index >= shift, moved, 0.0)


def outputs_kernel(
    shift,
    s_ref,
    c0,
    c1,
    c2,
    c3,
    out_w_ref,
    query_w_ref,
    hidden_ref,
    cotangent_ref,
    mixed_ref,
    grad_ref,
    mixed_sum_ref,
    grad_sum_ref,
):
    step = pl.program_id(0)
    half = out_w_ref.shape[2] // 2
    wide = out_w_ref.shape[3]
    length = c0.shape[1]
    parts = (c0, c1, c2, c3)
    ctx = jnp.concatenate([ref[0] for ref in parts], axis=0)
    d_query = jnp.concatenate([ref[1] for ref in parts], axis=0)

    @pl.when(step == 0)
    def _():
        mixed_sum_ref[...] = jnp.zeros_like(mixed_sum_ref)
        grad_sum_ref[...] = jnp.zeros_like(grad_sum_ref)

    for side in range(2):
        weight = out_w_ref[:, :, side * half : (side + 1) * half, :].reshape(-1, wide)
        mixed_sum_ref[:, side * wide : (side + 1) * wide] += dot(ctx, weight)
    grad_sum_ref[...] += dot(d_query, query_w_ref[...].reshape(-1, wide), ROWS_T)

    @pl.when(step == pl.num_programs(0) - 1)
    def _():
        by = (s_ref[0] * length + shift) % mixed_ref.shape[0]
        moved = placed_rows(mixed_sum_ref[...], by, shift)
        mixed_ref[...] = (hidden_ref[...].astype(F32) + moved).astype(mixed_ref.dtype)
        moved = placed_rows(grad_sum_ref[...], by, shift)
        grad_ref[...] = cotangent_ref[...].astype(F32) + moved


def shards(
    hidden,
    cotangent,
    counts,
    slot_of,
    neighbours,
    query_weight,
    key_weight,
    value_weight,
    out_weight,
    cond_weight,
    enc_query,
    enc_out,
):
    tokens, part_width = hidden.shape
    head_width = query_weight.shape[1]
    blocks = counts.shape[1]
    slots_per = slot_of.shape[2]
    item_total = blocks * slots_per
    slot_total, quarter, enc_width = neighbours.shape
    block_len = tokens // blocks
    shift = block_len - 1
    n_tensor = lax.axis_size("tensor")
    n_dp = lax.axis_size("dp")
    here = lax.axis_index("tensor")
    row = lax.axis_index("dp")
    all_width = head_width * n_tensor
    rows = slots_per * quarter * n_tensor
    enc_rows = enc_width // ENC_HEAD_DIM * block_len
    head_rows = head_width // HEAD_DIM * block_len
    sds = jax.ShapeDtypeStruct

    seq_counts = counts[0]
    count = lax.dynamic_slice_in_dim(seq_counts, here, 1, 0)
    scalars = jnp.concatenate([here.astype(jnp.int32)[None], count])

    wq_part = lax.dynamic_slice_in_dim(
        query_weight.reshape(n_tensor, part_width, head_width), row * SLICE, SLICE, 1
    )
    wo_part = lax.dynamic_slice_in_dim(out_weight, row * (SLICE // 2), SLICE // 2, 0)
    wo_part = wo_part.reshape(SLICE // 2, n_tensor, 2, head_width).transpose(1, 2, 0, 3)
    wo_part = wo_part.reshape(n_tensor, SLICE, head_width)
    kv_part = jnp.concatenate(
        [
            lax.dynamic_slice_in_dim(key_weight, row * SLICE, SLICE, 0),
            lax.dynamic_slice_in_dim(value_weight, row * SLICE, SLICE, 0),
        ],
        axis=0,
    )
    kv_part = jnp.broadcast_to(kv_part[None], (n_tensor, 2 * SLICE, head_width))
    weight_parts = exchange(jnp.concatenate([kv_part, wq_part, wo_part], axis=1), here)
    kv_parts = jnp.stack([part[: 2 * SLICE] for part in weight_parts])
    qo_parts = jnp.stack([part[2 * SLICE :] for part in weight_parts])
    hidden_parts = spread_halves(hidden)
    cot_parts = spread_ring(cotangent)

    def weight_spec(index):
        return pl.BlockSpec((n_dp, 1, SLICE, head_width), lambda g, s: (0, g, index, 0))

    c_spec = whole(block_len, 2 * enc_width)
    own_cond, *to_send = call(
        cond_kernel,
        "cond",
        1,
        [whole(tokens, part_width), whole(part_width, 2 * enc_width)],
        (c_spec,) * 4,
        (sds((block_len, 2 * enc_width), BF16),) * 4,
        [pltpu.VMEM((tokens, 2 * enc_width), F32)],
        20,
    )(scalars, hidden, cond_weight)
    ahead = (hidden_parts[1], hidden_parts[6], own_cond)
    kv_all = lax.all_gather(after(kv_parts, ahead), "dp", axis=0)
    cond_parts = [own_cond] + [
        lax.ppermute(array, "tensor", [(i, (i - k) % n_tensor) for i in range(n_tensor)])
        for k, array in enumerate(to_send, 1)
    ]

    def projected(parts, counts, weight, dims, weight_block, weight_map, name, before=None):
        out = (tokens, head_width)
        if before is not None:
            out = (blocks, 2, block_len, head_width)
        return call(
            functools.partial(project_kernel, dims, shift, counts),
            name,
            n_tensor,
            [whole(*part.shape) for part in parts]
            + [pl.BlockSpec(weight_block, weight_map)]
            + ([] if before is None else [whole(tokens, head_width)]),
            whole(*out),
            sds(out, BF16),
            [pltpu.VMEM((tokens, head_width), F32)],
            16,
        )(scalars, *parts, weight, *([] if before is None else [before]))

    query = projected(
        hidden_parts,
        (1, 2, 2, 2),
        query_weight,
        PLAIN,
        (part_width, head_width),
        lambda g, s: ((s[0] + g) % 4, 0),
        "query",
    )

    live = jnp.arange(slots_per)[None, :] < after(seq_counts, (query, cot_parts[1:], cond_parts[1:]))[:, None]
    slot_flat = slot_of.reshape(item_total)
    matches = (jnp.arange(slot_total)[:, None] == slot_flat[None, :]) & live.reshape(item_total)[
        None, :
    ]
    returned = lax.all_to_all(neighbours, "dp", split_axis=0, concat_axis=0, tiled=True)
    items = jnp.einsum(
        "si,sre->ire", matches.astype(BF16), returned, preferred_element_type=F32
    ).astype(BF16)
    items = items.reshape(blocks, slots_per * quarter, enc_width)
    x = lax.all_to_all(items, "tensor", split_axis=0, concat_axis=0, tiled=True)
    x = x.reshape(rows, enc_width)

    qo_all = lax.all_gather(after(qo_parts, items), "dp", axis=0)
    query_d_ctx = projected(
        after(cot_parts, (items, cond_parts[1:])),
        (1, 1, 2, 1),
        out_weight,
        ROWS_T,
        (head_width, part_width),
        lambda g, s: (0, (s[0] + g) % 4),
        "d_ctx",
        before=query,
    )
    query_parts = exchange(query_d_ctx, here)

    c_spec = whole(block_len, 2 * enc_width)
    w_spec = whole(enc_width, enc_width)
    r_spec = whole(rows, enc_width)
    p_spec = whole(enc_rows, rows)
    cond, enc_queries, enc_probs, encoded = call(
        encode_kernel,
        "encode",
        1,
        [r_spec] + [c_spec] * 4 + [w_spec] * 2,
        (c_spec, r_spec, p_spec, r_spec),
        (
            sds((block_len, 2 * enc_width), BF16),
            sds((rows, enc_width), BF16),
            sds((enc_rows, rows), F32),
            sds((rows, enc_width), BF16),
        ),
        [],
        60,
    )(scalars, x, *cond_parts, enc_query, enc_out)

    q_spec = whole(2, block_len, head_width)
    big = pltpu.VMEM((head_rows, head_width), BF16)
    both_spec = pl.BlockSpec((2, block_len, head_width), lambda g, s: (0, 0, (s[0] + g) % 4))
    probs, d_scores, both = call(
        attention_kernel,
        "attention",
        n_tensor,
        [r_spec, weight_spec(0), weight_spec(1)] + [q_spec] * 4,
        (
            group(head_rows, rows),
            group(head_rows, rows),
            both_spec,
        ),
        (
            sds((n_tensor, head_rows, rows), BF16),
            sds((n_tensor, head_rows, rows), BF16),
            sds((2, block_len, all_width), BF16),
        ),
        [big, big],
        60,
    )(scalars, encoded, kv_all, kv_all, *query_parts)
    both_parts = spread(both, n_tensor)

    d_cond = call(
        encoded_back_kernel,
        "encoded_back",
        n_tensor,
        [group(head_rows, rows), group(head_rows, rows)]
        + [q_spec] * 4
        + [weight_spec(0), weight_spec(1), w_spec, p_spec, r_spec, c_spec],
        c_spec,
        sds((block_len, 2 * enc_width), BF16),
        [big, big, pltpu.VMEM((rows, enc_width), F32)],
        60,
    )(
        scalars,
        d_scores,
        probs,
        *query_parts,
        kv_all,
        kv_all,
        enc_out,
        enc_probs,
        enc_queries,
        cond,
    )
    d_cond_parts = spread(after(d_cond, both_parts[1]), n_tensor)

    out_spec = whole(tokens, part_width)
    acc = pltpu.VMEM((tokens, part_width), F32)
    mixed, from_query = call(
        functools.partial(outputs_kernel, shift),
        "outputs",
        n_tensor,
        [both_spec] * 4 + [weight_spec(1), weight_spec(0), out_spec, out_spec],
        (out_spec, out_spec),
        (sds((tokens, part_width), BF16), sds((tokens, part_width), F32)),
        [acc, acc],
        60,
    )(scalars, *both_parts, qo_all, qo_all, hidden, cotangent)
    d_cond_parts = after(d_cond_parts, from_query)
    d_cond_all = lax.dynamic_slice_in_dim(
        jnp.stack(d_cond_parts * 2), (n_tensor - here) % n_tensor, n_tensor, 0
    ).reshape(tokens, 2 * enc_width)
    grad_hidden = (from_query + dot(d_cond_all, cond_weight, ROWS_T)).astype(BF16)
    return (mixed, grad_hidden)


def solution(mesh):
    placed = (
        P("dp", "tensor"),
        P("dp", "tensor"),
        P("dp", None),
        P("dp", None, None),
        P("dp", "tensor", None),
        P(None, "tensor"),
        P(None, "tensor"),
        P(None, "tensor"),
        P("tensor", None),
        P("tensor", None),
        P(),
        P(),
    )
    return jax.shard_map(
        shards,
        mesh=mesh,
        in_specs=placed,
        out_specs=(P("dp", "tensor"), P("dp", "tensor")),
        check_vma=False,
    )
```

```python
import functools
import math

import jax
import jax.numpy as jnp
from jax import lax
from jax.experimental import pallas as pl
from jax.experimental.pallas import tpu as pltpu
from jax.sharding import PartitionSpec as P

HEAD_DIM = 128
ENC_HEAD_DIM = 128
F32 = jnp.float32
BF16 = jnp.bfloat16
PLAIN = (((1,), (0,)), ((), ()))
ROWS_T = (((1,), (1,)), ((), ()))
COLS_T = (((0,), (0,)), ((), ()))
SCALING = 1.0 / math.sqrt(HEAD_DIM)
ENC_SCALING = 1.0 / math.sqrt(ENC_HEAD_DIM)
SLICE = 32


def dot(a, b, dims=PLAIN):
    return lax.dot_general(a, b, dims, preferred_element_type=F32)


def call(kernel, name, grid, in_specs, out_specs, out_shape, scratch, vmem_mib):
    return pl.pallas_call(
        kernel,
        out_shape=out_shape,
        grid_spec=pltpu.PrefetchScalarGridSpec(
            num_scalar_prefetch=1,
            grid=(grid,),
            in_specs=in_specs,
            out_specs=out_specs,
            scratch_shapes=scratch,
        ),
        compiler_params=pltpu.CompilerParams(
            vmem_limit_bytes=vmem_mib * 1024 * 1024, dimension_semantics=("arbitrary",)
        ),
        name=name,
    )


def whole(*shape):
    return pl.BlockSpec(shape, lambda g, s: (0,) * len(shape))


def group(*shape):
    return pl.BlockSpec((1,) + shape, lambda g, s: (g,) + (0,) * len(shape))


def exchange(pieces, position, axis="tensor"):
    size = pieces.shape[0]
    out = [lax.dynamic_index_in_dim(pieces, position, 0, keepdims=False)]
    for k in range(1, size):
        piece = lax.dynamic_index_in_dim(pieces, (position - k) % size, 0, keepdims=False)
        out.append(lax.ppermute(piece, axis, [(i, (i - k) % size) for i in range(size)]))
    return out


def spread(shard, size, axis="tensor"):
    return [shard] + [
        lax.ppermute(shard, axis, [(i, (i - k) % size) for i in range(size)])
        for k in range(1, size)
    ]


def spread_ring(shard, axis="tensor"):
    down = [(i, (i - 1) % 4) for i in range(4)]
    up = [(i, (i + 1) % 4) for i in range(4)]
    half = shard.shape[0] // 2
    next_one = lax.ppermute(shard, axis, down)
    last_one = lax.ppermute(shard, axis, up)
    far_top = lax.ppermute(next_one[:half], axis, down)
    far_bottom = lax.ppermute(last_one[half:], axis, up)
    return [shard, next_one, far_top, far_bottom, last_one]


def spread_halves(shard, axis="tensor"):
    down = [(i, (i - 1) % 4) for i in range(4)]
    up = [(i, (i + 1) % 4) for i in range(4)]
    half = shard.shape[0] // 2
    top, bottom = shard[:half], shard[half:]
    next_top = lax.ppermute(top, axis, down)
    last_bottom = lax.ppermute(bottom, axis, up)
    next_bottom = lax.ppermute(bottom, axis, down)
    last_top = lax.ppermute(top, axis, up)
    far_top = lax.ppermute(next_top, axis, down)
    far_bottom = lax.ppermute(last_bottom, axis, up)
    return [shard, next_top, next_bottom, far_top, far_bottom, last_top, last_bottom]


def after(value, earlier):
    return lax.optimization_barrier((value, earlier))[0]


def live_columns(count, shape):
    column = lax.broadcasted_iota(jnp.int32, shape, len(shape) - 1)
    return (column // 32) % 4 < count


def by_heads(array, head_dim):
    head = lax.broadcasted_iota(jnp.int32, array.shape, 1) // head_dim
    zero = jnp.zeros_like(array)
    count = array.shape[1] // head_dim
    return jnp.concatenate([jnp.where(head == h, array, zero) for h in range(count)], axis=0)


def head_blocks(array, rows, head_dim):
    count = array.shape[1] // head_dim
    return [
        array[h * rows : (h + 1) * rows, h * head_dim : (h + 1) * head_dim] for h in range(count)
    ]


def cond_kernel(s_ref, hidden_ref, weight_ref, c0, c1, c2, c3, total_ref):
    length = c0.shape[0]
    total_ref[...] = dot(hidden_ref[...], weight_ref[...])
    for k, ref in enumerate((c0, c1, c2, c3)):
        start = pl.multiple_of(((s_ref[0] + 4 - k) % 4) * length, length)
        ref[...] = total_ref[pl.ds(start, length), :].astype(BF16)


def project_kernel(dims, shift, counts, s_ref, *refs):
    total_ref = refs[-1]
    weight_ref = refs[sum(counts)]
    rest = refs[sum(counts) + 1 : -1]
    step = pl.program_id(0)
    for k, size in enumerate(counts):
        first = sum(counts[:k])
        parts = refs[first : first + size]

        @pl.when(step == k)
        def _(parts=parts, k=k):
            part = jnp.concatenate([ref[...] for ref in parts], axis=0)
            term = dot(part, weight_ref[...], dims)
            total_ref[...] = term if k == 0 else total_ref[...] + term

    @pl.when(step == pl.num_programs(0) - 1)
    def _():
        rows = total_ref.shape[0]
        moved = pltpu.roll(total_ref[...], rows - shift, 0)
        index = lax.broadcasted_iota(jnp.int32, moved.shape, 0)
        result = jnp.where(index < rows - shift, moved, 0.0)
        if len(rest) == 1:
            rest[0][...] = result.astype(BF16)
        else:
            total_ref[...] = result
            for k, ref in enumerate(rest[1:]):
                length = ref.shape[1]
                start = pl.multiple_of(((s_ref[0] + 4 - k) % 4) * length, length)
                ref[0] = rest[0][pl.ds(start, length), :]
                ref[1] = total_ref[pl.ds(start, length), :].astype(BF16)


def encode_kernel(
    s_ref,
    x_ref,
    c0,
    c1,
    c2,
    c3,
    enc_query_ref,
    enc_out_ref,
    cond_ref,
    queries_ref,
    probs_ref,
    encoded_ref,
):
    width = x_ref.shape[1]
    x = x_ref[...]
    cond = (c0[...].astype(F32) + c1[...].astype(F32)) + (
        c2[...].astype(F32) + c3[...].astype(F32)
    )
    cond = cond.astype(BF16)
    cond_ref[...] = cond
    length = cond.shape[0]
    queries = dot(x, enc_query_ref[...]).astype(BF16)
    queries_ref[...] = queries
    attended = []
    for head in range(width // ENC_HEAD_DIM):
        cols = slice(head * ENC_HEAD_DIM, (head + 1) * ENC_HEAD_DIM)
        vals = slice(width + head * ENC_HEAD_DIM, width + (head + 1) * ENC_HEAD_DIM)
        exponents = jnp.exp(dot(cond[:, cols], queries[:, cols], ROWS_T) * ENC_SCALING)
        probs = exponents / jnp.sum(exponents, axis=0, keepdims=True)
        probs_ref[head * length : (head + 1) * length, :] = probs
        attended.append(dot(probs.astype(BF16), cond[:, vals], COLS_T).astype(BF16))
    attended = jnp.concatenate(attended, axis=1)
    mixing = dot(attended, enc_out_ref[...])
    encoded_ref[...] = (x.astype(F32) + mixing).astype(BF16)


def pick(refs, query_ref, d_ctx_ref):
    for k, ref in enumerate(refs):

        @pl.when(pl.program_id(0) == k)
        def _(ref=ref):
            query_ref[...] = by_heads(ref[0], HEAD_DIM)
            d_ctx_ref[...] = by_heads(ref[1], HEAD_DIM)


def attention_kernel(
    s_ref,
    encoded_ref,
    key_w_ref,
    val_w_ref,
    q0,
    q1,
    q2,
    q3,
    probs_ref,
    d_scores_ref,
    out_ref,
    query_ref,
    d_ctx_ref,
):
    width = encoded_ref.shape[1]
    length = out_ref.shape[1]
    pick((q0, q1, q2, q3), query_ref, d_ctx_ref)
    encoded = encoded_ref[...]
    keys = dot(encoded, key_w_ref[...].reshape(width, -1)).astype(BF16)
    vals = dot(encoded, val_w_ref[...].reshape(width, -1)).astype(BF16)
    count = s_ref[1]
    scores = dot(query_ref[...], keys, ROWS_T) * SCALING
    expd = jnp.where(live_columns(count, scores.shape), jnp.exp(scores), 0.0)
    totals = jnp.sum(expd, axis=1, keepdims=True)
    probs = expd / jnp.where(count > 0, totals, 1.0)
    probs_low = probs.astype(BF16)
    probs_ref[0] = probs_low
    ctx = head_blocks(dot(probs_low, vals), length, HEAD_DIM)
    out_ref[0] = jnp.concatenate(ctx, axis=1).astype(BF16)
    weighted = probs * dot(d_ctx_ref[...], vals, ROWS_T)
    d_scores = (weighted - probs * jnp.sum(weighted, axis=1, keepdims=True)) * SCALING
    d_scores = d_scores.astype(BF16)
    d_scores_ref[0] = d_scores
    d_query = head_blocks(dot(d_scores, keys), length, HEAD_DIM)
    out_ref[1] = jnp.concatenate(d_query, axis=1).astype(BF16)


def encoded_back_kernel(
    s_ref,
    d_scores_ref,
    probs_ref,
    q0,
    q1,
    q2,
    q3,
    key_w_ref,
    val_w_ref,
    enc_out_ref,
    enc_probs_ref,
    enc_queries_ref,
    cond_ref,
    d_cond_ref,
    query_ref,
    d_ctx_ref,
    total_ref,
):
    step = pl.program_id(0)
    width = total_ref.shape[1]
    pick((q0, q1, q2, q3), query_ref, d_ctx_ref)
    d_keys = dot(d_scores_ref[0], query_ref[...], COLS_T).astype(BF16)
    d_vals = dot(probs_ref[0], d_ctx_ref[...], COLS_T).astype(BF16)
    term = dot(d_keys, key_w_ref[...].reshape(width, -1), ROWS_T)
    term = term + dot(d_vals, val_w_ref[...].reshape(width, -1), ROWS_T)
    term = term.astype(BF16).astype(F32)

    @pl.when(step == 0)
    def _():
        total_ref[...] = term

    @pl.when(step > 0)
    def _():
        total_ref[...] += term

    @pl.when(step == pl.num_programs(0) - 1)
    def _():
        length = cond_ref.shape[0]
        d_att = dot(total_ref[...].astype(BF16), enc_out_ref[...], ROWS_T).astype(BF16)
        probs = enc_probs_ref[...]
        d_probs = dot(by_heads(cond_ref[:, width:], ENC_HEAD_DIM), d_att, ROWS_T)
        weighted = probs * d_probs
        sums = jnp.sum(weighted.reshape(-1, length, weighted.shape[1]), axis=1, keepdims=True)
        spread_sums = (probs.reshape(-1, length, probs.shape[1]) * sums).reshape(probs.shape)
        d_scores = (weighted - spread_sums) * ENC_SCALING
        live = live_columns(s_ref[1], probs.shape)
        d_scores = jnp.where(live, d_scores, 0.0).astype(BF16)
        low = jnp.where(live, probs, 0.0).astype(BF16)
        d_keys = head_blocks(dot(d_scores, enc_queries_ref[...]), length, ENC_HEAD_DIM)
        d_vals = head_blocks(dot(low, d_att), length, ENC_HEAD_DIM)
        d_cond_ref[...] = jnp.concatenate(d_keys + d_vals, axis=1).astype(BF16)


def placed_rows(rows, by, shift):
    moved = pltpu.roll(rows, by, 0)
    if shift == 0:
        return moved
    index = lax.broadcasted_iota(jnp.int32, rows.shape, 0)
    return jnp.where(index >= shift, moved, 0.0)


def outputs_kernel(
    shift,
    s_ref,
    c0,
    c1,
    c2,
    c3,
    out_w_ref,
    query_w_ref,
    hidden_ref,
    cotangent_ref,
    mixed_ref,
    grad_ref,
    mixed_sum_ref,
    grad_sum_ref,
):
    step = pl.program_id(0)
    half = out_w_ref.shape[2] // 2
    wide = out_w_ref.shape[3]
    length = c0.shape[1]
    parts = (c0, c1, c2, c3)
    ctx = jnp.concatenate([ref[0] for ref in parts], axis=0)
    d_query = jnp.concatenate([ref[1] for ref in parts], axis=0)

    @pl.when(step == 0)
    def _():
        mixed_sum_ref[...] = jnp.zeros_like(mixed_sum_ref)
        grad_sum_ref[...] = jnp.zeros_like(grad_sum_ref)

    for side in range(2):
        weight = out_w_ref[:, :, side * half : (side + 1) * half, :].reshape(-1, wide)
        mixed_sum_ref[:, side * wide : (side + 1) * wide] += dot(ctx, weight)
    grad_sum_ref[...] += dot(d_query, query_w_ref[...].reshape(-1, wide), ROWS_T)

    @pl.when(step == pl.num_programs(0) - 1)
    def _():
        by = (s_ref[0] * length + shift) % mixed_ref.shape[0]
        moved = placed_rows(mixed_sum_ref[...], by, shift)
        mixed_ref[...] = (hidden_ref[...].astype(F32) + moved).astype(mixed_ref.dtype)
        moved = placed_rows(grad_sum_ref[...], by, shift)
        grad_ref[...] = cotangent_ref[...].astype(F32) + moved


def shards(
    hidden,
    cotangent,
    counts,
    slot_of,
    neighbours,
    query_weight,
    key_weight,
    value_weight,
    out_weight,
    cond_weight,
    enc_query,
    enc_out,
):
    tokens, part_width = hidden.shape
    head_width = query_weight.shape[1]
    blocks = counts.shape[1]
    slots_per = slot_of.shape[2]
    item_total = blocks * slots_per
    slot_total, quarter, enc_width = neighbours.shape
    block_len = tokens // blocks
    shift = block_len - 1
    n_tensor = lax.axis_size("tensor")
    n_dp = lax.axis_size("dp")
    here = lax.axis_index("tensor")
    row = lax.axis_index("dp")
    all_width = head_width * n_tensor
    rows = slots_per * quarter * n_tensor
    enc_rows = enc_width // ENC_HEAD_DIM * block_len
    head_rows = head_width // HEAD_DIM * block_len
    sds = jax.ShapeDtypeStruct

    seq_counts = counts[0]
    count = lax.dynamic_slice_in_dim(seq_counts, here, 1, 0)
    scalars = jnp.concatenate([here.astype(jnp.int32)[None], count])

    wq_part = lax.dynamic_slice_in_dim(
        query_weight.reshape(n_tensor, part_width, head_width), row * SLICE, SLICE, 1
    )
    wo_part = lax.dynamic_slice_in_dim(out_weight, row * (SLICE // 2), SLICE // 2, 0)
    wo_part = wo_part.reshape(SLICE // 2, n_tensor, 2, head_width).transpose(1, 2, 0, 3)
    wo_part = wo_part.reshape(n_tensor, SLICE, head_width)
    kv_rows = 2 * enc_width // n_dp
    kv_part = jnp.where(
        row < n_dp // 2,
        lax.dynamic_slice_in_dim(key_weight, row % (n_dp // 2) * kv_rows, kv_rows, 0),
        lax.dynamic_slice_in_dim(value_weight, row % (n_dp // 2) * kv_rows, kv_rows, 0),
    )
    kv_part = jnp.broadcast_to(kv_part[None], (n_tensor, kv_rows, head_width))
    weight_parts = exchange(jnp.concatenate([wq_part, wo_part, kv_part], axis=1), here)
    qo_parts = jnp.stack([part[: 2 * SLICE] for part in weight_parts])
    kv_parts = jnp.stack([part[2 * SLICE :] for part in weight_parts])
    hidden_parts = spread_halves(hidden)
    cot_parts = spread_ring(cotangent)

    def kv_spec(index):
        return pl.BlockSpec((n_dp // 2, 1, kv_rows, head_width), lambda g, s: (index, g, 0, 0))

    def weight_spec(index):
        return pl.BlockSpec((n_dp, 1, SLICE, head_width), lambda g, s: (0, g, index, 0))

    c_spec = whole(block_len, 2 * enc_width)
    own_cond, *to_send = call(
        cond_kernel,
        "cond",
        1,
        [whole(tokens, part_width), whole(part_width, 2 * enc_width)],
        (c_spec,) * 4,
        (sds((block_len, 2 * enc_width), BF16),) * 4,
        [pltpu.VMEM((tokens, 2 * enc_width), F32)],
        20,
    )(scalars, hidden, cond_weight)
    ahead = (hidden_parts[1], hidden_parts[6], own_cond)
    kv_all = lax.all_gather(after(kv_parts, ahead), "dp", axis=0)
    cond_parts = [own_cond] + [
        lax.ppermute(array, "tensor", [(i, (i - k) % n_tensor) for i in range(n_tensor)])
        for k, array in enumerate(to_send, 1)
    ]

    def projected(parts, counts, weight, dims, weight_block, weight_map, name, vmem, before=None):
        full = whole(tokens, head_width)
        if before is None:
            out_specs, out_shape = full, sds((tokens, head_width), BF16)
        else:
            out_specs = (whole(2, block_len, head_width),) * n_tensor
            out_shape = (sds((2, block_len, head_width), BF16),) * n_tensor
        return call(
            functools.partial(project_kernel, dims, shift, counts),
            name,
            n_tensor,
            [whole(*part.shape) for part in parts]
            + [pl.BlockSpec(weight_block, weight_map)]
            + ([] if before is None else [full]),
            out_specs,
            out_shape,
            [pltpu.VMEM((tokens, head_width), F32)],
            vmem,
        )(scalars, *parts, weight, *([] if before is None else [before]))

    query = projected(
        hidden_parts,
        (1, 2, 2, 2),
        query_weight,
        PLAIN,
        (part_width, head_width),
        lambda g, s: ((s[0] + g) % 4, 0),
        "query",
        60,
    )

    live = jnp.arange(slots_per)[None, :] < after(seq_counts, (query, cot_parts[1:], cond_parts[1:]))[:, None]
    slot_flat = slot_of.reshape(item_total)
    matches = (jnp.arange(slot_total)[:, None] == slot_flat[None, :]) & live.reshape(item_total)[
        None, :
    ]
    returned = lax.all_to_all(neighbours, "dp", split_axis=0, concat_axis=0, tiled=True)
    items = jnp.einsum(
        "si,sre->ire", matches.astype(BF16), returned, preferred_element_type=F32
    ).astype(BF16)
    items = items.reshape(blocks, slots_per * quarter, enc_width)
    x = lax.all_to_all(items, "tensor", split_axis=0, concat_axis=0, tiled=True)
    x = x.reshape(rows, enc_width)

    qo_all = lax.all_gather(after(qo_parts, items), "dp", axis=0)
    own_query, *to_send = projected(
        after(cot_parts, (items, cond_parts[1:])),
        (1, 1, 2, 1),
        out_weight,
        ROWS_T,
        (head_width, part_width),
        lambda g, s: (0, (s[0] + g) % 4),
        "d_ctx",
        16,
        before=query,
    )
    query_parts = [own_query] + [
        lax.ppermute(array, "tensor", [(i, (i - k) % n_tensor) for i in range(n_tensor)])
        for k, array in enumerate(to_send, 1)
    ]

    c_spec = whole(block_len, 2 * enc_width)
    w_spec = whole(enc_width, enc_width)
    r_spec = whole(rows, enc_width)
    p_spec = whole(enc_rows, rows)
    cond, enc_queries, enc_probs, encoded = call(
        encode_kernel,
        "encode",
        1,
        [r_spec] + [c_spec] * 4 + [w_spec] * 2,
        (c_spec, r_spec, p_spec, r_spec),
        (
            sds((block_len, 2 * enc_width), BF16),
            sds((rows, enc_width), BF16),
            sds((enc_rows, rows), F32),
            sds((rows, enc_width), BF16),
        ),
        [],
        60,
    )(scalars, x, *cond_parts, enc_query, enc_out)

    q_spec = whole(2, block_len, head_width)
    big = pltpu.VMEM((head_rows, head_width), BF16)
    both_spec = pl.BlockSpec((2, block_len, head_width), lambda g, s: (0, 0, (s[0] + g) % 4))
    probs, d_scores, both = call(
        attention_kernel,
        "attention",
        n_tensor,
        [r_spec, kv_spec(0), kv_spec(1)] + [q_spec] * 4,
        (
            group(head_rows, rows),
            group(head_rows, rows),
            both_spec,
        ),
        (
            sds((n_tensor, head_rows, rows), BF16),
            sds((n_tensor, head_rows, rows), BF16),
            sds((2, block_len, all_width), BF16),
        ),
        [big, big],
        60,
    )(scalars, encoded, kv_all, kv_all, *query_parts)
    both_parts = spread(both, n_tensor)

    d_cond = call(
        encoded_back_kernel,
        "encoded_back",
        n_tensor,
        [group(head_rows, rows), group(head_rows, rows)]
        + [q_spec] * 4
        + [kv_spec(0), kv_spec(1), w_spec, p_spec, r_spec, c_spec],
        c_spec,
        sds((block_len, 2 * enc_width), BF16),
        [big, big, pltpu.VMEM((rows, enc_width), F32)],
        60,
    )(
        scalars,
        d_scores,
        probs,
        *query_parts,
        kv_all,
        kv_all,
        enc_out,
        enc_probs,
        enc_queries,
        cond,
    )
    d_cond_parts = spread(after(d_cond, both_parts[1]), n_tensor)

    out_spec = whole(tokens, part_width)
    acc = pltpu.VMEM((tokens, part_width), F32)
    mixed, from_query = call(
        functools.partial(outputs_kernel, shift),
        "outputs",
        n_tensor,
        [both_spec] * 4 + [weight_spec(1), weight_spec(0), out_spec, out_spec],
        (out_spec, out_spec),
        (sds((tokens, part_width), BF16), sds((tokens, part_width), F32)),
        [acc, acc],
        60,
    )(scalars, *both_parts, qo_all, qo_all, hidden, cotangent)
    d_cond_parts = after(d_cond_parts, from_query)
    d_cond_all = lax.dynamic_slice_in_dim(
        jnp.stack(d_cond_parts * 2), (n_tensor - here) % n_tensor, n_tensor, 0
    ).reshape(tokens, 2 * enc_width)
    grad_hidden = (from_query + dot(d_cond_all, cond_weight, ROWS_T)).astype(BF16)
    return (mixed, grad_hidden)


def solution(mesh):
    placed = (
        P("dp", "tensor"),
        P("dp", "tensor"),
        P("dp", None),
        P("dp", None, None),
        P("dp", "tensor", None),
        P(None, "tensor"),
        P(None, "tensor"),
        P(None, "tensor"),
        P("tensor", None),
        P("tensor", None),
        P(),
        P(),
    )
    return jax.shard_map(
        shards,
        mesh=mesh,
        in_specs=placed,
        out_specs=(P("dp", "tensor"), P("dp", "tensor")),
        check_vma=False,
    )
```

```python
import functools
import math

import jax
import jax.numpy as jnp
from jax import lax
from jax.experimental import pallas as pl
from jax.experimental.pallas import tpu as pltpu
from jax.sharding import PartitionSpec as P

HEAD_DIM = 128
ENC_HEAD_DIM = 128
F32 = jnp.float32
BF16 = jnp.bfloat16
PLAIN = (((1,), (0,)), ((), ()))
ROWS_T = (((1,), (1,)), ((), ()))
COLS_T = (((0,), (0,)), ((), ()))
SCALING = 1.0 / math.sqrt(HEAD_DIM)
ENC_SCALING = 1.0 / math.sqrt(ENC_HEAD_DIM)
SLICE = 32


def dot(a, b, dims=PLAIN):
    return lax.dot_general(a, b, dims, preferred_element_type=F32)


def call(kernel, name, grid, in_specs, out_specs, out_shape, scratch, vmem_mib):
    return pl.pallas_call(
        kernel,
        out_shape=out_shape,
        grid_spec=pltpu.PrefetchScalarGridSpec(
            num_scalar_prefetch=1,
            grid=(grid,),
            in_specs=in_specs,
            out_specs=out_specs,
            scratch_shapes=scratch,
        ),
        compiler_params=pltpu.CompilerParams(
            vmem_limit_bytes=vmem_mib * 1024 * 1024, dimension_semantics=("arbitrary",)
        ),
        name=name,
    )


def whole(*shape):
    return pl.BlockSpec(shape, lambda g, s: (0,) * len(shape))


def group(*shape):
    return pl.BlockSpec((1,) + shape, lambda g, s: (g,) + (0,) * len(shape))


def exchange(pieces, position, axis="tensor"):
    size = pieces.shape[0]
    out = [lax.dynamic_index_in_dim(pieces, position, 0, keepdims=False)]
    for k in range(1, size):
        piece = lax.dynamic_index_in_dim(pieces, (position - k) % size, 0, keepdims=False)
        out.append(lax.ppermute(piece, axis, [(i, (i - k) % size) for i in range(size)]))
    return out


def spread(shard, size, axis="tensor"):
    return [shard] + [
        lax.ppermute(shard, axis, [(i, (i - k) % size) for i in range(size)])
        for k in range(1, size)
    ]


def spread_ring(shard, axis="tensor"):
    down = [(i, (i - 1) % 4) for i in range(4)]
    up = [(i, (i + 1) % 4) for i in range(4)]
    half = shard.shape[0] // 2
    next_one = lax.ppermute(shard, axis, down)
    last_one = lax.ppermute(shard, axis, up)
    far_top = lax.ppermute(next_one[:half], axis, down)
    far_bottom = lax.ppermute(last_one[half:], axis, up)
    return [shard, next_one, far_top, far_bottom, last_one]


def spread_halves(shard, axis="tensor"):
    down = [(i, (i - 1) % 4) for i in range(4)]
    up = [(i, (i + 1) % 4) for i in range(4)]
    half = shard.shape[0] // 2
    top, bottom = shard[:half], shard[half:]
    next_top = lax.ppermute(top, axis, down)
    last_bottom = lax.ppermute(bottom, axis, up)
    next_bottom = lax.ppermute(bottom, axis, down)
    last_top = lax.ppermute(top, axis, up)
    far_top = lax.ppermute(next_top, axis, down)
    far_bottom = lax.ppermute(last_bottom, axis, up)
    return [shard, next_top, next_bottom, far_top, far_bottom, last_top, last_bottom]


def after(value, earlier):
    return lax.optimization_barrier((value, earlier))[0]


def live_columns(count, shape):
    column = lax.broadcasted_iota(jnp.int32, shape, len(shape) - 1)
    return (column // 32) % 4 < count


def by_heads(array, head_dim):
    head = lax.broadcasted_iota(jnp.int32, array.shape, 1) // head_dim
    zero = jnp.zeros_like(array)
    count = array.shape[1] // head_dim
    return jnp.concatenate([jnp.where(head == h, array, zero) for h in range(count)], axis=0)


def head_blocks(array, rows, head_dim):
    count = array.shape[1] // head_dim
    return [
        array[h * rows : (h + 1) * rows, h * head_dim : (h + 1) * head_dim] for h in range(count)
    ]


def cond_kernel(s_ref, hidden_ref, weight_ref, c0, c1, c2, c3, total_ref):
    length = c0.shape[0]
    total_ref[...] = dot(hidden_ref[...], weight_ref[...])
    for k, ref in enumerate((c0, c1, c2, c3)):
        start = pl.multiple_of(((s_ref[0] + 4 - k) % 4) * length, length)
        ref[...] = total_ref[pl.ds(start, length), :].astype(BF16)


def pick_kernel(slots_ref, stored_ref, out_ref, sems):
    blocks, length, _ = out_ref.shape
    tokens = stored_ref.shape[1]
    per = length // tokens
    copies = [
        pltpu.make_async_copy(
            stored_ref.at[slots_ref[item]],
            out_ref.at[item // per, pl.ds(item % per * tokens, tokens), :],
            sems.at[item],
        )
        for item in range(blocks * per)
    ]
    for copy in copies:
        copy.start()
    for copy in copies:
        copy.wait()


def project_kernel(dims, shift, counts, s_ref, *refs):
    total_ref = refs[-1]
    weight_ref = refs[sum(counts)]
    rest = refs[sum(counts) + 1 : -1]
    step = pl.program_id(0)
    for k, size in enumerate(counts):
        first = sum(counts[:k])
        parts = refs[first : first + size]

        @pl.when(step == k)
        def _(parts=parts, k=k):
            part = jnp.concatenate([ref[...] for ref in parts], axis=0)
            term = dot(part, weight_ref[...], dims)
            total_ref[...] = term if k == 0 else total_ref[...] + term

    @pl.when(step == pl.num_programs(0) - 1)
    def _():
        rows = total_ref.shape[0]
        moved = pltpu.roll(total_ref[...], rows - shift, 0)
        index = lax.broadcasted_iota(jnp.int32, moved.shape, 0)
        result = jnp.where(index < rows - shift, moved, 0.0)
        if len(rest) == 1:
            rest[0][...] = result.astype(BF16)
        else:
            total_ref[...] = result
            for k, ref in enumerate(rest[1:]):
                length = ref.shape[1]
                start = pl.multiple_of(((s_ref[0] + 4 - k) % 4) * length, length)
                ref[0] = rest[0][pl.ds(start, length), :]
                ref[1] = total_ref[pl.ds(start, length), :].astype(BF16)


def encode_kernel(
    s_ref,
    x_ref,
    c0,
    c1,
    c2,
    c3,
    enc_query_ref,
    enc_out_ref,
    cond_ref,
    queries_ref,
    probs_ref,
    encoded_ref,
):
    width = x_ref.shape[1]
    x = x_ref[...]
    cond = (c0[...].astype(F32) + c1[...].astype(F32)) + (
        c2[...].astype(F32) + c3[...].astype(F32)
    )
    cond = cond.astype(BF16)
    cond_ref[...] = cond
    length = cond.shape[0]
    queries = dot(x, enc_query_ref[...]).astype(BF16)
    queries_ref[...] = queries
    attended = []
    for head in range(width // ENC_HEAD_DIM):
        cols = slice(head * ENC_HEAD_DIM, (head + 1) * ENC_HEAD_DIM)
        vals = slice(width + head * ENC_HEAD_DIM, width + (head + 1) * ENC_HEAD_DIM)
        exponents = jnp.exp(dot(cond[:, cols], queries[:, cols], ROWS_T) * ENC_SCALING)
        probs = exponents / jnp.sum(exponents, axis=0, keepdims=True)
        probs_ref[head * length : (head + 1) * length, :] = probs
        attended.append(dot(probs.astype(BF16), cond[:, vals], COLS_T).astype(BF16))
    attended = jnp.concatenate(attended, axis=1)
    mixing = dot(attended, enc_out_ref[...])
    encoded_ref[...] = (x.astype(F32) + mixing).astype(BF16)


def pick(refs, query_ref, d_ctx_ref):
    for k, ref in enumerate(refs):

        @pl.when(pl.program_id(0) == k)
        def _(ref=ref):
            query_ref[...] = by_heads(ref[0], HEAD_DIM)
            d_ctx_ref[...] = by_heads(ref[1], HEAD_DIM)


def attention_kernel(
    s_ref,
    encoded_ref,
    key_w_ref,
    val_w_ref,
    q0,
    q1,
    q2,
    q3,
    probs_ref,
    d_scores_ref,
    out_ref,
    query_ref,
    d_ctx_ref,
):
    width = encoded_ref.shape[1]
    length = out_ref.shape[1]
    pick((q0, q1, q2, q3), query_ref, d_ctx_ref)
    encoded = encoded_ref[...]
    keys = dot(encoded, key_w_ref[...].reshape(width, -1)).astype(BF16)
    vals = dot(encoded, val_w_ref[...].reshape(width, -1)).astype(BF16)
    count = s_ref[1]
    scores = dot(query_ref[...], keys, ROWS_T) * SCALING
    expd = jnp.where(live_columns(count, scores.shape), jnp.exp(scores), 0.0)
    totals = jnp.sum(expd, axis=1, keepdims=True)
    probs = expd / jnp.where(count > 0, totals, 1.0)
    probs_low = probs.astype(BF16)
    probs_ref[0] = probs_low
    ctx = head_blocks(dot(probs_low, vals), length, HEAD_DIM)
    out_ref[0] = jnp.concatenate(ctx, axis=1).astype(BF16)
    weighted = probs * dot(d_ctx_ref[...], vals, ROWS_T)
    d_scores = (weighted - probs * jnp.sum(weighted, axis=1, keepdims=True)) * SCALING
    d_scores = d_scores.astype(BF16)
    d_scores_ref[0] = d_scores
    d_query = head_blocks(dot(d_scores, keys), length, HEAD_DIM)
    out_ref[1] = jnp.concatenate(d_query, axis=1).astype(BF16)


def encoded_back_kernel(
    s_ref,
    d_scores_ref,
    probs_ref,
    q0,
    q1,
    q2,
    q3,
    key_w_ref,
    val_w_ref,
    enc_out_ref,
    enc_probs_ref,
    enc_queries_ref,
    cond_ref,
    d_cond_ref,
    query_ref,
    d_ctx_ref,
    total_ref,
):
    step = pl.program_id(0)
    width = total_ref.shape[1]
    pick((q0, q1, q2, q3), query_ref, d_ctx_ref)
    d_keys = dot(d_scores_ref[0], query_ref[...], COLS_T).astype(BF16)
    d_vals = dot(probs_ref[0], d_ctx_ref[...], COLS_T).astype(BF16)
    term = dot(d_keys, key_w_ref[...].reshape(width, -1), ROWS_T)
    term = term + dot(d_vals, val_w_ref[...].reshape(width, -1), ROWS_T)
    term = term.astype(BF16).astype(F32)

    @pl.when(step == 0)
    def _():
        total_ref[...] = term

    @pl.when(step > 0)
    def _():
        total_ref[...] += term

    @pl.when(step == pl.num_programs(0) - 1)
    def _():
        length = cond_ref.shape[0]
        d_att = dot(total_ref[...].astype(BF16), enc_out_ref[...], ROWS_T).astype(BF16)
        probs = enc_probs_ref[...]
        d_probs = dot(by_heads(cond_ref[:, width:], ENC_HEAD_DIM), d_att, ROWS_T)
        weighted = probs * d_probs
        sums = jnp.sum(weighted.reshape(-1, length, weighted.shape[1]), axis=1, keepdims=True)
        spread_sums = (probs.reshape(-1, length, probs.shape[1]) * sums).reshape(probs.shape)
        d_scores = (weighted - spread_sums) * ENC_SCALING
        live = live_columns(s_ref[1], probs.shape)
        d_scores = jnp.where(live, d_scores, 0.0).astype(BF16)
        low = jnp.where(live, probs, 0.0).astype(BF16)
        d_keys = head_blocks(dot(d_scores, enc_queries_ref[...]), length, ENC_HEAD_DIM)
        d_vals = head_blocks(dot(low, d_att), length, ENC_HEAD_DIM)
        d_cond_ref[...] = jnp.concatenate(d_keys + d_vals, axis=1).astype(BF16)


def shifted_down(rows, shift):
    moved = pltpu.roll(rows, shift, 0)
    index = lax.broadcasted_iota(jnp.int32, rows.shape, 0)
    return jnp.where(index >= shift, moved, 0.0)


def outputs_kernel(
    shift,
    s_ref,
    c0,
    c1,
    c2,
    c3,
    out_w_ref,
    query_w_ref,
    hidden_ref,
    cotangent_ref,
    mixed_ref,
    grad_ref,
    rows_ref,
    mixed_sum_ref,
    grad_sum_ref,
):
    step = pl.program_id(0)
    half = out_w_ref.shape[2] // 2
    wide = out_w_ref.shape[3]
    length = c0.shape[1]
    for k, ref in enumerate((c0, c1, c2, c3)):
        start = pl.multiple_of(((s_ref[0] + k) % 4) * length, length)
        rows_ref[:, pl.ds(start, length), :] = ref[...]
    ctx = rows_ref[0]
    d_query = rows_ref[1]

    @pl.when(step == 0)
    def _():
        mixed_sum_ref[...] = jnp.zeros_like(mixed_sum_ref)
        grad_sum_ref[...] = jnp.zeros_like(grad_sum_ref)

    for side in range(2):
        weight = out_w_ref[:, :, side * half : (side + 1) * half, :].reshape(-1, wide)
        mixed_sum_ref[:, side * wide : (side + 1) * wide] += dot(ctx, weight)
    grad_sum_ref[...] += dot(d_query, query_w_ref[...].reshape(-1, wide), ROWS_T)

    @pl.when(step == pl.num_programs(0) - 1)
    def _():
        moved = shifted_down(mixed_sum_ref[...], shift)
        mixed_ref[...] = (hidden_ref[...].astype(F32) + moved).astype(mixed_ref.dtype)
        moved = shifted_down(grad_sum_ref[...], shift)
        grad_ref[...] = cotangent_ref[...].astype(F32) + moved


def shards(
    hidden,
    cotangent,
    counts,
    slot_of,
    neighbours,
    query_weight,
    key_weight,
    value_weight,
    out_weight,
    cond_weight,
    enc_query,
    enc_out,
):
    tokens, part_width = hidden.shape
    head_width = query_weight.shape[1]
    blocks = counts.shape[1]
    slots_per = slot_of.shape[2]
    item_total = blocks * slots_per
    slot_total, quarter, enc_width = neighbours.shape
    block_len = tokens // blocks
    shift = block_len - 1
    n_tensor = lax.axis_size("tensor")
    n_dp = lax.axis_size("dp")
    here = lax.axis_index("tensor")
    row = lax.axis_index("dp")
    all_width = head_width * n_tensor
    rows = slots_per * quarter * n_tensor
    enc_rows = enc_width // ENC_HEAD_DIM * block_len
    head_rows = head_width // HEAD_DIM * block_len
    sds = jax.ShapeDtypeStruct

    seq_counts = counts[0]
    count = lax.dynamic_slice_in_dim(seq_counts, here, 1, 0)
    scalars = jnp.concatenate([here.astype(jnp.int32)[None], count])

    wq_part = lax.dynamic_slice_in_dim(
        query_weight.reshape(n_tensor, part_width, head_width), row * SLICE, SLICE, 1
    )
    wo_part = lax.dynamic_slice_in_dim(out_weight, row * (SLICE // 2), SLICE // 2, 0)
    wo_part = wo_part.reshape(SLICE // 2, n_tensor, 2, head_width).transpose(1, 2, 0, 3)
    wo_part = wo_part.reshape(n_tensor, SLICE, head_width)
    kv_rows = 2 * enc_width // n_dp
    kv_part = jnp.where(
        row < n_dp // 2,
        lax.dynamic_slice_in_dim(key_weight, row % (n_dp // 2) * kv_rows, kv_rows, 0),
        lax.dynamic_slice_in_dim(value_weight, row % (n_dp // 2) * kv_rows, kv_rows, 0),
    )
    kv_part = jnp.broadcast_to(kv_part[None], (n_tensor, kv_rows, head_width))
    weight_parts = exchange(jnp.concatenate([wq_part, wo_part, kv_part], axis=1), here)
    qo_parts = jnp.stack([part[: 2 * SLICE] for part in weight_parts])
    kv_parts = jnp.stack([part[2 * SLICE :] for part in weight_parts])
    hidden_parts = spread_halves(hidden)
    cot_parts = spread_ring(cotangent)

    def kv_spec(index):
        return pl.BlockSpec((n_dp // 2, 1, kv_rows, head_width), lambda g, s: (index, g, 0, 0))

    def weight_spec(index):
        return pl.BlockSpec((n_dp, 1, SLICE, head_width), lambda g, s: (0, g, index, 0))

    c_spec = whole(block_len, 2 * enc_width)
    own_cond, *to_send = call(
        cond_kernel,
        "cond",
        1,
        [whole(tokens, part_width), whole(part_width, 2 * enc_width)],
        (c_spec,) * 4,
        (sds((block_len, 2 * enc_width), BF16),) * 4,
        [pltpu.VMEM((tokens, 2 * enc_width), F32)],
        20,
    )(scalars, hidden, cond_weight)
    ahead = (hidden_parts[1], hidden_parts[6], own_cond)
    kv_all = lax.all_gather(after(kv_parts, ahead), "dp", axis=0)
    cond_parts = [own_cond] + [
        lax.ppermute(array, "tensor", [(i, (i - k) % n_tensor) for i in range(n_tensor)])
        for k, array in enumerate(to_send, 1)
    ]

    def projected(parts, counts, weight, dims, weight_block, weight_map, name, vmem, before=None):
        full = whole(tokens, head_width)
        if before is None:
            out_specs, out_shape = full, sds((tokens, head_width), BF16)
        else:
            out_specs = (whole(2, block_len, head_width),) * n_tensor
            out_shape = (sds((2, block_len, head_width), BF16),) * n_tensor
        return call(
            functools.partial(project_kernel, dims, shift, counts),
            name,
            n_tensor,
            [whole(*part.shape) for part in parts]
            + [pl.BlockSpec(weight_block, weight_map)]
            + ([] if before is None else [full]),
            out_specs,
            out_shape,
            [pltpu.VMEM((tokens, head_width), F32)],
            vmem,
        )(scalars, *parts, weight, *([] if before is None else [before]))

    query = projected(
        hidden_parts,
        (1, 2, 2, 2),
        query_weight,
        PLAIN,
        (part_width, head_width),
        lambda g, s: ((s[0] + g) % 4, 0),
        "query",
        60,
    )

    slots = after(slot_of.reshape(item_total), (query, cot_parts[1:], cond_parts[1:]))
    returned = lax.all_to_all(neighbours, "dp", split_axis=0, concat_axis=0, tiled=True)
    anywhere = pl.BlockSpec(memory_space=pl.ANY)
    items = call(
        pick_kernel,
        "pick",
        1,
        [anywhere],
        anywhere,
        sds((blocks, slots_per * quarter, enc_width), BF16),
        [pltpu.SemaphoreType.DMA((item_total,))],
        16,
    )(slots, returned)
    x = lax.all_to_all(items, "tensor", split_axis=0, concat_axis=0, tiled=True)
    x = x.reshape(rows, enc_width)

    qo_all = lax.all_gather(after(qo_parts, items), "dp", axis=0)
    own_query, *to_send = projected(
        after(cot_parts, (items, cond_parts[1:])),
        (1, 1, 2, 1),
        out_weight,
        ROWS_T,
        (head_width, part_width),
        lambda g, s: (0, (s[0] + g) % 4),
        "d_ctx",
        16,
        before=query,
    )
    query_parts = [own_query] + [
        lax.ppermute(array, "tensor", [(i, (i - k) % n_tensor) for i in range(n_tensor)])
        for k, array in enumerate(to_send, 1)
    ]

    c_spec = whole(block_len, 2 * enc_width)
    w_spec = whole(enc_width, enc_width)
    r_spec = whole(rows, enc_width)
    p_spec = whole(enc_rows, rows)
    cond, enc_queries, enc_probs, encoded = call(
        encode_kernel,
        "encode",
        1,
        [r_spec] + [c_spec] * 4 + [w_spec] * 2,
        (c_spec, r_spec, p_spec, r_spec),
        (
            sds((block_len, 2 * enc_width), BF16),
            sds((rows, enc_width), BF16),
            sds((enc_rows, rows), F32),
            sds((rows, enc_width), BF16),
        ),
        [],
        60,
    )(scalars, x, *cond_parts, enc_query, enc_out)

    q_spec = whole(2, block_len, head_width)
    big = pltpu.VMEM((head_rows, head_width), BF16)
    both_spec = pl.BlockSpec((2, block_len, head_width), lambda g, s: (0, 0, (s[0] + g) % 4))
    probs, d_scores, both = call(
        attention_kernel,
        "attention",
        n_tensor,
        [r_spec, kv_spec(0), kv_spec(1)] + [q_spec] * 4,
        (
            group(head_rows, rows),
            group(head_rows, rows),
            both_spec,
        ),
        (
            sds((n_tensor, head_rows, rows), BF16),
            sds((n_tensor, head_rows, rows), BF16),
            sds((2, block_len, all_width), BF16),
        ),
        [big, big],
        60,
    )(scalars, encoded, kv_all, kv_all, *query_parts)
    both_parts = spread(both, n_tensor)

    d_cond = call(
        encoded_back_kernel,
        "encoded_back",
        n_tensor,
        [group(head_rows, rows), group(head_rows, rows)]
        + [q_spec] * 4
        + [kv_spec(0), kv_spec(1), w_spec, p_spec, r_spec, c_spec],
        c_spec,
        sds((block_len, 2 * enc_width), BF16),
        [big, big, pltpu.VMEM((rows, enc_width), F32)],
        60,
    )(
        scalars,
        d_scores,
        probs,
        *query_parts,
        kv_all,
        kv_all,
        enc_out,
        enc_probs,
        enc_queries,
        cond,
    )
    d_cond_parts = spread(after(d_cond, both_parts[1]), n_tensor)

    out_spec = whole(tokens, part_width)
    acc = pltpu.VMEM((tokens, part_width), F32)
    mixed, from_query = call(
        functools.partial(outputs_kernel, shift),
        "outputs",
        n_tensor,
        [both_spec] * 4 + [weight_spec(1), weight_spec(0), out_spec, out_spec],
        (out_spec, out_spec),
        (sds((tokens, part_width), BF16), sds((tokens, part_width), F32)),
        [pltpu.VMEM((2, tokens, head_width), BF16), acc, acc],
        60,
    )(scalars, *both_parts, qo_all, qo_all, hidden, cotangent)
    d_cond_parts = after(d_cond_parts, from_query)
    d_cond_all = lax.dynamic_slice_in_dim(
        jnp.stack(d_cond_parts * 2), (n_tensor - here) % n_tensor, n_tensor, 0
    ).reshape(tokens, 2 * enc_width)
    grad_hidden = (from_query + dot(d_cond_all, cond_weight, ROWS_T)).astype(BF16)
    return (mixed, grad_hidden)


def solution(mesh):
    placed = (
        P("dp", "tensor"),
        P("dp", "tensor"),
        P("dp", None),
        P("dp", None, None),
        P("dp", "tensor", None),
        P(None, "tensor"),
        P(None, "tensor"),
        P(None, "tensor"),
        P("tensor", None),
        P("tensor", None),
        P(),
        P(),
    )
    return jax.shard_map(
        shards,
        mesh=mesh,
        in_specs=placed,
        out_specs=(P("dp", "tensor"), P("dp", "tensor")),
        check_vma=False,
    )
```

```python
import functools
import math

import jax
import jax.numpy as jnp
from jax import lax
from jax.experimental import pallas as pl
from jax.experimental.pallas import tpu as pltpu
from jax.sharding import PartitionSpec as P

HEAD_DIM = 128
ENC_HEAD_DIM = 128
F32 = jnp.float32
BF16 = jnp.bfloat16
PLAIN = (((1,), (0,)), ((), ()))
ROWS_T = (((1,), (1,)), ((), ()))
COLS_T = (((0,), (0,)), ((), ()))
SCALING = 1.0 / math.sqrt(HEAD_DIM)
ENC_SCALING = 1.0 / math.sqrt(ENC_HEAD_DIM)
SLICE = 32


def dot(a, b, dims=PLAIN):
    return lax.dot_general(a, b, dims, preferred_element_type=F32)


def call(kernel, name, grid, in_specs, out_specs, out_shape, scratch, vmem_mib):
    return pl.pallas_call(
        kernel,
        out_shape=out_shape,
        grid_spec=pltpu.PrefetchScalarGridSpec(
            num_scalar_prefetch=1,
            grid=(grid,),
            in_specs=in_specs,
            out_specs=out_specs,
            scratch_shapes=scratch,
        ),
        compiler_params=pltpu.CompilerParams(
            vmem_limit_bytes=vmem_mib * 1024 * 1024, dimension_semantics=("arbitrary",)
        ),
        name=name,
    )


def whole(*shape):
    return pl.BlockSpec(shape, lambda g, s: (0,) * len(shape))


def group(*shape):
    return pl.BlockSpec((1,) + shape, lambda g, s: (g,) + (0,) * len(shape))


def exchange(pieces, position, axis="tensor"):
    size = pieces.shape[0]
    out = [lax.dynamic_index_in_dim(pieces, position, 0, keepdims=False)]
    for k in range(1, size):
        piece = lax.dynamic_index_in_dim(pieces, (position - k) % size, 0, keepdims=False)
        out.append(lax.ppermute(piece, axis, [(i, (i - k) % size) for i in range(size)]))
    return out


def spread(shard, size, axis="tensor"):
    return [shard] + [
        lax.ppermute(shard, axis, [(i, (i - k) % size) for i in range(size)])
        for k in range(1, size)
    ]


def spread_ring(shard, axis="tensor"):
    down = [(i, (i - 1) % 4) for i in range(4)]
    up = [(i, (i + 1) % 4) for i in range(4)]
    half = shard.shape[0] // 2
    next_one = lax.ppermute(shard, axis, down)
    last_one = lax.ppermute(shard, axis, up)
    far_top = lax.ppermute(next_one[:half], axis, down)
    far_bottom = lax.ppermute(last_one[half:], axis, up)
    return [shard, next_one, far_top, far_bottom, last_one]


def spread_halves(shard, axis="tensor"):
    down = [(i, (i - 1) % 4) for i in range(4)]
    up = [(i, (i + 1) % 4) for i in range(4)]
    half = shard.shape[0] // 2
    top, bottom = shard[:half], shard[half:]
    next_top = lax.ppermute(top, axis, down)
    last_bottom = lax.ppermute(bottom, axis, up)
    next_bottom = lax.ppermute(bottom, axis, down)
    last_top = lax.ppermute(top, axis, up)
    far_top = lax.ppermute(next_top, axis, down)
    far_bottom = lax.ppermute(last_bottom, axis, up)
    return [shard, next_top, next_bottom, far_top, far_bottom, last_top, last_bottom]


def after(value, earlier):
    return lax.optimization_barrier((value, earlier))[0]


def live_columns(count, shape):
    column = lax.broadcasted_iota(jnp.int32, shape, len(shape) - 1)
    return (column // 32) % 4 < count


def by_heads(array, head_dim):
    head = lax.broadcasted_iota(jnp.int32, array.shape, 1) // head_dim
    zero = jnp.zeros_like(array)
    count = array.shape[1] // head_dim
    return jnp.concatenate([jnp.where(head == h, array, zero) for h in range(count)], axis=0)


def head_blocks(array, rows, head_dim):
    count = array.shape[1] // head_dim
    return [
        array[h * rows : (h + 1) * rows, h * head_dim : (h + 1) * head_dim] for h in range(count)
    ]


def cond_kernel(s_ref, hidden_ref, weight_ref, c0, c1, c2, c3, total_ref):
    length = c0.shape[0]
    total_ref[...] = dot(hidden_ref[...], weight_ref[...])
    for k, ref in enumerate((c0, c1, c2, c3)):
        start = pl.multiple_of(((s_ref[0] + 4 - k) % 4) * length, length)
        ref[...] = total_ref[pl.ds(start, length), :].astype(BF16)


def project_kernel(dims, shift, counts, s_ref, *refs):
    total_ref = refs[-1]
    weight_ref = refs[sum(counts)]
    rest = refs[sum(counts) + 1 : -1]
    step = pl.program_id(0)
    for k, size in enumerate(counts):
        first = sum(counts[:k])
        parts = refs[first : first + size]

        @pl.when(step == k)
        def _(parts=parts, k=k):
            part = jnp.concatenate([ref[...] for ref in parts], axis=0)
            term = dot(part, weight_ref[...], dims)
            total_ref[...] = term if k == 0 else total_ref[...] + term

    @pl.when(step == pl.num_programs(0) - 1)
    def _():
        rows = total_ref.shape[0]
        moved = pltpu.roll(total_ref[...], rows - shift, 0)
        index = lax.broadcasted_iota(jnp.int32, moved.shape, 0)
        result = jnp.where(index < rows - shift, moved, 0.0)
        if len(rest) == 1:
            rest[0][...] = result.astype(BF16)
        else:
            total_ref[...] = result
            for k, ref in enumerate(rest[1:]):
                length = ref.shape[1]
                start = pl.multiple_of(((s_ref[0] + 4 - k) % 4) * length, length)
                ref[0] = rest[0][pl.ds(start, length), :]
                ref[1] = total_ref[pl.ds(start, length), :].astype(BF16)


def encode_kernel(
    s_ref,
    x_ref,
    c0,
    c1,
    c2,
    c3,
    enc_query_ref,
    enc_out_ref,
    cond_ref,
    queries_ref,
    probs_ref,
    encoded_ref,
):
    width = x_ref.shape[1]
    x = x_ref[...]
    cond = (c0[...].astype(F32) + c1[...].astype(F32)) + (
        c2[...].astype(F32) + c3[...].astype(F32)
    )
    cond = cond.astype(BF16)
    cond_ref[...] = cond
    length = cond.shape[0]
    queries = dot(x, enc_query_ref[...]).astype(BF16)
    queries_ref[...] = queries
    attended = []
    for head in range(width // ENC_HEAD_DIM):
        cols = slice(head * ENC_HEAD_DIM, (head + 1) * ENC_HEAD_DIM)
        vals = slice(width + head * ENC_HEAD_DIM, width + (head + 1) * ENC_HEAD_DIM)
        exponents = jnp.exp(dot(cond[:, cols], queries[:, cols], ROWS_T) * ENC_SCALING)
        probs = exponents / jnp.sum(exponents, axis=0, keepdims=True)
        probs_ref[head * length : (head + 1) * length, :] = probs
        attended.append(dot(probs.astype(BF16), cond[:, vals], COLS_T).astype(BF16))
    attended = jnp.concatenate(attended, axis=1)
    mixing = dot(attended, enc_out_ref[...])
    encoded_ref[...] = (x.astype(F32) + mixing).astype(BF16)


def pick(refs, query_ref, d_ctx_ref):
    for k, ref in enumerate(refs):

        @pl.when(pl.program_id(0) == k)
        def _(ref=ref):
            query_ref[...] = by_heads(ref[0], HEAD_DIM)
            d_ctx_ref[...] = by_heads(ref[1], HEAD_DIM)


def attention_kernel(
    s_ref,
    encoded_ref,
    key_w_ref,
    val_w_ref,
    q0,
    q1,
    q2,
    q3,
    probs_ref,
    d_scores_ref,
    out_ref,
    query_ref,
    d_ctx_ref,
):
    width = encoded_ref.shape[1]
    length = out_ref.shape[1]
    pick((q0, q1, q2, q3), query_ref, d_ctx_ref)
    encoded = encoded_ref[...]
    keys = dot(encoded, key_w_ref[...].reshape(width, -1)).astype(BF16)
    vals = dot(encoded, val_w_ref[...].reshape(width, -1)).astype(BF16)
    count = s_ref[1]
    scores = dot(query_ref[...], keys, ROWS_T) * SCALING
    expd = jnp.where(live_columns(count, scores.shape), jnp.exp(scores), 0.0)
    totals = jnp.sum(expd, axis=1, keepdims=True)
    probs = expd / jnp.where(count > 0, totals, 1.0)
    probs_low = probs.astype(BF16)
    probs_ref[0] = probs_low
    ctx = head_blocks(dot(probs_low, vals), length, HEAD_DIM)
    out_ref[0] = jnp.concatenate(ctx, axis=1).astype(BF16)
    weighted = probs * dot(d_ctx_ref[...], vals, ROWS_T)
    d_scores = (weighted - probs * jnp.sum(weighted, axis=1, keepdims=True)) * SCALING
    d_scores = d_scores.astype(BF16)
    d_scores_ref[0] = d_scores
    d_query = head_blocks(dot(d_scores, keys), length, HEAD_DIM)
    out_ref[1] = jnp.concatenate(d_query, axis=1).astype(BF16)


def encoded_back_kernel(
    s_ref,
    d_scores_ref,
    probs_ref,
    q0,
    q1,
    q2,
    q3,
    key_w_ref,
    val_w_ref,
    enc_out_ref,
    enc_probs_ref,
    enc_queries_ref,
    cond_ref,
    d_cond_ref,
    query_ref,
    d_ctx_ref,
    total_ref,
):
    step = pl.program_id(0)
    width = total_ref.shape[1]
    pick((q0, q1, q2, q3), query_ref, d_ctx_ref)
    d_keys = dot(d_scores_ref[0], query_ref[...], COLS_T).astype(BF16)
    d_vals = dot(probs_ref[0], d_ctx_ref[...], COLS_T).astype(BF16)
    term = dot(d_keys, key_w_ref[...].reshape(width, -1), ROWS_T)
    term = term + dot(d_vals, val_w_ref[...].reshape(width, -1), ROWS_T)
    term = term.astype(BF16).astype(F32)

    @pl.when(step == 0)
    def _():
        total_ref[...] = term

    @pl.when(step > 0)
    def _():
        total_ref[...] += term

    @pl.when(step == pl.num_programs(0) - 1)
    def _():
        length = cond_ref.shape[0]
        d_att = dot(total_ref[...].astype(BF16), enc_out_ref[...], ROWS_T).astype(BF16)
        probs = enc_probs_ref[...]
        d_probs = dot(by_heads(cond_ref[:, width:], ENC_HEAD_DIM), d_att, ROWS_T)
        weighted = probs * d_probs
        sums = jnp.sum(weighted.reshape(-1, length, weighted.shape[1]), axis=1, keepdims=True)
        spread_sums = (probs.reshape(-1, length, probs.shape[1]) * sums).reshape(probs.shape)
        d_scores = (weighted - spread_sums) * ENC_SCALING
        live = live_columns(s_ref[1], probs.shape)
        d_scores = jnp.where(live, d_scores, 0.0).astype(BF16)
        low = jnp.where(live, probs, 0.0).astype(BF16)
        d_keys = head_blocks(dot(d_scores, enc_queries_ref[...]), length, ENC_HEAD_DIM)
        d_vals = head_blocks(dot(low, d_att), length, ENC_HEAD_DIM)
        d_cond_ref[...] = jnp.concatenate(d_keys + d_vals, axis=1).astype(BF16)


def shifted_down(rows, shift):
    moved = pltpu.roll(rows, shift, 0)
    index = lax.broadcasted_iota(jnp.int32, rows.shape, 0)
    return jnp.where(index >= shift, moved, 0.0)


def outputs_kernel(
    shift,
    s_ref,
    c0,
    c1,
    c2,
    c3,
    out_w_ref,
    query_w_ref,
    hidden_ref,
    cotangent_ref,
    mixed_ref,
    grad_ref,
    rows_ref,
    mixed_sum_ref,
    grad_sum_ref,
):
    step = pl.program_id(0)
    half = out_w_ref.shape[2] // 2
    wide = out_w_ref.shape[3]
    length = c0.shape[1]
    for k, ref in enumerate((c0, c1, c2, c3)):
        start = pl.multiple_of(((s_ref[0] + k) % 4) * length, length)
        rows_ref[:, pl.ds(start, length), :] = ref[...]
    ctx = rows_ref[0]
    d_query = rows_ref[1]

    @pl.when(step == 0)
    def _():
        mixed_sum_ref[...] = jnp.zeros_like(mixed_sum_ref)
        grad_sum_ref[...] = jnp.zeros_like(grad_sum_ref)

    for side in range(2):
        weight = out_w_ref[:, :, side * half : (side + 1) * half, :].reshape(-1, wide)
        mixed_sum_ref[:, side * wide : (side + 1) * wide] += dot(ctx, weight)
    grad_sum_ref[...] += dot(d_query, query_w_ref[...].reshape(-1, wide), ROWS_T)

    @pl.when(step == pl.num_programs(0) - 1)
    def _():
        moved = shifted_down(mixed_sum_ref[...], shift)
        mixed_ref[...] = (hidden_ref[...].astype(F32) + moved).astype(mixed_ref.dtype)
        moved = shifted_down(grad_sum_ref[...], shift)
        grad_ref[...] = cotangent_ref[...].astype(F32) + moved


def shards(
    hidden,
    cotangent,
    counts,
    slot_of,
    neighbours,
    query_weight,
    key_weight,
    value_weight,
    out_weight,
    cond_weight,
    enc_query,
    enc_out,
):
    tokens, part_width = hidden.shape
    head_width = query_weight.shape[1]
    blocks = counts.shape[1]
    slots_per = slot_of.shape[2]
    item_total = blocks * slots_per
    slot_total, quarter, enc_width = neighbours.shape
    block_len = tokens // blocks
    shift = block_len - 1
    n_tensor = lax.axis_size("tensor")
    n_dp = lax.axis_size("dp")
    here = lax.axis_index("tensor")
    row = lax.axis_index("dp")
    all_width = head_width * n_tensor
    rows = slots_per * quarter * n_tensor
    enc_rows = enc_width // ENC_HEAD_DIM * block_len
    head_rows = head_width // HEAD_DIM * block_len
    sds = jax.ShapeDtypeStruct

    seq_counts = counts[0]
    count = lax.dynamic_slice_in_dim(seq_counts, here, 1, 0)
    scalars = jnp.concatenate([here.astype(jnp.int32)[None], count])

    wq_part = lax.dynamic_slice_in_dim(
        query_weight.reshape(n_tensor, part_width, head_width), row * SLICE, SLICE, 1
    )
    wo_part = lax.dynamic_slice_in_dim(out_weight, row * (SLICE // 2), SLICE // 2, 0)
    wo_part = wo_part.reshape(SLICE // 2, n_tensor, 2, head_width).transpose(1, 2, 0, 3)
    wo_part = wo_part.reshape(n_tensor, SLICE, head_width)
    kv_rows = 2 * enc_width // n_dp
    kv_part = jnp.where(
        row < n_dp // 2,
        lax.dynamic_slice_in_dim(key_weight, row % (n_dp // 2) * kv_rows, kv_rows, 0),
        lax.dynamic_slice_in_dim(value_weight, row % (n_dp // 2) * kv_rows, kv_rows, 0),
    )
    kv_part = jnp.broadcast_to(kv_part[None], (n_tensor, kv_rows, head_width))
    weight_parts = exchange(jnp.concatenate([wq_part, wo_part, kv_part], axis=1), here)
    qo_parts = jnp.stack([part[: 2 * SLICE] for part in weight_parts])
    kv_parts = jnp.stack([part[2 * SLICE :] for part in weight_parts])
    hidden_parts = spread_halves(hidden)
    cot_parts = spread_ring(cotangent)

    def kv_spec(index):
        return pl.BlockSpec((n_dp // 2, 1, kv_rows, head_width), lambda g, s: (index, g, 0, 0))

    def weight_spec(index):
        return pl.BlockSpec((n_dp, 1, SLICE, head_width), lambda g, s: (0, g, index, 0))

    c_spec = whole(block_len, 2 * enc_width)
    own_cond, *to_send = call(
        cond_kernel,
        "cond",
        1,
        [whole(tokens, part_width), whole(part_width, 2 * enc_width)],
        (c_spec,) * 4,
        (sds((block_len, 2 * enc_width), BF16),) * 4,
        [pltpu.VMEM((tokens, 2 * enc_width), F32)],
        20,
    )(scalars, hidden, cond_weight)
    ahead = (hidden_parts[1], hidden_parts[6], own_cond)
    kv_all = lax.all_gather(after(kv_parts, ahead), "dp", axis=0)
    cond_parts = [own_cond] + [
        lax.ppermute(array, "tensor", [(i, (i - k) % n_tensor) for i in range(n_tensor)])
        for k, array in enumerate(to_send, 1)
    ]

    def projected(parts, counts, weight, dims, weight_block, weight_map, name, vmem, before=None):
        full = whole(tokens, head_width)
        if before is None:
            out_specs, out_shape = full, sds((tokens, head_width), BF16)
        else:
            out_specs = (whole(2, block_len, head_width),) * n_tensor
            out_shape = (sds((2, block_len, head_width), BF16),) * n_tensor
        return call(
            functools.partial(project_kernel, dims, shift, counts),
            name,
            n_tensor,
            [whole(*part.shape) for part in parts]
            + [pl.BlockSpec(weight_block, weight_map)]
            + ([] if before is None else [full]),
            out_specs,
            out_shape,
            [pltpu.VMEM((tokens, head_width), F32)],
            vmem,
        )(scalars, *parts, weight, *([] if before is None else [before]))

    query = projected(
        hidden_parts,
        (1, 2, 2, 2),
        query_weight,
        PLAIN,
        (part_width, head_width),
        lambda g, s: ((s[0] + g) % 4, 0),
        "query",
        60,
    )

    live = jnp.arange(slots_per)[None, :] < after(seq_counts, (query, cot_parts[1:], cond_parts[1:]))[:, None]
    slot_flat = slot_of.reshape(item_total)
    matches = (jnp.arange(slot_total)[:, None] == slot_flat[None, :]) & live.reshape(item_total)[
        None, :
    ]
    returned = lax.all_to_all(neighbours, "dp", split_axis=0, concat_axis=0, tiled=True)
    items = jnp.einsum(
        "si,sre->ire", matches.astype(BF16), returned, preferred_element_type=F32
    ).astype(BF16)
    items = items.reshape(blocks, slots_per * quarter, enc_width)
    x = lax.all_to_all(items, "tensor", split_axis=0, concat_axis=0, tiled=True)
    x = x.reshape(rows, enc_width)

    qo_all = lax.all_gather(after(qo_parts, items), "dp", axis=0)
    own_query, *to_send = projected(
        after(cot_parts, (items, cond_parts[1:])),
        (1, 1, 2, 1),
        out_weight,
        ROWS_T,
        (head_width, part_width),
        lambda g, s: (0, (s[0] + g) % 4),
        "d_ctx",
        16,
        before=query,
    )
    query_parts = [own_query] + [
        lax.ppermute(array, "tensor", [(i, (i - k) % n_tensor) for i in range(n_tensor)])
        for k, array in enumerate(to_send, 1)
    ]

    c_spec = whole(block_len, 2 * enc_width)
    w_spec = whole(enc_width, enc_width)
    r_spec = whole(rows, enc_width)
    p_spec = whole(enc_rows, rows)
    cond, enc_queries, enc_probs, encoded = call(
        encode_kernel,
        "encode",
        1,
        [r_spec] + [c_spec] * 4 + [w_spec] * 2,
        (c_spec, r_spec, p_spec, r_spec),
        (
            sds((block_len, 2 * enc_width), BF16),
            sds((rows, enc_width), BF16),
            sds((enc_rows, rows), F32),
            sds((rows, enc_width), BF16),
        ),
        [],
        60,
    )(scalars, x, *cond_parts, enc_query, enc_out)

    q_spec = whole(2, block_len, head_width)
    big = pltpu.VMEM((head_rows, head_width), BF16)
    both_spec = pl.BlockSpec((2, block_len, head_width), lambda g, s: (0, 0, (s[0] + g) % 4))
    probs, d_scores, both = call(
        attention_kernel,
        "attention",
        n_tensor,
        [r_spec, kv_spec(0), kv_spec(1)] + [q_spec] * 4,
        (
            group(head_rows, rows),
            group(head_rows, rows),
            both_spec,
        ),
        (
            sds((n_tensor, head_rows, rows), BF16),
            sds((n_tensor, head_rows, rows), BF16),
            sds((2, block_len, all_width), BF16),
        ),
        [big, big],
        60,
    )(scalars, encoded, kv_all, kv_all, *query_parts)
    both_parts = spread(both, n_tensor)

    d_cond = call(
        encoded_back_kernel,
        "encoded_back",
        n_tensor,
        [group(head_rows, rows), group(head_rows, rows)]
        + [q_spec] * 4
        + [kv_spec(0), kv_spec(1), w_spec, p_spec, r_spec, c_spec],
        c_spec,
        sds((block_len, 2 * enc_width), BF16),
        [big, big, pltpu.VMEM((rows, enc_width), F32)],
        60,
    )(
        scalars,
        d_scores,
        probs,
        *query_parts,
        kv_all,
        kv_all,
        enc_out,
        enc_probs,
        enc_queries,
        cond,
    )
    d_cond_parts = spread(after(d_cond, both_parts[1]), n_tensor)

    out_spec = whole(tokens, part_width)
    acc = pltpu.VMEM((tokens, part_width), F32)
    mixed, from_query = call(
        functools.partial(outputs_kernel, shift),
        "outputs",
        n_tensor,
        [both_spec] * 4 + [weight_spec(1), weight_spec(0), out_spec, out_spec],
        (out_spec, out_spec),
        (sds((tokens, part_width), BF16), sds((tokens, part_width), F32)),
        [pltpu.VMEM((2, tokens, head_width), BF16), acc, acc],
        60,
    )(scalars, *both_parts, qo_all, qo_all, hidden, cotangent)
    d_cond_parts = after(d_cond_parts, from_query)
    d_cond_all = lax.dynamic_slice_in_dim(
        jnp.stack(d_cond_parts * 2), (n_tensor - here) % n_tensor, n_tensor, 0
    ).reshape(tokens, 2 * enc_width)
    grad_hidden = (from_query + dot(d_cond_all, cond_weight, ROWS_T)).astype(BF16)
    return (mixed, grad_hidden)


def solution(mesh):
    placed = (
        P("dp", "tensor"),
        P("dp", "tensor"),
        P("dp", None),
        P("dp", None, None),
        P("dp", "tensor", None),
        P(None, "tensor"),
        P(None, "tensor"),
        P(None, "tensor"),
        P("tensor", None),
        P("tensor", None),
        P(),
        P(),
    )
    return jax.shard_map(
        shards,
        mesh=mesh,
        in_specs=placed,
        out_specs=(P("dp", "tensor"), P("dp", "tensor")),
        check_vma=False,
    )
```

```python
import functools
import math

import jax
import jax.numpy as jnp
from jax import lax
from jax.experimental import pallas as pl
from jax.experimental.pallas import tpu as pltpu
from jax.sharding import PartitionSpec as P

HEAD_DIM = 128
ENC_HEAD_DIM = 128
F32 = jnp.float32
BF16 = jnp.bfloat16
PLAIN = (((1,), (0,)), ((), ()))
ROWS_T = (((1,), (1,)), ((), ()))
COLS_T = (((0,), (0,)), ((), ()))
SCALING = 1.0 / math.sqrt(HEAD_DIM)
ENC_SCALING = 1.0 / math.sqrt(ENC_HEAD_DIM)
SLICE = 32


def dot(a, b, dims=PLAIN):
    return lax.dot_general(a, b, dims, preferred_element_type=F32)


def call(kernel, name, grid, in_specs, out_specs, out_shape, scratch, vmem_mib):
    return pl.pallas_call(
        kernel,
        out_shape=out_shape,
        grid_spec=pltpu.PrefetchScalarGridSpec(
            num_scalar_prefetch=1,
            grid=(grid,),
            in_specs=in_specs,
            out_specs=out_specs,
            scratch_shapes=scratch,
        ),
        compiler_params=pltpu.CompilerParams(
            vmem_limit_bytes=vmem_mib * 1024 * 1024, dimension_semantics=("arbitrary",)
        ),
        name=name,
    )


def whole(*shape):
    return pl.BlockSpec(shape, lambda g, s: (0,) * len(shape))


def group(*shape):
    return pl.BlockSpec((1,) + shape, lambda g, s: (g,) + (0,) * len(shape))


def exchange(pieces, position, axis="tensor"):
    size = pieces.shape[0]
    out = [lax.dynamic_index_in_dim(pieces, position, 0, keepdims=False)]
    for k in range(1, size):
        piece = lax.dynamic_index_in_dim(pieces, (position - k) % size, 0, keepdims=False)
        out.append(lax.ppermute(piece, axis, [(i, (i - k) % size) for i in range(size)]))
    return out


def spread(shard, size, axis="tensor"):
    return [shard] + [
        lax.ppermute(shard, axis, [(i, (i - k) % size) for i in range(size)])
        for k in range(1, size)
    ]


def spread_ring(shard, axis="tensor"):
    down = [(i, (i - 1) % 4) for i in range(4)]
    up = [(i, (i + 1) % 4) for i in range(4)]
    half = shard.shape[0] // 2
    next_one = lax.ppermute(shard, axis, down)
    last_one = lax.ppermute(shard, axis, up)
    far_top = lax.ppermute(next_one[:half], axis, down)
    far_bottom = lax.ppermute(last_one[half:], axis, up)
    return [shard, next_one, far_top, far_bottom, last_one]


def spread_halves(shard, axis="tensor"):
    down = [(i, (i - 1) % 4) for i in range(4)]
    up = [(i, (i + 1) % 4) for i in range(4)]
    half = shard.shape[0] // 2
    top, bottom = shard[:half], shard[half:]
    next_top = lax.ppermute(top, axis, down)
    last_bottom = lax.ppermute(bottom, axis, up)
    next_bottom = lax.ppermute(bottom, axis, down)
    last_top = lax.ppermute(top, axis, up)
    far_top = lax.ppermute(next_top, axis, down)
    far_bottom = lax.ppermute(last_bottom, axis, up)
    return [shard, next_top, next_bottom, far_top, far_bottom, last_top, last_bottom]


def after(value, earlier):
    return lax.optimization_barrier((value, earlier))[0]


def live_columns(count, shape):
    column = lax.broadcasted_iota(jnp.int32, shape, len(shape) - 1)
    return (column // 32) % 4 < count


def by_heads(array, head_dim):
    head = lax.broadcasted_iota(jnp.int32, array.shape, 1) // head_dim
    zero = jnp.zeros_like(array)
    count = array.shape[1] // head_dim
    return jnp.concatenate([jnp.where(head == h, array, zero) for h in range(count)], axis=0)


def head_blocks(array, rows, head_dim):
    count = array.shape[1] // head_dim
    return [
        array[h * rows : (h + 1) * rows, h * head_dim : (h + 1) * head_dim] for h in range(count)
    ]


def cond_kernel(s_ref, hidden_ref, weight_ref, c0, c1, c2, c3, total_ref):
    length = c0.shape[0]
    total_ref[...] = dot(hidden_ref[...], weight_ref[...])
    for k, ref in enumerate((c0, c1, c2, c3)):
        start = pl.multiple_of(((s_ref[0] + 4 - k) % 4) * length, length)
        ref[...] = total_ref[pl.ds(start, length), :].astype(BF16)


def project_kernel(dims, shift, counts, s_ref, *refs):
    total_ref = refs[-1]
    weight_ref = refs[sum(counts)]
    rest = refs[sum(counts) + 1 : -1]
    step = pl.program_id(0)
    for k, size in enumerate(counts):
        first = sum(counts[:k])
        parts = refs[first : first + size]

        @pl.when(step == k)
        def _(parts=parts, k=k):
            part = jnp.concatenate([ref[...] for ref in parts], axis=0)
            term = dot(part, weight_ref[...], dims)
            total_ref[...] = term if k == 0 else total_ref[...] + term

    @pl.when(step == pl.num_programs(0) - 1)
    def _():
        rows = total_ref.shape[0]
        moved = pltpu.roll(total_ref[...], rows - shift, 0)
        index = lax.broadcasted_iota(jnp.int32, moved.shape, 0)
        result = jnp.where(index < rows - shift, moved, 0.0)
        if len(rest) == 1:
            rest[0][...] = result.astype(BF16)
        else:
            total_ref[...] = result
            for k, ref in enumerate(rest[1:]):
                length = ref.shape[1]
                start = pl.multiple_of(((s_ref[0] + 4 - k) % 4) * length, length)
                ref[0] = rest[0][pl.ds(start, length), :]
                ref[1] = total_ref[pl.ds(start, length), :].astype(BF16)


def encode_kernel(
    s_ref,
    x_ref,
    c0,
    c1,
    c2,
    c3,
    enc_query_ref,
    enc_out_ref,
    cond_ref,
    queries_ref,
    probs_ref,
    encoded_ref,
):
    width = x_ref.shape[1]
    x = x_ref[...]
    cond = (c0[...].astype(F32) + c1[...].astype(F32)) + (
        c2[...].astype(F32) + c3[...].astype(F32)
    )
    cond = cond.astype(BF16)
    cond_ref[...] = cond
    length = cond.shape[0]
    queries = dot(x, enc_query_ref[...]).astype(BF16)
    queries_ref[...] = queries
    attended = []
    for head in range(width // ENC_HEAD_DIM):
        cols = slice(head * ENC_HEAD_DIM, (head + 1) * ENC_HEAD_DIM)
        vals = slice(width + head * ENC_HEAD_DIM, width + (head + 1) * ENC_HEAD_DIM)
        exponents = jnp.exp(dot(cond[:, cols], queries[:, cols], ROWS_T) * ENC_SCALING)
        probs = exponents / jnp.sum(exponents, axis=0, keepdims=True)
        probs_ref[head * length : (head + 1) * length, :] = probs
        attended.append(dot(probs.astype(BF16), cond[:, vals], COLS_T).astype(BF16))
    attended = jnp.concatenate(attended, axis=1)
    mixing = dot(attended, enc_out_ref[...])
    encoded_ref[...] = (x.astype(F32) + mixing).astype(BF16)


def pick(refs, query_ref, d_ctx_ref):
    for k, ref in enumerate(refs):

        @pl.when(pl.program_id(0) == k)
        def _(ref=ref):
            query_ref[...] = by_heads(ref[0], HEAD_DIM)
            d_ctx_ref[...] = by_heads(ref[1], HEAD_DIM)


def attention_kernel(
    s_ref,
    encoded_ref,
    key_w_ref,
    val_w_ref,
    q0,
    q1,
    q2,
    q3,
    probs_ref,
    d_scores_ref,
    out_ref,
    query_ref,
    d_ctx_ref,
):
    width = encoded_ref.shape[1]
    length = out_ref.shape[1]
    pick((q0, q1, q2, q3), query_ref, d_ctx_ref)
    encoded = encoded_ref[...]
    keys = dot(encoded, key_w_ref[...].reshape(width, -1)).astype(BF16)
    vals = dot(encoded, val_w_ref[...].reshape(width, -1)).astype(BF16)
    count = s_ref[1]
    scores = dot(query_ref[...], keys, ROWS_T) * SCALING
    expd = jnp.where(live_columns(count, scores.shape), jnp.exp(scores), 0.0)
    totals = jnp.sum(expd, axis=1, keepdims=True)
    probs = expd / jnp.where(count > 0, totals, 1.0)
    probs_low = probs.astype(BF16)
    probs_ref[0] = probs_low
    ctx = head_blocks(dot(probs_low, vals), length, HEAD_DIM)
    out_ref[0] = jnp.concatenate(ctx, axis=1).astype(BF16)
    weighted = probs * dot(d_ctx_ref[...], vals, ROWS_T)
    d_scores = (weighted - probs * jnp.sum(weighted, axis=1, keepdims=True)) * SCALING
    d_scores = d_scores.astype(BF16)
    d_scores_ref[0] = d_scores
    d_query = head_blocks(dot(d_scores, keys), length, HEAD_DIM)
    out_ref[1] = jnp.concatenate(d_query, axis=1).astype(BF16)


def encoded_back_kernel(
    s_ref,
    d_scores_ref,
    probs_ref,
    q0,
    q1,
    q2,
    q3,
    key_w_ref,
    val_w_ref,
    enc_out_ref,
    enc_probs_ref,
    enc_queries_ref,
    cond_ref,
    d_cond_ref,
    query_ref,
    d_ctx_ref,
    total_ref,
):
    step = pl.program_id(0)
    width = total_ref.shape[1]
    pick((q0, q1, q2, q3), query_ref, d_ctx_ref)
    d_keys = dot(d_scores_ref[0], query_ref[...], COLS_T).astype(BF16)
    d_vals = dot(probs_ref[0], d_ctx_ref[...], COLS_T).astype(BF16)
    term = dot(d_keys, key_w_ref[...].reshape(width, -1), ROWS_T)
    term = term + dot(d_vals, val_w_ref[...].reshape(width, -1), ROWS_T)
    term = term.astype(BF16).astype(F32)

    @pl.when(step == 0)
    def _():
        total_ref[...] = term

    @pl.when(step > 0)
    def _():
        total_ref[...] += term

    @pl.when(step == pl.num_programs(0) - 1)
    def _():
        length = cond_ref.shape[0]
        d_att = dot(total_ref[...].astype(BF16), enc_out_ref[...], ROWS_T).astype(BF16)
        probs = enc_probs_ref[...]
        d_probs = dot(by_heads(cond_ref[:, width:], ENC_HEAD_DIM), d_att, ROWS_T)
        weighted = probs * d_probs
        sums = jnp.sum(weighted.reshape(-1, length, weighted.shape[1]), axis=1, keepdims=True)
        spread_sums = (probs.reshape(-1, length, probs.shape[1]) * sums).reshape(probs.shape)
        d_scores = (weighted - spread_sums) * ENC_SCALING
        live = live_columns(s_ref[1], probs.shape)
        d_scores = jnp.where(live, d_scores, 0.0).astype(BF16)
        low = jnp.where(live, probs, 0.0).astype(BF16)
        d_keys = head_blocks(dot(d_scores, enc_queries_ref[...]), length, ENC_HEAD_DIM)
        d_vals = head_blocks(dot(low, d_att), length, ENC_HEAD_DIM)
        d_cond_ref[...] = jnp.concatenate(d_keys + d_vals, axis=1).astype(BF16)


def shifted_down(rows, shift):
    moved = pltpu.roll(rows, shift, 0)
    index = lax.broadcasted_iota(jnp.int32, rows.shape, 0)
    return jnp.where(index >= shift, moved, 0.0)


def outputs_kernel(
    shift,
    s_ref,
    c0,
    c1,
    c2,
    c3,
    out_w_ref,
    query_w_ref,
    hidden_ref,
    cotangent_ref,
    mixed_ref,
    grad_ref,
    rows_ref,
    mixed_sum_ref,
    grad_sum_ref,
):
    step = pl.program_id(0)
    half = out_w_ref.shape[2] // 2
    wide = out_w_ref.shape[3]
    length = c0.shape[1]
    for k, ref in enumerate((c0, c1, c2, c3)):
        start = pl.multiple_of(((s_ref[0] + k) % 4) * length, length)
        rows_ref[:, pl.ds(start, length), :] = ref[...]
    ctx = rows_ref[0]
    d_query = rows_ref[1]

    @pl.when(step == 0)
    def _():
        mixed_sum_ref[...] = jnp.zeros_like(mixed_sum_ref)
        grad_sum_ref[...] = jnp.zeros_like(grad_sum_ref)

    for side in range(2):
        weight = out_w_ref[:, :, side * half : (side + 1) * half, :].reshape(-1, wide)
        mixed_sum_ref[:, side * wide : (side + 1) * wide] += dot(ctx, weight)
    grad_sum_ref[...] += dot(d_query, query_w_ref[...].reshape(-1, wide), ROWS_T)

    @pl.when(step == pl.num_programs(0) - 1)
    def _():
        moved = shifted_down(mixed_sum_ref[...], shift)
        mixed_ref[...] = (hidden_ref[...].astype(F32) + moved).astype(mixed_ref.dtype)
        moved = shifted_down(grad_sum_ref[...], shift)
        grad_ref[...] = cotangent_ref[...].astype(F32) + moved


def shards(
    hidden,
    cotangent,
    counts,
    slot_of,
    neighbours,
    query_weight,
    key_weight,
    value_weight,
    out_weight,
    cond_weight,
    enc_query,
    enc_out,
):
    tokens, part_width = hidden.shape
    head_width = query_weight.shape[1]
    blocks = counts.shape[1]
    slots_per = slot_of.shape[2]
    item_total = blocks * slots_per
    slot_total, quarter, enc_width = neighbours.shape
    block_len = tokens // blocks
    shift = block_len - 1
    n_tensor = lax.axis_size("tensor")
    n_dp = lax.axis_size("dp")
    here = lax.axis_index("tensor")
    row = lax.axis_index("dp")
    all_width = head_width * n_tensor
    rows = slots_per * quarter * n_tensor
    enc_rows = enc_width // ENC_HEAD_DIM * block_len
    head_rows = head_width // HEAD_DIM * block_len
    sds = jax.ShapeDtypeStruct

    seq_counts = counts[0]
    count = lax.dynamic_slice_in_dim(seq_counts, here, 1, 0)
    scalars = jnp.concatenate([here.astype(jnp.int32)[None], count])

    wq_part = lax.dynamic_slice_in_dim(
        query_weight.reshape(n_tensor, part_width, head_width), row * SLICE, SLICE, 1
    )
    wo_part = lax.dynamic_slice_in_dim(out_weight, row * (SLICE // 2), SLICE // 2, 0)
    wo_part = wo_part.reshape(SLICE // 2, n_tensor, 2, head_width).transpose(1, 2, 0, 3)
    wo_part = wo_part.reshape(n_tensor, SLICE, head_width)
    kv_rows = 2 * enc_width // n_dp
    kv_part = jnp.where(
        row < n_dp // 2,
        lax.dynamic_slice_in_dim(key_weight, row % (n_dp // 2) * kv_rows, kv_rows, 0),
        lax.dynamic_slice_in_dim(value_weight, row % (n_dp // 2) * kv_rows, kv_rows, 0),
    )
    kv_part = jnp.broadcast_to(kv_part[None], (n_tensor, kv_rows, head_width))
    weight_parts = exchange(jnp.concatenate([wq_part, wo_part, kv_part], axis=1), here)
    qo_parts = jnp.stack([part[: 2 * SLICE] for part in weight_parts])
    kv_parts = jnp.stack([part[2 * SLICE :] for part in weight_parts])
    hidden_parts = spread_halves(hidden)
    cot_parts = spread_ring(cotangent)

    def kv_spec(index):
        return pl.BlockSpec((n_dp // 2, 1, kv_rows, head_width), lambda g, s: (index, g, 0, 0))

    def weight_spec(index):
        return pl.BlockSpec((n_dp, 1, SLICE, head_width), lambda g, s: (0, g, index, 0))

    c_spec = whole(block_len, 2 * enc_width)
    own_cond, *to_send = call(
        cond_kernel,
        "cond",
        1,
        [whole(tokens, part_width), whole(part_width, 2 * enc_width)],
        (c_spec,) * 4,
        (sds((block_len, 2 * enc_width), BF16),) * 4,
        [pltpu.VMEM((tokens, 2 * enc_width), F32)],
        20,
    )(scalars, hidden, cond_weight)
    ahead = (hidden_parts[1], hidden_parts[6], own_cond)
    kv_all = lax.all_gather(after(kv_parts, ahead), "dp", axis=0)
    cond_parts = [own_cond] + [
        lax.ppermute(array, "tensor", [(i, (i - k) % n_tensor) for i in range(n_tensor)])
        for k, array in enumerate(to_send, 1)
    ]

    def projected(parts, counts, weight, dims, weight_block, weight_map, name, vmem, before=None):
        full = whole(tokens, head_width)
        if before is None:
            out_specs, out_shape = full, sds((tokens, head_width), BF16)
        else:
            out_specs = (whole(2, block_len, head_width),) * n_tensor
            out_shape = (sds((2, block_len, head_width), BF16),) * n_tensor
        return call(
            functools.partial(project_kernel, dims, shift, counts),
            name,
            n_tensor,
            [whole(*part.shape) for part in parts]
            + [pl.BlockSpec(weight_block, weight_map)]
            + ([] if before is None else [full]),
            out_specs,
            out_shape,
            [pltpu.VMEM((tokens, head_width), F32)],
            vmem,
        )(scalars, *parts, weight, *([] if before is None else [before]))

    query = projected(
        hidden_parts,
        (1, 2, 2, 2),
        query_weight,
        PLAIN,
        (part_width, head_width),
        lambda g, s: ((s[0] + g) % 4, 0),
        "query",
        60,
    )

    live = jnp.arange(slots_per)[None, :] < after(seq_counts, (query, cot_parts[1:], cond_parts[1:]))[:, None]
    slot_flat = slot_of.reshape(item_total)
    matches = (jnp.arange(slot_total)[:, None] == slot_flat[None, :]) & live.reshape(item_total)[
        None, :
    ]
    returned = lax.all_to_all(neighbours, "dp", split_axis=0, concat_axis=0, tiled=True)
    items = jnp.einsum(
        "si,sre->ire", matches.astype(BF16), returned, preferred_element_type=F32
    ).astype(BF16)
    items = items.reshape(blocks, slots_per * quarter, enc_width)
    x = lax.all_to_all(items, "tensor", split_axis=0, concat_axis=0, tiled=True)
    x = x.reshape(rows, enc_width)

    qo_all = lax.all_gather(after(qo_parts, items), "dp", axis=0)
    own_query, *to_send = projected(
        after(cot_parts, (items, cond_parts[1:])),
        (1, 1, 2, 1),
        out_weight,
        ROWS_T,
        (head_width, part_width),
        lambda g, s: (0, (s[0] + g) % 4),
        "d_ctx",
        16,
        before=query,
    )
    query_parts = [own_query] + [
        lax.ppermute(array, "tensor", [(i, (i - k) % n_tensor) for i in range(n_tensor)])
        for k, array in enumerate(to_send, 1)
    ]

    c_spec = whole(block_len, 2 * enc_width)
    w_spec = whole(enc_width, enc_width)
    r_spec = whole(rows, enc_width)
    p_spec = whole(enc_rows, rows)
    cond, enc_queries, enc_probs, encoded = call(
        encode_kernel,
        "encode",
        1,
        [r_spec] + [c_spec] * 4 + [w_spec] * 2,
        (c_spec, r_spec, p_spec, r_spec),
        (
            sds((block_len, 2 * enc_width), BF16),
            sds((rows, enc_width), BF16),
            sds((enc_rows, rows), F32),
            sds((rows, enc_width), BF16),
        ),
        [],
        60,
    )(scalars, x, *cond_parts, enc_query, enc_out)

    q_spec = whole(2, block_len, head_width)
    big = pltpu.VMEM((head_rows, head_width), BF16)
    both_spec = pl.BlockSpec((2, block_len, head_width), lambda g, s: (0, 0, (s[0] + g) % 4))
    probs, d_scores, both = call(
        attention_kernel,
        "attention",
        n_tensor,
        [r_spec, kv_spec(0), kv_spec(1)] + [q_spec] * 4,
        (
            group(head_rows, rows),
            group(head_rows, rows),
            both_spec,
        ),
        (
            sds((n_tensor, head_rows, rows), BF16),
            sds((n_tensor, head_rows, rows), BF16),
            sds((2, block_len, all_width), BF16),
        ),
        [big, big],
        60,
    )(scalars, encoded, kv_all, kv_all, *query_parts)
    both_parts = spread(both, n_tensor)

    d_cond = call(
        encoded_back_kernel,
        "encoded_back",
        n_tensor,
        [group(head_rows, rows), group(head_rows, rows)]
        + [q_spec] * 4
        + [kv_spec(0), kv_spec(1), w_spec, p_spec, r_spec, c_spec],
        c_spec,
        sds((block_len, 2 * enc_width), BF16),
        [big, big, pltpu.VMEM((rows, enc_width), F32)],
        60,
    )(
        scalars,
        d_scores,
        probs,
        *query_parts,
        kv_all,
        kv_all,
        enc_out,
        enc_probs,
        enc_queries,
        cond,
    )
    d_cond_parts = spread(after(d_cond, both_parts[1]), n_tensor)

    out_spec = whole(tokens, part_width)
    acc = pltpu.VMEM((tokens, part_width), F32)
    mixed, from_query = call(
        functools.partial(outputs_kernel, shift),
        "outputs",
        n_tensor,
        [both_spec] * 4 + [weight_spec(1), weight_spec(0), out_spec, out_spec],
        (out_spec, out_spec),
        (sds((tokens, part_width), BF16), sds((tokens, part_width), F32)),
        [pltpu.VMEM((2, tokens, head_width), BF16), acc, acc],
        40,
    )(scalars, *both_parts, qo_all, qo_all, hidden, cotangent)
    d_cond_parts = after(d_cond_parts, from_query)
    d_cond_all = lax.dynamic_slice_in_dim(
        jnp.stack(d_cond_parts * 2), (n_tensor - here) % n_tensor, n_tensor, 0
    ).reshape(tokens, 2 * enc_width)
    grad_hidden = (from_query + dot(d_cond_all, cond_weight, ROWS_T)).astype(BF16)
    return (mixed, grad_hidden)


def solution(mesh):
    placed = (
        P("dp", "tensor"),
        P("dp", "tensor"),
        P("dp", None),
        P("dp", None, None),
        P("dp", "tensor", None),
        P(None, "tensor"),
        P(None, "tensor"),
        P(None, "tensor"),
        P("tensor", None),
        P("tensor", None),
        P(),
        P(),
    )
    return jax.shard_map(
        shards,
        mesh=mesh,
        in_specs=placed,
        out_specs=(P("dp", "tensor"), P("dp", "tensor")),
        check_vma=False,
    )
```

```python
import functools
import math

import jax
import jax.numpy as jnp
from jax import lax
from jax.experimental import pallas as pl
from jax.experimental.pallas import tpu as pltpu
from jax.sharding import PartitionSpec as P

HEAD_DIM = 128
ENC_HEAD_DIM = 128
F32 = jnp.float32
BF16 = jnp.bfloat16
PLAIN = (((1,), (0,)), ((), ()))
ROWS_T = (((1,), (1,)), ((), ()))
COLS_T = (((0,), (0,)), ((), ()))
SCALING = 1.0 / math.sqrt(HEAD_DIM)
ENC_SCALING = 1.0 / math.sqrt(ENC_HEAD_DIM)
SLICE = 32


def dot(a, b, dims=PLAIN):
    return lax.dot_general(a, b, dims, preferred_element_type=F32)


def call(kernel, name, grid, in_specs, out_specs, out_shape, scratch, vmem_mib):
    return pl.pallas_call(
        kernel,
        out_shape=out_shape,
        grid_spec=pltpu.PrefetchScalarGridSpec(
            num_scalar_prefetch=1,
            grid=(grid,),
            in_specs=in_specs,
            out_specs=out_specs,
            scratch_shapes=scratch,
        ),
        compiler_params=pltpu.CompilerParams(
            vmem_limit_bytes=vmem_mib * 1024 * 1024, dimension_semantics=("arbitrary",)
        ),
        name=name,
    )


def whole(*shape):
    return pl.BlockSpec(shape, lambda g, s: (0,) * len(shape))


def group(*shape):
    return pl.BlockSpec((1,) + shape, lambda g, s: (g,) + (0,) * len(shape))


def exchange(pieces, position, axis="tensor"):
    size = pieces.shape[0]
    out = [lax.dynamic_index_in_dim(pieces, position, 0, keepdims=False)]
    for k in range(1, size):
        piece = lax.dynamic_index_in_dim(pieces, (position - k) % size, 0, keepdims=False)
        out.append(lax.ppermute(piece, axis, [(i, (i - k) % size) for i in range(size)]))
    return out


def spread(shard, size, axis="tensor"):
    return [shard] + [
        lax.ppermute(shard, axis, [(i, (i - k) % size) for i in range(size)])
        for k in range(1, size)
    ]


def spread_ring(shard, axis="tensor"):
    down = [(i, (i - 1) % 4) for i in range(4)]
    up = [(i, (i + 1) % 4) for i in range(4)]
    half = shard.shape[0] // 2
    next_one = lax.ppermute(shard, axis, down)
    last_one = lax.ppermute(shard, axis, up)
    far_top = lax.ppermute(next_one[:half], axis, down)
    far_bottom = lax.ppermute(last_one[half:], axis, up)
    return [shard, next_one, far_top, far_bottom, last_one]


def spread_halves(shard, axis="tensor"):
    down = [(i, (i - 1) % 4) for i in range(4)]
    up = [(i, (i + 1) % 4) for i in range(4)]
    half = shard.shape[0] // 2
    top, bottom = shard[:half], shard[half:]
    next_top = lax.ppermute(top, axis, down)
    last_bottom = lax.ppermute(bottom, axis, up)
    next_bottom = lax.ppermute(bottom, axis, down)
    last_top = lax.ppermute(top, axis, up)
    far_top = lax.ppermute(next_top, axis, down)
    far_bottom = lax.ppermute(last_bottom, axis, up)
    return [shard, next_top, next_bottom, far_top, far_bottom, last_top, last_bottom]


def after(value, earlier):
    return lax.optimization_barrier((value, earlier))[0]


def live_columns(count, shape):
    column = lax.broadcasted_iota(jnp.int32, shape, len(shape) - 1)
    return (column // 32) % 4 < count


def by_heads(array, head_dim):
    head = lax.broadcasted_iota(jnp.int32, array.shape, 1) // head_dim
    zero = jnp.zeros_like(array)
    count = array.shape[1] // head_dim
    return jnp.concatenate([jnp.where(head == h, array, zero) for h in range(count)], axis=0)


def head_blocks(array, rows, head_dim):
    count = array.shape[1] // head_dim
    return [
        array[h * rows : (h + 1) * rows, h * head_dim : (h + 1) * head_dim] for h in range(count)
    ]


def cond_kernel(s_ref, hidden_ref, weight_ref, c0, c1, c2, c3, total_ref):
    length = c0.shape[0]
    total_ref[...] = dot(hidden_ref[...], weight_ref[...])
    for k, ref in enumerate((c0, c1, c2, c3)):
        start = pl.multiple_of(((s_ref[0] + 4 - k) % 4) * length, length)
        ref[...] = total_ref[pl.ds(start, length), :].astype(BF16)


def project_kernel(dims, shift, counts, s_ref, *refs):
    total_ref = refs[-1]
    weight_ref = refs[sum(counts)]
    rest = refs[sum(counts) + 1 : -1]
    step = pl.program_id(0)
    for k, size in enumerate(counts):
        first = sum(counts[:k])
        parts = refs[first : first + size]

        @pl.when(step == k)
        def _(parts=parts, k=k):
            part = jnp.concatenate([ref[...] for ref in parts], axis=0)
            term = dot(part, weight_ref[...], dims)
            total_ref[...] = term if k == 0 else total_ref[...] + term

    @pl.when(step == pl.num_programs(0) - 1)
    def _():
        rows = total_ref.shape[0]
        moved = pltpu.roll(total_ref[...], rows - shift, 0)
        index = lax.broadcasted_iota(jnp.int32, moved.shape, 0)
        result = jnp.where(index < rows - shift, moved, 0.0)
        if len(rest) == 1:
            rest[0][...] = result.astype(BF16)
        else:
            total_ref[...] = result
            for k, ref in enumerate(rest[1:]):
                length = ref.shape[1]
                start = pl.multiple_of(((s_ref[0] + 4 - k) % 4) * length, length)
                ref[0] = rest[0][pl.ds(start, length), :]
                ref[1] = total_ref[pl.ds(start, length), :].astype(BF16)


def encode_kernel(
    s_ref,
    x_ref,
    c0,
    c1,
    c2,
    c3,
    enc_query_ref,
    enc_out_ref,
    cond_ref,
    queries_ref,
    probs_ref,
    encoded_ref,
):
    width = x_ref.shape[1]
    x = x_ref[...]
    cond = (c0[...].astype(F32) + c1[...].astype(F32)) + (
        c2[...].astype(F32) + c3[...].astype(F32)
    )
    cond = cond.astype(BF16)
    cond_ref[...] = cond
    length = cond.shape[0]
    queries = dot(x, enc_query_ref[...]).astype(BF16)
    queries_ref[...] = queries
    attended = []
    for head in range(width // ENC_HEAD_DIM):
        cols = slice(head * ENC_HEAD_DIM, (head + 1) * ENC_HEAD_DIM)
        vals = slice(width + head * ENC_HEAD_DIM, width + (head + 1) * ENC_HEAD_DIM)
        exponents = jnp.exp(dot(cond[:, cols], queries[:, cols], ROWS_T) * ENC_SCALING)
        probs = exponents / jnp.sum(exponents, axis=0, keepdims=True)
        probs_ref[head * length : (head + 1) * length, :] = probs
        attended.append(dot(probs.astype(BF16), cond[:, vals], COLS_T).astype(BF16))
    attended = jnp.concatenate(attended, axis=1)
    mixing = dot(attended, enc_out_ref[...])
    encoded_ref[...] = (x.astype(F32) + mixing).astype(BF16)


def pick(refs, query_ref, d_ctx_ref):
    for k, ref in enumerate(refs):

        @pl.when(pl.program_id(0) == k)
        def _(ref=ref):
            query_ref[...] = by_heads(ref[0], HEAD_DIM)
            d_ctx_ref[...] = by_heads(ref[1], HEAD_DIM)


def attention_kernel(
    s_ref,
    encoded_ref,
    key_w_ref,
    val_w_ref,
    q0,
    q1,
    q2,
    q3,
    probs_ref,
    d_scores_ref,
    out_ref,
    query_ref,
    d_ctx_ref,
):
    width = encoded_ref.shape[1]
    length = out_ref.shape[1]
    pick((q0, q1, q2, q3), query_ref, d_ctx_ref)
    encoded = encoded_ref[...]
    keys = dot(encoded, key_w_ref[...].reshape(width, -1)).astype(BF16)
    vals = dot(encoded, val_w_ref[...].reshape(width, -1)).astype(BF16)
    count = s_ref[1]
    scores = dot(query_ref[...], keys, ROWS_T) * SCALING
    expd = jnp.where(live_columns(count, scores.shape), jnp.exp(scores), 0.0)
    totals = jnp.sum(expd, axis=1, keepdims=True)
    probs = expd / jnp.where(count > 0, totals, 1.0)
    probs_low = probs.astype(BF16)
    probs_ref[0] = probs_low
    ctx = head_blocks(dot(probs_low, vals), length, HEAD_DIM)
    out_ref[0] = jnp.concatenate(ctx, axis=1).astype(BF16)
    weighted = probs * dot(d_ctx_ref[...], vals, ROWS_T)
    d_scores = (weighted - probs * jnp.sum(weighted, axis=1, keepdims=True)) * SCALING
    d_scores = d_scores.astype(BF16)
    d_scores_ref[0] = d_scores
    d_query = head_blocks(dot(d_scores, keys), length, HEAD_DIM)
    out_ref[1] = jnp.concatenate(d_query, axis=1).astype(BF16)


def encoded_back_kernel(
    s_ref,
    d_scores_ref,
    probs_ref,
    q0,
    q1,
    q2,
    q3,
    key_w_ref,
    val_w_ref,
    enc_out_ref,
    enc_probs_ref,
    enc_queries_ref,
    cond_ref,
    d_cond_ref,
    query_ref,
    d_ctx_ref,
    total_ref,
):
    step = pl.program_id(0)
    width = total_ref.shape[1]
    pick((q0, q1, q2, q3), query_ref, d_ctx_ref)
    d_keys = dot(d_scores_ref[0], query_ref[...], COLS_T).astype(BF16)
    d_vals = dot(probs_ref[0], d_ctx_ref[...], COLS_T).astype(BF16)
    term = dot(d_keys, key_w_ref[...].reshape(width, -1), ROWS_T)
    term = term + dot(d_vals, val_w_ref[...].reshape(width, -1), ROWS_T)
    term = term.astype(BF16).astype(F32)

    @pl.when(step == 0)
    def _():
        total_ref[...] = term

    @pl.when(step > 0)
    def _():
        total_ref[...] += term

    @pl.when(step == pl.num_programs(0) - 1)
    def _():
        length = cond_ref.shape[0]
        d_att = dot(total_ref[...].astype(BF16), enc_out_ref[...], ROWS_T).astype(BF16)
        probs = enc_probs_ref[...]
        d_probs = dot(by_heads(cond_ref[:, width:], ENC_HEAD_DIM), d_att, ROWS_T)
        weighted = probs * d_probs
        sums = jnp.sum(weighted.reshape(-1, length, weighted.shape[1]), axis=1, keepdims=True)
        spread_sums = (probs.reshape(-1, length, probs.shape[1]) * sums).reshape(probs.shape)
        d_scores = (weighted - spread_sums) * ENC_SCALING
        live = live_columns(s_ref[1], probs.shape)
        d_scores = jnp.where(live, d_scores, 0.0).astype(BF16)
        low = jnp.where(live, probs, 0.0).astype(BF16)
        d_keys = head_blocks(dot(d_scores, enc_queries_ref[...]), length, ENC_HEAD_DIM)
        d_vals = head_blocks(dot(low, d_att), length, ENC_HEAD_DIM)
        d_cond_ref[...] = jnp.concatenate(d_keys + d_vals, axis=1).astype(BF16)


def shifted_down(rows, shift):
    moved = pltpu.roll(rows, shift, 0)
    index = lax.broadcasted_iota(jnp.int32, rows.shape, 0)
    return jnp.where(index >= shift, moved, 0.0)


def outputs_kernel(
    shift,
    s_ref,
    c0,
    c1,
    c2,
    c3,
    out_w_ref,
    query_w_ref,
    hidden_ref,
    cotangent_ref,
    mixed_ref,
    grad_ref,
    rows_ref,
    mixed_sum_ref,
    grad_sum_ref,
):
    step = pl.program_id(0)
    half = out_w_ref.shape[2] // 2
    wide = out_w_ref.shape[3]
    length = c0.shape[1]
    for k, ref in enumerate((c0, c1, c2, c3)):
        start = pl.multiple_of(((s_ref[0] + k) % 4) * length, length)
        rows_ref[:, pl.ds(start, length), :] = ref[...]
    ctx = rows_ref[0]
    d_query = rows_ref[1]

    @pl.when(step == 0)
    def _():
        mixed_sum_ref[...] = jnp.zeros_like(mixed_sum_ref)
        grad_sum_ref[...] = jnp.zeros_like(grad_sum_ref)

    for side in range(2):
        weight = out_w_ref[:, :, side * half : (side + 1) * half, :].reshape(-1, wide)
        mixed_sum_ref[:, side * wide : (side + 1) * wide] += dot(ctx, weight)
    grad_sum_ref[...] += dot(d_query, query_w_ref[...].reshape(-1, wide), ROWS_T)

    @pl.when(step == pl.num_programs(0) - 1)
    def _():
        moved = shifted_down(mixed_sum_ref[...], shift)
        mixed_ref[...] = (hidden_ref[...].astype(F32) + moved).astype(mixed_ref.dtype)
        moved = shifted_down(grad_sum_ref[...], shift)
        grad_ref[...] = cotangent_ref[...].astype(F32) + moved


def shards(
    hidden,
    cotangent,
    counts,
    slot_of,
    neighbours,
    query_weight,
    key_weight,
    value_weight,
    out_weight,
    cond_weight,
    enc_query,
    enc_out,
):
    tokens, part_width = hidden.shape
    head_width = query_weight.shape[1]
    blocks = counts.shape[1]
    slots_per = slot_of.shape[2]
    item_total = blocks * slots_per
    slot_total, quarter, enc_width = neighbours.shape
    block_len = tokens // blocks
    shift = block_len - 1
    n_tensor = lax.axis_size("tensor")
    n_dp = lax.axis_size("dp")
    here = lax.axis_index("tensor")
    row = lax.axis_index("dp")
    all_width = head_width * n_tensor
    rows = slots_per * quarter * n_tensor
    enc_rows = enc_width // ENC_HEAD_DIM * block_len
    head_rows = head_width // HEAD_DIM * block_len
    sds = jax.ShapeDtypeStruct

    seq_counts = counts[0]
    count = lax.dynamic_slice_in_dim(seq_counts, here, 1, 0)
    scalars = jnp.concatenate([here.astype(jnp.int32)[None], count])

    wq_part = lax.dynamic_slice_in_dim(
        query_weight.reshape(n_tensor, part_width, head_width), row * SLICE, SLICE, 1
    )
    wo_part = lax.dynamic_slice_in_dim(out_weight, row * (SLICE // 2), SLICE // 2, 0)
    wo_part = wo_part.reshape(SLICE // 2, n_tensor, 2, head_width).transpose(1, 2, 0, 3)
    wo_part = wo_part.reshape(n_tensor, SLICE, head_width)
    kv_rows = 2 * enc_width // n_dp
    kv_part = jnp.where(
        row < n_dp // 2,
        lax.dynamic_slice_in_dim(key_weight, row % (n_dp // 2) * kv_rows, kv_rows, 0),
        lax.dynamic_slice_in_dim(value_weight, row % (n_dp // 2) * kv_rows, kv_rows, 0),
    )
    kv_part = jnp.broadcast_to(kv_part[None], (n_tensor, kv_rows, head_width))
    weight_parts = exchange(jnp.concatenate([wq_part, wo_part, kv_part], axis=1), here)
    qo_parts = jnp.stack([part[: 2 * SLICE] for part in weight_parts])
    kv_parts = jnp.stack([part[2 * SLICE :] for part in weight_parts])
    hidden_parts = spread_halves(hidden)
    cot_parts = spread_ring(cotangent)

    def kv_spec(index):
        return pl.BlockSpec((n_dp // 2, 1, kv_rows, head_width), lambda g, s: (index, g, 0, 0))

    def weight_spec(index):
        return pl.BlockSpec((n_dp, 1, SLICE, head_width), lambda g, s: (0, g, index, 0))

    c_spec = whole(block_len, 2 * enc_width)
    own_cond, *to_send = call(
        cond_kernel,
        "cond",
        1,
        [whole(tokens, part_width), whole(part_width, 2 * enc_width)],
        (c_spec,) * 4,
        (sds((block_len, 2 * enc_width), BF16),) * 4,
        [pltpu.VMEM((tokens, 2 * enc_width), F32)],
        20,
    )(scalars, hidden, cond_weight)
    ahead = (hidden_parts[1], hidden_parts[6], own_cond)
    kv_all = lax.all_gather(after(kv_parts, ahead), "dp", axis=0)
    cond_parts = [own_cond] + [
        lax.ppermute(array, "tensor", [(i, (i - k) % n_tensor) for i in range(n_tensor)])
        for k, array in enumerate(to_send, 1)
    ]

    def projected(parts, counts, weight, dims, weight_block, weight_map, name, vmem, before=None):
        full = whole(tokens, head_width)
        if before is None:
            out_specs, out_shape = full, sds((tokens, head_width), BF16)
        else:
            out_specs = (whole(2, block_len, head_width),) * n_tensor
            out_shape = (sds((2, block_len, head_width), BF16),) * n_tensor
        return call(
            functools.partial(project_kernel, dims, shift, counts),
            name,
            n_tensor,
            [whole(*part.shape) for part in parts]
            + [pl.BlockSpec(weight_block, weight_map)]
            + ([] if before is None else [full]),
            out_specs,
            out_shape,
            [pltpu.VMEM((tokens, head_width), F32)],
            vmem,
        )(scalars, *parts, weight, *([] if before is None else [before]))

    query = projected(
        hidden_parts,
        (1, 2, 2, 2),
        query_weight,
        PLAIN,
        (part_width, head_width),
        lambda g, s: ((s[0] + g) % 4, 0),
        "query",
        60,
    )

    live = jnp.arange(slots_per)[None, :] < after(seq_counts, (query, cot_parts[1:], cond_parts[1:]))[:, None]
    slot_flat = slot_of.reshape(item_total)
    matches = (jnp.arange(slot_total)[:, None] == slot_flat[None, :]) & live.reshape(item_total)[
        None, :
    ]
    returned = lax.all_to_all(neighbours, "dp", split_axis=0, concat_axis=0, tiled=True)
    items = jnp.einsum(
        "si,sre->ire", matches.astype(BF16), returned, preferred_element_type=F32
    ).astype(BF16)
    items = items.reshape(blocks, slots_per * quarter, enc_width)
    x = lax.all_to_all(items, "tensor", split_axis=0, concat_axis=0, tiled=True)
    x = x.reshape(rows, enc_width)

    qo_all = lax.all_gather(after(qo_parts, items), "dp", axis=0)
    own_query, *to_send = projected(
        after(cot_parts, (items, cond_parts[1:])),
        (1, 1, 2, 1),
        out_weight,
        ROWS_T,
        (head_width, part_width),
        lambda g, s: (0, (s[0] + g) % 4),
        "d_ctx",
        16,
        before=query,
    )
    query_parts = [own_query] + [
        lax.ppermute(array, "tensor", [(i, (i - k) % n_tensor) for i in range(n_tensor)])
        for k, array in enumerate(to_send, 1)
    ]

    c_spec = whole(block_len, 2 * enc_width)
    w_spec = whole(enc_width, enc_width)
    r_spec = whole(rows, enc_width)
    p_spec = whole(enc_rows, rows)
    cond, enc_queries, enc_probs, encoded = call(
        encode_kernel,
        "encode",
        1,
        [r_spec] + [c_spec] * 4 + [w_spec] * 2,
        (c_spec, r_spec, p_spec, r_spec),
        (
            sds((block_len, 2 * enc_width), BF16),
            sds((rows, enc_width), BF16),
            sds((enc_rows, rows), F32),
            sds((rows, enc_width), BF16),
        ),
        [],
        60,
    )(scalars, x, *cond_parts, enc_query, enc_out)

    q_spec = whole(2, block_len, head_width)
    big = pltpu.VMEM((head_rows, head_width), BF16)
    both_spec = pl.BlockSpec((2, block_len, head_width), lambda g, s: (0, 0, (s[0] + g) % 4))
    probs, d_scores, both = call(
        attention_kernel,
        "attention",
        n_tensor,
        [r_spec, kv_spec(0), kv_spec(1)] + [q_spec] * 4,
        (
            group(head_rows, rows),
            group(head_rows, rows),
            both_spec,
        ),
        (
            sds((n_tensor, head_rows, rows), BF16),
            sds((n_tensor, head_rows, rows), BF16),
            sds((2, block_len, all_width), BF16),
        ),
        [big, big],
        60,
    )(scalars, encoded, kv_all, kv_all, *query_parts)
    both_parts = spread(both, n_tensor)

    d_cond = call(
        encoded_back_kernel,
        "encoded_back",
        n_tensor,
        [group(head_rows, rows), group(head_rows, rows)]
        + [q_spec] * 4
        + [kv_spec(0), kv_spec(1), w_spec, p_spec, r_spec, c_spec],
        c_spec,
        sds((block_len, 2 * enc_width), BF16),
        [big, big, pltpu.VMEM((rows, enc_width), F32)],
        60,
    )(
        scalars,
        d_scores,
        probs,
        *query_parts,
        kv_all,
        kv_all,
        enc_out,
        enc_probs,
        enc_queries,
        cond,
    )
    d_cond_parts = spread(after(d_cond, both_parts[1]), n_tensor)

    out_spec = whole(tokens, part_width)
    acc = pltpu.VMEM((tokens, part_width), F32)
    mixed, from_query = call(
        functools.partial(outputs_kernel, shift),
        "outputs",
        n_tensor,
        [both_spec] * 4 + [weight_spec(1), weight_spec(0), out_spec, out_spec],
        (out_spec, out_spec),
        (sds((tokens, part_width), BF16), sds((tokens, part_width), F32)),
        [pltpu.VMEM((2, tokens, head_width), BF16), acc, acc],
        24,
    )(scalars, *both_parts, qo_all, qo_all, hidden, cotangent)
    d_cond_parts = after(d_cond_parts, from_query)
    d_cond_all = jnp.zeros((n_tensor, block_len, 2 * enc_width), BF16)
    for k, part in enumerate(d_cond_parts):
        d_cond_all = lax.dynamic_update_index_in_dim(d_cond_all, part, (here + k) % n_tensor, 0)
    d_cond_all = d_cond_all.reshape(tokens, 2 * enc_width)
    grad_hidden = (from_query + dot(d_cond_all, cond_weight, ROWS_T)).astype(BF16)
    return (mixed, grad_hidden)


def solution(mesh):
    placed = (
        P("dp", "tensor"),
        P("dp", "tensor"),
        P("dp", None),
        P("dp", None, None),
        P("dp", "tensor", None),
        P(None, "tensor"),
        P(None, "tensor"),
        P(None, "tensor"),
        P("tensor", None),
        P("tensor", None),
        P(),
        P(),
    )
    return jax.shard_map(
        shards,
        mesh=mesh,
        in_specs=placed,
        out_specs=(P("dp", "tensor"), P("dp", "tensor")),
        check_vma=False,
    )
```
